32 devices in a mesh: grp: 2 (over core), fsdp: 16 (over z, y, x).
Axes of the slice: x: 2, y: 2, z: 4, core: 2. Of those that a mesh axis runs over, the one named last changes fastest.
Arguments:
- features: bfloat16 [12288, 128], P(('grp', 'fsdp')), may hold values from -6 to 6
- adjacency: int32 [96, 128, 128], P(('grp', 'fsdp')), may hold values from 0 to 1, as said below
- counts: int32 [96], P(('grp', 'fsdp')), may hold values from 64 to 128, as said below
- input_weight: bfloat16 [128, 512], P('fsdp'), may hold values from -0.5 to 0.5
- first_gain: bfloat16 [512], P('fsdp'), may hold values from 0.5 to 1.5
- first_shift: bfloat16 [512], P('fsdp'), may hold values from -1.75 to 1.75
- attend_weight: bfloat16 [512, 1536], P('fsdp'), may hold values from -0.25 to 0.25
- merge_weight: bfloat16 [512, 512], P('fsdp'), may hold values from -0.75 to 0.75
- second_gain: bfloat16 [512], P('fsdp'), may hold values from 0.5 to 1.5
- second_shift: bfloat16 [512], P('fsdp'), may hold values from -1.75 to 1.75
- expand_weight: bfloat16 [512, 1024], P('fsdp'), may hold values from -0.25 to 0.25
- reduce_weight: bfloat16 [1024, 512], P('fsdp'), may hold values from -0.1875 to 0.1875
- readout_weight: bfloat16 [1024], P('fsdp'), may hold values from -0.25 to 0.25
- cotangent: float32 [12288, 512], P(('grp', 'fsdp')), may hold values from -6 to 6
Outputs:
- node_output: float32 [12288, 512], P(('grp', 'fsdp'))
- grad_features: float32 [12288, 128], P(('grp', 'fsdp'))
- grad_input_weight: float32 [128, 512], P('fsdp')
- grad_first_gain: float32 [512], P('fsdp')
- grad_first_shift: float32 [512], P('fsdp')
- grad_attend: float32 [512, 1536], P('fsdp')
- grad_merge: float32 [512, 512], P('fsdp')
- grad_second_gain: float32 [512], P('fsdp')
- grad_second_shift: float32 [512], P('fsdp')
- grad_expand: float32 [512, 1024], P('fsdp')
- grad_reduce: float32 [1024, 512], P('fsdp')
- grad_readout: float32 [1024], P('fsdp')
The draws below stay inside these ranges and needn't reach their ends.
Inputs may be any that keep to these rules, and one draw needn't show every extreme that they name: `counts`: the live nodes of a cluster fill its first slots; the other slots of its 128 are empty. `adjacency`: symmetric within each cluster, with a zero diagonal; links of empty slots are ignored.
All inputs are finite; a program needn't handle non-finite values.
Results may differ from the reference program's by a relative error of at most 0.012.
The reference program's roundings to bfloat16 on the way count: a program that leaves them out, or rounds other values in their place, can miss the bound.
Values may be sent and summed in bfloat16 or wider, within the bound.
A program may use at most 192 MiB of HBM per device.

```python
import jax
import jax.numpy as jnp
from jax import lax

D = 512
HEADS = 8
HEAD = 64
FF = 1024
F = 128
HOPS = 7
CAP = 128
CLUSTERS = 96
NODES = 12288


def draw_counts(key, part):
    key = jax.random.fold_in(key, 11)
    drawn = jax.random.randint(key, (CLUSTERS,), CAP // 2, CAP + 1, dtype=jnp.int32)
    places = jnp.arange(CLUSTERS, dtype=jnp.int32)
    drawn = jnp.where(places == 0, CAP, drawn)
    return jnp.where(places == 1, CAP // 2, drawn).astype(jnp.int32)


def draw_adjacency(key, part):
    key = jax.random.fold_in(key, 23)
    picks = jax.random.randint(key, (CLUSTERS, CAP, CAP), 0, 8, dtype=jnp.int32)
    upper = jnp.triu(jnp.where(picks == 0, 1, 0).astype(jnp.int32), 1)
    return (upper + jnp.swapaxes(upper, 1, 2)).astype(jnp.int32)


def shard_levels(key, extent, shards, least, high):
    level = 1.0
    for position, shards_of in shards:
        heights = jax.random.uniform(jax.random.fold_in(jax.random.fold_in(key, 6), position), (shards_of,), jnp.float32, least / len(shards), high / len(shards))
        level = level * jnp.repeat(jnp.exp(heights), extent[position] // shards_of).reshape((-1,) + (1,) * (len(extent) - 1 - position))
    return level


def bell_draw(rng, dims, spread, limit, cuts=(), kind=jnp.bfloat16):
    values = jax.random.normal(rng, dims, jnp.float32) * spread
    if len(cuts) > 0:
        values = shard_levels(rng, dims, cuts, -0.22, 0.18) * values
    return jnp.clip(values, min=-limit, max=limit).astype(kind)


def setup_inputs(seed: int = 0) -> dict:
    arg_keys = jax.random.split(jax.random.key(seed), 15)
    features = bell_draw(arg_keys[0], (NODES, F), 1.0, 6.0, ((0, 32),))
    adjacency = draw_adjacency(jax.random.fold_in(arg_keys[14], 71), 0)
    counts = draw_counts(jax.random.fold_in(arg_keys[14], 71), 0)
    input_weight = bell_draw(arg_keys[3], (F, D), F ** -0.5, 0.5, ((0, 16),))
    first_gain = jnp.clip(1.0 + 0.1 * jax.random.normal(arg_keys[4], (D,), jnp.float32), 0.5, 1.5).astype(jnp.bfloat16)
    first_shift = bell_draw(arg_keys[5], (D,), 0.3, 1.75, ((0, 16),))
    attend_weight = bell_draw(arg_keys[6], (D, 3 * D), D ** -0.5, 0.25, ((0, 16),))
    merge_weight = bell_draw(arg_keys[7], (D, D), (D // 8) ** -0.5, 0.75, ((0, 16),))
    second_gain = jnp.clip(1.0 + 0.1 * jax.random.normal(arg_keys[8], (D,), jnp.float32), 0.5, 1.5).astype(jnp.bfloat16)
    second_shift = bell_draw(arg_keys[9], (D,), 0.3, 1.75, ((0, 16),))
    expand_weight = bell_draw(arg_keys[10], (D, FF), D ** -0.5, 0.25, ((0, 16),))
    reduce_weight = bell_draw(arg_keys[11], (FF, D), FF ** -0.5, 0.1875, ((0, 16),))
    readout_weight = bell_draw(arg_keys[12], (2 * D,), D ** -0.5, 0.25, ((0, 16),))
    cotangent = bell_draw(arg_keys[13], (NODES, D), 1.0, 6.0, ((0, 32),), jnp.float32)
    return {"features": features, "adjacency": adjacency, "counts": counts, "input_weight": input_weight, "first_gain": first_gain, "first_shift": first_shift, "attend_weight": attend_weight, "merge_weight": merge_weight, "second_gain": second_gain, "second_shift": second_shift, "expand_weight": expand_weight, "reduce_weight": reduce_weight, "readout_weight": readout_weight, "cotangent": cotangent}


@jax.custom_vjp
def low(v):
    return lax.optimization_barrier(v.astype(jnp.bfloat16)).astype(jnp.float32)

@jax.custom_vjp
def low_back(v):
    return v

def low_keep(v):
    return (low(v), None)

def low_pass(kept, grad):
    return (grad,)

def back_keep(v):
    return (v, None)

def back_low(kept, grad):
    return (low(grad),)
low.defvjp(low_keep, low_pass)
low_back.defvjp(back_keep, back_low)
highest = lax.Precision.HIGHEST

def norm_rows(values_in, gain_row, shift_row):
    row_mean = lax.optimization_barrier(jnp.mean(values_in, axis=-1, keepdims=True))
    centred = values_in - row_mean
    row_var = lax.optimization_barrier(jnp.mean(centred * centred, axis=-1, keepdims=True))
    return centred * lax.rsqrt(row_var + 1e-05) * gain_row + shift_row

def hop_operator(adjacency, counts):
    slot_index = jnp.arange(adjacency.shape[-1], dtype=jnp.int32)
    valid_mask = (slot_index[None, :] < counts[:, None]).astype(jnp.float32)
    link_matrix = adjacency.astype(jnp.float32) * valid_mask[:, :, None] * valid_mask[:, None, :]
    link_matrix = link_matrix + jnp.eye(adjacency.shape[-1], dtype=jnp.float32)
    root_scale = lax.rsqrt(lax.optimization_barrier(jnp.sum(link_matrix, axis=-1)))
    return (link_matrix * root_scale[:, :, None] * root_scale[:, None, :], valid_mask)

def read_nodes(third_sum, readout, keep_mask):
    model_width = third_sum.shape[-1]
    centre = third_sum[:, 0]
    others = third_sum[:, 1:]
    logits = jnp.dot(centre, readout[:model_width], precision=highest)[:, None]
    logits = logits + jnp.einsum('nkd,d->nk', others, readout[model_width:], precision=highest)
    hop_weights = jax.nn.softmax(logits, axis=-1)
    return (centre + jnp.einsum('nk,nkd->nd', hop_weights, others, precision=highest)) * keep_mask

def forward_block(params, feature_block, operator, valid_mask):
    embedder, gain_one, shift_one, attend, merger, gain_two, shift_two, expand, reducer, readout = params
    hop_state = feature_block * valid_mask[:, :, None]
    hop_list = [hop_state]
    for hop_step in range(HOPS):
        hop_state = jnp.einsum('cij,cjf->cif', operator, hop_state, precision=highest)
        hop_list.append(hop_state)
    stacked = jnp.stack(hop_list, axis=2).reshape(-1, HOPS + 1, F)
    node_count = stacked.shape[0]
    hidden = low_back(jnp.einsum('ntf,fd->ntd', low(stacked), embedder, precision=highest))
    normed = low(norm_rows(hidden, gain_one, shift_one))
    triple = low(low_back(jnp.einsum('ntd,de->nte', normed, attend, precision=highest)))
    shaped = triple.reshape(node_count, HOPS + 1, 3, HEADS, HEAD)
    scores = low_back(HEAD ** (-0.5) * jnp.einsum('nihd,njhd->nhij', shaped[:, :, 0], shaped[:, :, 1], precision=highest))
    prob_rows = jax.nn.softmax(scores, axis=-1)
    mixed_heads = jnp.einsum('nhij,njhd->nihd', low(prob_rows), shaped[:, :, 2], precision=highest)
    mixed_heads = low(low_back(mixed_heads.reshape(node_count, HOPS + 1, D)))
    second = hidden + low_back(jnp.einsum('ntd,de->nte', mixed_heads, merger, precision=highest))
    inner = low(norm_rows(second, gain_two, shift_two))
    before = low_back(jnp.einsum('ntd,de->nte', inner, expand, precision=highest))
    after = low(jax.nn.gelu(before))
    third_sum = second + low_back(jnp.einsum('nte,ed->ntd', after, reducer, precision=highest))
    return read_nodes(third_sum, readout, valid_mask.reshape(-1)[:, None])

def reference(features, adjacency, counts, input_weight, first_gain, first_shift, attend_weight, merge_weight, second_gain, second_shift, expand_weight, reduce_weight, readout_weight, cotangent):
    params = tuple((matrix.astype(jnp.float32) for matrix in (input_weight, first_gain, first_shift, attend_weight, merge_weight, second_gain, second_shift, expand_weight, reduce_weight, readout_weight)))
    operator, valid_mask = hop_operator(adjacency, counts)
    block_count = CLUSTERS // 2
    operator = operator.reshape(block_count, 2, CAP, CAP)
    valid_mask = valid_mask.reshape(block_count, 2, CAP)
    feature_blocks = features.astype(jnp.float32).reshape(block_count, 2, CAP, F)
    block_fn = jax.checkpoint(forward_block)

    def whole(params_in, blocks_in):
        return lax.map(lambda block_item: block_fn(params_in, block_item[0], block_item[1], block_item[2]), (blocks_in, operator, valid_mask))
    node_output, pull_back = jax.vjp(whole, params, feature_blocks)
    grad_params, grad_blocks = pull_back(cotangent.reshape(block_count, 2 * CAP, D))
    return (node_output.reshape(NODES, D), grad_blocks.reshape(NODES, F), grad_params[0], grad_params[1], grad_params[2], grad_params[3], grad_params[4], grad_params[5], grad_params[6], grad_params[7], grad_params[8], grad_params[9])
```

```python
import functools

import jax
import jax.numpy as jnp
from jax import lax
from jax.experimental import pallas as pl
from jax.experimental.pallas import tpu as pltpu
from jax.sharding import PartitionSpec as P

HEADS = 8
HEAD = 64
HOPS = 7
HOP_TOKENS = HOPS + 1
NODES_PER_TILE = 64
TOKENS = NODES_PER_TILE * HOP_TOKENS
GROUP = 16
MIB = 1 << 20
F32 = jnp.float32
BF16 = jnp.bfloat16
GELU_A = 0.7978845608028654
GELU_B = 0.044715


def dot(left, right):
    return jnp.dot(left, right, preferred_element_type=F32)


def dot_lead(left, right):
    return lax.dot_general(left, right, (((0,), (0,)), ((), ())), preferred_element_type=F32)


def dot_last(left, right):
    return lax.dot_general(left, right, (((1,), (1,)), ((), ())), preferred_element_type=F32)


def link_of(adjacency, count):
    slots = adjacency.shape[0]
    rows = lax.broadcasted_iota(jnp.int32, (slots, slots), 0)
    cols = lax.broadcasted_iota(jnp.int32, (slots, slots), 1)
    live = jnp.logical_and(rows < count, cols < count)
    link = jnp.where(live, adjacency, 0) + jnp.where(rows == cols, 1, 0)
    link = link.astype(F32)
    root = lax.rsqrt(jnp.sum(link, axis=-1, keepdims=True))
    return link.astype(BF16), root


def hop(link, root, state):
    width = state.shape[1]
    scaled = state * root
    high = scaled.astype(BF16)
    rest = scaled - high.astype(F32)
    middle = rest.astype(BF16)
    low = (rest - middle.astype(F32)).astype(BF16)
    spread = dot(link, jnp.concatenate([high, middle, low], axis=1))
    return (spread[:, :width] + (spread[:, width : 2 * width] + spread[:, 2 * width :])) * root


def live_rows(count, first, rows):
    index = lax.broadcasted_iota(jnp.int32, (rows, 1), 0) + first
    return jnp.where(index < count, 1.0, 0.0).astype(F32)


def norm_stats(values):
    mean = jnp.mean(values, axis=-1, keepdims=True)
    centred = values - mean
    var = jnp.mean(centred * centred, axis=-1, keepdims=True)
    inv = lax.rsqrt(var + 1e-05)
    return centred * inv, inv


def head_masks():
    lane = lax.broadcasted_iota(jnp.int32, (GROUP * HOP_TOKENS, 2 * HEAD), 1)
    return lane < HEAD


def pair_stack(block, first_half):
    zero = jnp.zeros_like(block)
    return jnp.concatenate(
        [jnp.where(first_half, block, zero), jnp.where(first_half, zero, block)], axis=0
    )


def same_node():
    span = GROUP * HOP_TOKENS
    row = lax.broadcasted_iota(jnp.int32, (span, span), 0) % GROUP
    col = lax.broadcasted_iota(jnp.int32, (span, span), 1) % GROUP
    return row == col


def pair_probs(queries, key_stack, keep):
    span = GROUP * HOP_TOKENS
    scores = dot_last(queries, key_stack)
    halves = []
    for half in range(2):
        part = jnp.where(keep, scores[:, half * span : (half + 1) * span], -jnp.inf)
        top = jnp.max(part, axis=-1, keepdims=True)
        power = jnp.exp((part - top) * HEAD ** (-0.5))
        halves.append(power * (1.0 / jnp.sum(power, axis=-1, keepdims=True)))
    return halves


def read_block(ref, group, first):
    rows = pl.ds(pl.multiple_of(group * GROUP, GROUP), GROUP)
    return ref[:, rows, first : first + 2 * HEAD].reshape(GROUP * HOP_TOKENS, 2 * HEAD)


def write_block(ref, group, first, block):
    rows = pl.ds(pl.multiple_of(group * GROUP, GROUP), GROUP)
    ref[:, rows, first : first + 2 * HEAD] = block.reshape(HOP_TOKENS, GROUP, 2 * HEAD)


def forward_kernel(
    counts_ref,
    adjacency_ref,
    features_ref,
    embed_ref,
    gain_ref,
    shift_ref,
    attend_ref,
    merge_ref,
    stacked_ref,
    hidden_ref,
    normed_ref,
    triple_ref,
    mixed_ref,
    second_ref,
):
    step = pl.program_id(0)
    clusters, slots = adjacency_ref.shape[:2]
    width = hidden_ref.shape[-1]
    per_cluster = slots // NODES_PER_TILE

    @pl.when(step == 0)
    def _():
        links = []
        states = []
        for cluster in range(clusters):
            count = counts_ref[cluster]
            links.append(link_of(adjacency_ref[cluster], count))
            states.append(
                features_ref[cluster * slots : (cluster + 1) * slots].astype(F32)
                * live_rows(count, 0, slots)
            )
        for index in range(HOP_TOKENS):
            for cluster in range(clusters):
                if index > 0:
                    states[cluster] = hop(*links[cluster], states[cluster])
                rounded = states[cluster].astype(BF16)
                for part in range(per_cluster):
                    stacked_ref[cluster * per_cluster + part, index] = rounded[
                        part * NODES_PER_TILE : (part + 1) * NODES_PER_TILE
                    ]

    stacked = stacked_ref[step].reshape(TOKENS, stacked_ref.shape[-1])
    hidden = dot(stacked, embed_ref[...])
    hidden_ref[...] = hidden
    normal, _ = norm_stats(hidden)
    normed = (normal * gain_ref[...] + shift_ref[...]).astype(BF16)
    normed_ref[...] = normed
    triple = dot(normed, attend_ref[...]).astype(BF16)
    triple_ref[...] = triple.reshape(triple_ref.shape)
    first_half = head_masks()
    keep = same_node()

    def group_step(group, carry):
        for first in range(0, width, 2 * HEAD):
            queries = read_block(triple_ref, group, first)
            keys = pair_stack(read_block(triple_ref, group, width + first), first_half)
            values = pair_stack(read_block(triple_ref, group, 2 * width + first), first_half)
            probs = pair_probs(queries, keys, keep)
            rounded = jnp.concatenate([half.astype(BF16) for half in probs], axis=1)
            write_block(mixed_ref, group, first, dot(rounded, values).astype(BF16))
        return carry

    lax.fori_loop(0, NODES_PER_TILE // GROUP, group_step, 0)
    mixed = mixed_ref[...].reshape(TOKENS, width)
    second_ref[...] = hidden_ref[...] + dot(mixed, merge_ref[...])


def middle_kernel(
    counts_ref,
    second_ref,
    mixed_ref,
    cotangent_ref,
    gain_ref,
    shift_ref,
    expand_ref,
    reduce_ref,
    readout_ref,
    output_ref,
    grad_second_ref,
    grad_merge_ref,
    grad_gain_ref,
    grad_shift_ref,
    grad_expand_ref,
    grad_reduce_ref,
    grad_readout_ref,
):
    step = pl.program_id(0)
    width = second_ref.shape[-1]
    per_cluster = 128 // NODES_PER_TILE

    @pl.when(step == 0)
    def _():
        for ref in (
            grad_merge_ref,
            grad_gain_ref,
            grad_shift_ref,
            grad_expand_ref,
            grad_reduce_ref,
            grad_readout_ref,
        ):
            ref[...] = jnp.zeros_like(ref)

    second = second_ref[...]
    normal, inv = norm_stats(second)
    inner = (normal * gain_ref[...] + shift_ref[...]).astype(BF16)
    before = dot(inner, expand_ref[...])
    square = before * before
    curve = jnp.tanh(GELU_A * before * (1.0 + GELU_B * square))
    after = (0.5 * before * (1.0 + curve)).astype(BF16)
    slope = 0.5 * (1.0 + curve) + (0.5 * GELU_A) * before * (1.0 - curve * curve) * (
        1.0 + (3.0 * GELU_B) * square
    )
    third = second + dot(after, reduce_ref[...])
    shaped = third.reshape(HOP_TOKENS, NODES_PER_TILE, width)
    keep = live_rows(
        counts_ref[step // per_cluster], (step % per_cluster) * NODES_PER_TILE, NODES_PER_TILE
    )
    centre = shaped[0]
    row_node = readout_ref[0:1]
    row_hop = readout_ref[1:2]
    base = jnp.sum(centre * row_node, axis=-1, keepdims=True)
    logits = [
        base + jnp.sum(shaped[k] * row_hop, axis=-1, keepdims=True) for k in range(1, HOP_TOKENS)
    ]
    top = functools.reduce(jnp.maximum, logits)
    powers = [jnp.exp(logit - top) for logit in logits]
    scale = 1.0 / functools.reduce(jnp.add, powers)
    shares = [power * scale for power in powers]
    total = centre
    for k in range(1, HOP_TOKENS):
        total = total + shares[k - 1] * shaped[k]
    output_ref[...] = total * keep
    cotangent = cotangent_ref[...] * keep
    grad_shares = [
        jnp.sum(cotangent * shaped[k], axis=-1, keepdims=True) for k in range(1, HOP_TOKENS)
    ]
    mean_share = functools.reduce(jnp.add, [s * g for s, g in zip(shares, grad_shares)])
    grad_logits = [s * (g - mean_share) for s, g in zip(shares, grad_shares)]
    grad_base = functools.reduce(jnp.add, grad_logits)
    parts = [cotangent + grad_base * row_node]
    read_hop = jnp.zeros((NODES_PER_TILE, width), F32)
    for k in range(1, HOP_TOKENS):
        parts.append(shares[k - 1] * cotangent + grad_logits[k - 1] * row_hop)
        read_hop = read_hop + grad_logits[k - 1] * shaped[k]
    grad_readout_ref[0:1] += jnp.sum(grad_base * centre, axis=0, keepdims=True)
    grad_readout_ref[1:2] += jnp.sum(read_hop, axis=0, keepdims=True)
    grad_third = jnp.concatenate(parts, axis=0)
    grad_branch = grad_third.astype(BF16)
    grad_reduce_ref[...] += dot_lead(after, grad_branch)
    grad_before = (slope * dot_last(grad_branch, reduce_ref[...])).astype(BF16)
    grad_expand_ref[...] += dot_lead(inner, grad_before)
    grad_inner = dot_last(grad_before, expand_ref[...])
    grad_gain_ref[...] += jnp.sum(grad_inner * normal, axis=0, keepdims=True)
    grad_shift_ref[...] += jnp.sum(grad_inner, axis=0, keepdims=True)
    grad_normal = grad_inner * gain_ref[...]
    grad_second = grad_third + inv * (
        grad_normal
        - jnp.mean(grad_normal, axis=-1, keepdims=True)
        - normal * jnp.mean(grad_normal * normal, axis=-1, keepdims=True)
    )
    grad_second_ref[...] = grad_second
    grad_merge_ref[...] += dot_lead(mixed_ref[...].reshape(TOKENS, width), grad_second.astype(BF16))


def backward_kernel(
    counts_ref,
    adjacency_ref,
    stacked_ref,
    hidden_ref,
    normed_ref,
    triple_ref,
    grad_second_ref,
    embed_ref,
    gain_ref,
    attend_ref,
    merge_ref,
    grad_features_ref,
    grad_embed_ref,
    grad_gain_ref,
    grad_shift_ref,
    grad_attend_ref,
    grad_mixed_ref,
    grad_triple_ref,
    grad_stacked_ref,
):
    step = pl.program_id(0)
    steps = pl.num_programs(0)
    clusters, slots = adjacency_ref.shape[:2]
    width = hidden_ref.shape[-1]
    per_cluster = slots // NODES_PER_TILE

    @pl.when(step == 0)
    def _():
        for ref in (grad_embed_ref, grad_gain_ref, grad_shift_ref, grad_attend_ref):
            ref[...] = jnp.zeros_like(ref)

    grad_second = grad_second_ref[...]
    grad_mixed = dot_last(grad_second.astype(BF16), merge_ref[...]).astype(BF16)
    grad_mixed_ref[...] = grad_mixed.reshape(grad_mixed_ref.shape)
    first_half = head_masks()
    keep = same_node()
    span = GROUP * HOP_TOKENS

    def group_step(group, carry):
        for first in range(0, width, 2 * HEAD):
            queries = read_block(triple_ref, group, first)
            keys = pair_stack(read_block(triple_ref, group, width + first), first_half)
            values = pair_stack(read_block(triple_ref, group, 2 * width + first), first_half)
            out_grad = read_block(grad_mixed_ref, group, first)
            probs = pair_probs(queries, keys, keep)
            grad_probs = dot_last(out_grad, values)
            grad_halves = []
            for half in range(2):
                part = grad_probs[:, half * span : (half + 1) * span]
                weighted = probs[half] * part
                grad_halves.append(
                    (weighted - probs[half] * jnp.sum(weighted, axis=-1, keepdims=True)).astype(
                        BF16
                    )
                )
            grad_scores = jnp.concatenate(grad_halves, axis=1)
            grad_query = dot(grad_scores, keys) * HEAD ** (-0.5)
            grad_key = dot_lead(
                jnp.concatenate(grad_halves, axis=0), pair_stack(queries, first_half)
            ) * HEAD ** (-0.5)
            grad_value = dot_lead(
                jnp.concatenate([half.astype(BF16) for half in probs], axis=0),
                pair_stack(out_grad, first_half),
            )
            write_block(grad_triple_ref, group, first, grad_query.astype(BF16))
            write_block(grad_triple_ref, group, width + first, grad_key.astype(BF16))
            write_block(grad_triple_ref, group, 2 * width + first, grad_value.astype(BF16))
        return carry

    lax.fori_loop(0, NODES_PER_TILE // GROUP, group_step, 0)
    grad_triple = grad_triple_ref[...].reshape(TOKENS, 3 * width)
    grad_attend_ref[...] += dot_lead(normed_ref[...], grad_triple)
    grad_normed = dot_last(grad_triple, attend_ref[...])
    normal, inv = norm_stats(hidden_ref[...])
    grad_gain_ref[...] += jnp.sum(grad_normed * normal, axis=0, keepdims=True)
    grad_shift_ref[...] += jnp.sum(grad_normed, axis=0, keepdims=True)
    grad_normal = grad_normed * gain_ref[...]
    grad_hidden = grad_second_ref[...] + inv * (
        grad_normal
        - jnp.mean(grad_normal, axis=-1, keepdims=True)
        - normal * jnp.mean(grad_normal * normal, axis=-1, keepdims=True)
    )
    grad_hidden = grad_hidden.astype(BF16)
    stacked = stacked_ref[...].reshape(TOKENS, stacked_ref.shape[-1])
    grad_embed_ref[...] += dot_lead(stacked, grad_hidden)
    grad_stacked_ref[step] = dot_last(grad_hidden, embed_ref[...]).reshape(
        grad_stacked_ref.shape[1:]
    )

    @pl.when(step == steps - 1)
    def _():
        links = []
        states = []

        def hop_grad(cluster, index):
            return jnp.concatenate(
                [grad_stacked_ref[cluster * per_cluster + p, index] for p in range(per_cluster)],
                axis=0,
            )

        for cluster in range(clusters):
            links.append(link_of(adjacency_ref[cluster], counts_ref[cluster]))
            states.append(hop_grad(cluster, HOPS))
        for index in range(HOPS - 1, -1, -1):
            for cluster in range(clusters):
                states[cluster] = hop_grad(cluster, index) + hop(*links[cluster], states[cluster])
        for cluster in range(clusters):
            grad_features_ref[cluster * slots : (cluster + 1) * slots] = states[
                cluster
            ] * live_rows(counts_ref[cluster], 0, slots)


def whole(shape):
    return pl.BlockSpec(shape, lambda t: (0,) * len(shape), pipeline_mode=pl.Buffered(1))


def kept(shape):
    return pl.BlockSpec(shape, lambda t: (0,) * len(shape))


def tiled(*shape):
    return pl.BlockSpec((None,) + shape, lambda t: (t,) + (0,) * len(shape))


def rows_of(*shape):
    return pl.BlockSpec(shape, lambda t: (t,) + (0,) * (len(shape) - 1))


def sds(shape, dtype):
    return jax.ShapeDtypeStruct(shape, dtype)


SMEM_SPEC = pl.BlockSpec(memory_space=pltpu.SMEM)


def params():
    return pltpu.CompilerParams(
        vmem_limit_bytes=56 * MIB, dimension_semantics=("arbitrary",)
    )


def forward_part(counts, adjacency, features, embed, gain, shift, attend, merge):
    nodes, feat = features.shape
    width = merge.shape[0]
    tiles = nodes // NODES_PER_TILE
    hops, per = HOP_TOKENS, NODES_PER_TILE
    return pl.pallas_call(
        forward_kernel,
        grid=(tiles,),
        in_specs=[
            SMEM_SPEC,
            whole(adjacency.shape),
            whole(features.shape),
            whole(embed.shape),
            whole(gain.shape),
            whole(shift.shape),
            whole(attend.shape),
            whole(merge.shape),
        ],
        out_specs=[
            kept((tiles, hops, per, feat)),
            tiled(TOKENS, width),
            tiled(TOKENS, width),
            rows_of(hops, per, 3 * width),
            rows_of(hops, per, width),
            tiled(TOKENS, width),
        ],
        out_shape=[
            sds((tiles, hops, per, feat), BF16),
            sds((tiles, TOKENS, width), F32),
            sds((tiles, TOKENS, width), BF16),
            sds((tiles * hops, per, 3 * width), BF16),
            sds((tiles * hops, per, width), BF16),
            sds((tiles, TOKENS, width), F32),
        ],
        compiler_params=params(),
        name="hops_attention",
    )(counts, adjacency, features, embed, gain, shift, attend, merge)


def middle_part(counts, second, mixed, cotangent, gain, shift, expand, reducer, readout):
    tiles, _, width = second.shape
    hops, per = HOP_TOKENS, NODES_PER_TILE
    grads = [
        (width, width),
        (1, width),
        (1, width),
        expand.shape,
        reducer.shape,
        readout.shape,
    ]
    return pl.pallas_call(
        middle_kernel,
        grid=(tiles,),
        in_specs=[
            SMEM_SPEC,
            tiled(TOKENS, width),
            rows_of(hops, per, width),
            rows_of(per, width),
            whole(gain.shape),
            whole(shift.shape),
            whole(expand.shape),
            whole(reducer.shape),
            whole(readout.shape),
        ],
        out_specs=[rows_of(per, width), tiled(TOKENS, width)] + [kept(shape) for shape in grads],
        out_shape=[sds(cotangent.shape, F32), sds(second.shape, F32)]
        + [sds(shape, F32) for shape in grads],
        compiler_params=params(),
        name="feed_forward",
    )(counts, second, mixed, cotangent, gain, shift, expand, reducer, readout)


def backward_part(
    counts, adjacency, stacked, hidden, normed, triple, grad_second, embed, gain, attend, merge
):
    tiles, _, width = hidden.shape
    hops, per = HOP_TOKENS, NODES_PER_TILE
    feat = stacked.shape[-1]
    grads = [(tiles * per, feat), embed.shape, (1, width), (1, width), attend.shape]
    return pl.pallas_call(
        backward_kernel,
        grid=(tiles,),
        in_specs=[
            SMEM_SPEC,
            whole(adjacency.shape),
            tiled(hops, per, feat),
            tiled(TOKENS, width),
            tiled(TOKENS, width),
            rows_of(hops, per, 3 * width),
            tiled(TOKENS, width),
            whole(embed.shape),
            whole(gain.shape),
            whole(attend.shape),
            whole(merge.shape),
        ],
        out_specs=[kept(shape) for shape in grads],
        out_shape=[sds(shape, F32) for shape in grads],
        scratch_shapes=[
            pltpu.VMEM((hops, per, width), BF16),
            pltpu.VMEM((hops, per, 3 * width), BF16),
            pltpu.VMEM((tiles, hops, per, feat), F32),
        ],
        compiler_params=params(),
        name="attention_backward",
    )(counts, adjacency, stacked, hidden, normed, triple, grad_second, embed, gain, attend, merge)


def local_layer(
    features,
    adjacency,
    counts,
    embed,
    gain_one,
    shift_one,
    attend,
    merge,
    gain_two,
    shift_two,
    expand,
    reducer,
    readout,
    cotangent,
):
    row = lambda v: v.astype(F32).reshape(1, -1)
    gain_one, shift_one, gain_two, shift_two = map(row, (gain_one, shift_one, gain_two, shift_two))
    readout = readout.astype(F32).reshape(2, -1)
    stacked, hidden, normed, triple, mixed, second = forward_part(
        counts, adjacency, features, embed, gain_one, shift_one, attend, merge
    )
    (
        output,
        grad_second,
        grad_merge,
        grad_gain_two,
        grad_shift_two,
        grad_expand,
        grad_reduce,
        grad_readout,
    ) = middle_part(
        counts, second, mixed, cotangent, gain_two, shift_two, expand, reducer, readout
    )
    grad_features, grad_embed, grad_gain_one, grad_shift_one, grad_attend = backward_part(
        counts, adjacency, stacked, hidden, normed, triple, grad_second, embed, gain_one, attend, merge
    )
    return (
        output,
        grad_features,
        grad_embed,
        grad_gain_one.reshape(-1),
        grad_shift_one.reshape(-1),
        grad_attend,
        grad_merge,
        grad_gain_two.reshape(-1),
        grad_shift_two.reshape(-1),
        grad_expand,
        grad_reduce,
        grad_readout.reshape(-1),
    )


def gather(block):
    return lax.all_gather(block, "fsdp", axis=0, tiled=True)


def share(term):
    part = lax.psum_scatter(term.astype(BF16), "fsdp", scatter_dimension=0, tiled=True)
    return lax.psum(part.astype(F32), "grp")


def body(
    features,
    adjacency,
    counts,
    input_weight,
    first_gain,
    first_shift,
    attend_weight,
    merge_weight,
    second_gain,
    second_shift,
    expand_weight,
    reduce_weight,
    readout_weight,
    cotangent,
):
    vectors = (first_gain, first_shift, second_gain, second_shift, readout_weight)
    lengths = [v.shape[0] for v in vectors]
    places = [sum(lengths[:i]) for i in range(len(lengths) + 1)]
    packed = lax.all_gather(jnp.concatenate(vectors), "fsdp", axis=0, tiled=False)
    full = [
        packed[:, places[i] : places[i + 1]].reshape(-1) for i in range(len(lengths))
    ]
    terms = local_layer(
        features,
        adjacency,
        counts,
        gather(input_weight),
        full[0],
        full[1],
        gather(attend_weight),
        gather(merge_weight),
        full[2],
        full[3],
        gather(expand_weight),
        gather(reduce_weight),
        full[4],
        cotangent,
    )
    output, grad_features, *grads = terms
    small = [1, 2, 5, 6, 9]
    parts = packed.shape[0]
    packed_grad = jnp.concatenate([grads[i].reshape(parts, -1) for i in small], axis=1)
    packed_grad = lax.psum(
        lax.psum_scatter(packed_grad, "fsdp", scatter_dimension=0, tiled=True), "grp"
    ).reshape(-1)
    shares = [None if i in small else share(grad) for i, grad in enumerate(grads)]
    for place, i in enumerate(small):
        shares[i] = packed_grad[places[place] : places[place + 1]]
    return (output, grad_features, *shares)


def solution(mesh):
    nodes = ("grp", "fsdp")
    rows = P("fsdp", None)
    vector = P("fsdp")
    in_specs = (
        P(nodes, None),
        P(nodes, None, None),
        P(nodes),
        rows,
        vector,
        vector,
        rows,
        rows,
        vector,
        vector,
        rows,
        rows,
        vector,
        P(nodes, None),
    )
    out_specs = (
        P(nodes, None),
        P(nodes, None),
        rows,
        vector,
        vector,
        rows,
        rows,
        vector,
        vector,
        rows,
        rows,
        vector,
    )
    return jax.shard_map(body, mesh=mesh, in_specs=in_specs, out_specs=out_specs, check_vma=False)
```

```python
import functools

import jax
import jax.numpy as jnp
from jax import lax
from jax.experimental import pallas as pl
from jax.experimental.pallas import tpu as pltpu
from jax.sharding import PartitionSpec as P

HEADS = 8
HEAD = 64
HOPS = 7
HOP_TOKENS = HOPS + 1
NODES_PER_TILE = 64
TOKENS = NODES_PER_TILE * HOP_TOKENS
GROUP = 16
MIB = 1 << 20
F32 = jnp.float32
BF16 = jnp.bfloat16
GELU_A = 0.7978845608028654
GELU_B = 0.044715
PLANE = 4
PACK = 16
MESH = pl.DeviceIdType.MESH


def dot(left, right):
    return jnp.dot(left, right, preferred_element_type=F32)


def dot_lead(left, right):
    return lax.dot_general(left, right, (((0,), (0,)), ((), ())), preferred_element_type=F32)


def dot_last(left, right):
    return lax.dot_general(left, right, (((1,), (1,)), ((), ())), preferred_element_type=F32)


def link_of(adjacency, count):
    slots = adjacency.shape[0]
    rows = lax.broadcasted_iota(jnp.int32, (slots, slots), 0)
    cols = lax.broadcasted_iota(jnp.int32, (slots, slots), 1)
    live = jnp.logical_and(rows < count, cols < count)
    link = jnp.where(live, adjacency, 0) + jnp.where(rows == cols, 1, 0)
    link = link.astype(F32)
    root = lax.rsqrt(jnp.sum(link, axis=-1, keepdims=True))
    return link.astype(BF16), root


def hop(link, root, state):
    width = state.shape[1]
    scaled = state * root
    high = scaled.astype(BF16)
    rest = scaled - high.astype(F32)
    middle = rest.astype(BF16)
    low = (rest - middle.astype(F32)).astype(BF16)
    spread = dot(link, jnp.concatenate([high, middle, low], axis=1))
    return (spread[:, :width] + (spread[:, width : 2 * width] + spread[:, 2 * width :])) * root


def live_rows(count, first, rows):
    index = lax.broadcasted_iota(jnp.int32, (rows, 1), 0) + first
    return jnp.where(index < count, 1.0, 0.0).astype(F32)


def norm_stats(values):
    mean = jnp.mean(values, axis=-1, keepdims=True)
    centred = values - mean
    var = jnp.mean(centred * centred, axis=-1, keepdims=True)
    inv = lax.rsqrt(var + 1e-05)
    return centred * inv, inv


def head_masks():
    lane = lax.broadcasted_iota(jnp.int32, (GROUP * HOP_TOKENS, 2 * HEAD), 1)
    return lane < HEAD


def pair_stack(block, first_half):
    zero = jnp.zeros_like(block)
    return jnp.concatenate(
        [jnp.where(first_half, block, zero), jnp.where(first_half, zero, block)], axis=0
    )


def same_node():
    span = GROUP * HOP_TOKENS
    row = lax.broadcasted_iota(jnp.int32, (span, span), 0) % GROUP
    col = lax.broadcasted_iota(jnp.int32, (span, span), 1) % GROUP
    return row == col


def pair_probs(queries, key_stack, keep):
    span = GROUP * HOP_TOKENS
    scores = dot_last(queries, key_stack)
    halves = []
    for half in range(2):
        part = jnp.where(keep, scores[:, half * span : (half + 1) * span], -jnp.inf)
        top = jnp.max(part, axis=-1, keepdims=True)
        power = jnp.exp((part - top) * HEAD ** (-0.5))
        halves.append(power * (1.0 / jnp.sum(power, axis=-1, keepdims=True)))
    return halves


def read_block(ref, group, first):
    rows = pl.ds(pl.multiple_of(group * GROUP, GROUP), GROUP)
    return ref[:, rows, first : first + 2 * HEAD].reshape(GROUP * HOP_TOKENS, 2 * HEAD)


def write_block(ref, group, first, block):
    rows = pl.ds(pl.multiple_of(group * GROUP, GROUP), GROUP)
    ref[:, rows, first : first + 2 * HEAD] = block.reshape(HOP_TOKENS, GROUP, 2 * HEAD)


class Place:
    def __init__(self, lines):
        self.lines = lines
        self.core = lax.axis_index("grp")
        self.owner = lax.axis_index("fsdp")
        self.line = lax.div(self.owner, PLANE)
        self.spot = lax.rem(self.owner, PLANE)

    def line_turn(self, ahead):
        return lax.rem(self.line + ahead + self.lines, self.lines)

    def spot_turn(self, ahead):
        return lax.rem(self.spot + ahead + PLANE, PLANE)

    def line_peer(self, ahead):
        return (self.core, self.line_turn(ahead) * PLANE + self.spot)

    def plane_peer(self, ahead):
        return (self.core, self.line * PLANE + self.spot_turn(ahead))

    def sibling(self):
        return (1 - self.core, self.owner)

    def peers(self):
        return (
            [self.line_peer(d) for d in range(1, self.lines)]
            + [self.plane_peer(e) for e in range(1, PLANE)]
            + [self.sibling()]
        )

    def greet(self):
        barrier = pltpu.get_barrier_semaphore()
        for peer in self.peers():
            pl.semaphore_signal(barrier, inc=1, device_id=peer, device_id_type=MESH)

    def greeted(self):
        pl.semaphore_wait(pltpu.get_barrier_semaphore(), self.lines + PLANE - 1)


def remote(source, target, send, recv, device):
    return pltpu.make_async_remote_copy(
        src_ref=source,
        dst_ref=target,
        send_sem=send,
        recv_sem=recv,
        device_id=device,
        device_id_type=MESH,
    )


class Gather:
    def __init__(self, place, slots, source, send, recv, pair, halves=True):
        self.place, self.slots, self.source = place, slots, source
        self.send, self.recv, self.pair_sems, self.halves = send, recv, pair, halves

    def slot(self, owner):
        return self.slots.at[owner, self.place.core] if self.halves else self.slots.at[owner]

    def own_copies(self):
        place = self.place
        peers = [place.line_peer(d) for d in range(1, place.lines)]
        peers += [place.plane_peer(e) for e in range(1, PLANE)]
        return [
            remote(
                self.source, self.slot(place.owner), self.send.at[i], self.recv.at[place.owner], peer
            )
            for i, peer in enumerate(peers)
        ]

    def onward(self, d):
        place = self.place
        owner = place.line_turn(-d) * PLANE + place.spot
        first = place.lines + PLANE - 2 + (d - 1) * (PLANE - 1)
        return [
            remote(
                self.slot(owner),
                self.slot(owner),
                self.send.at[first + e - 1],
                self.recv.at[owner],
                place.plane_peer(e),
            )
            for e in range(1, PLANE)
        ]

    def start(self):
        for copy in self.own_copies():
            copy.start()

    def forward(self):
        for d in range(1, self.place.lines):
            copies = self.onward(d)
            copies[0].wait_recv()
            for copy in copies:
                copy.start()

    def finish(self):
        place = self.place
        for d in range(place.lines):
            for e in range(1, PLANE):
                owner = place.line_turn(d) * PLANE + place.spot_turn(-e)
                remote(
                    self.slot(owner),
                    self.slot(owner),
                    self.send.at[0],
                    self.recv.at[owner],
                    place.plane_peer(e),
                ).wait_recv()
        for copy in self.own_copies():
            copy.wait_send()
        for d in range(1, place.lines):
            for copy in self.onward(d):
                copy.wait_send()

    def pair(self):
        half = self.slots.at[:, self.place.core]
        return remote(half, half, self.pair_sems.at[0], self.pair_sems.at[1], self.place.sibling())


class Scatter:
    def __init__(self, place, terms, got, chip, plane_got, line_out, line_got, result, sems):
        self.place, self.terms, self.got, self.chip = place, terms, got, chip
        self.plane_got, self.line_out, self.line_got = plane_got, line_out, line_got
        self.result, self.sems = result, sems

    def pair(self):
        place = self.place
        return remote(
            self.terms.at[:, 1 - place.core],
            self.got,
            self.sems.at[0, 0],
            self.sems.at[1, 0],
            place.sibling(),
        )

    def plane(self):
        place = self.place
        return [
            remote(
                self.chip.at[:, place.spot_turn(e)],
                self.plane_got.at[e - 1],
                self.sems.at[0, e],
                self.sems.at[1, e],
                place.plane_peer(e),
            )
            for e in range(1, PLANE)
        ]

    def line(self):
        place = self.place
        return [
            remote(
                self.line_out.at[place.line_turn(d)],
                self.line_got.at[d - 1],
                self.sems.at[0, PLANE + d - 1],
                self.sems.at[1, PLANE + d - 1],
                place.line_peer(d),
            )
            for d in range(1, place.lines)
        ]

    def last(self):
        place = self.place
        half = self.result.at[place.core]
        k = PLANE + place.lines - 1
        return remote(half, half, self.sems.at[0, k], self.sems.at[1, k], place.sibling())

    def begin(self):
        self.pair().start()

    def to_plane(self):
        place = self.place
        self.pair().wait()

        def add(line, carry):
            for spot in range(PLANE):
                owner = line * PLANE + spot
                both = self.terms[owner, place.core].astype(F32) + self.got[owner].astype(F32)
                self.chip[line, spot] = both.astype(BF16)
            return carry

        lax.fori_loop(0, place.lines, add, 0)
        for copy in self.plane():
            copy.start()

    def to_line(self):
        place = self.place
        for copy in self.plane():
            copy.wait()

        def add(line, carry):
            total = self.chip[line, place.spot].astype(F32)
            for e in range(PLANE - 1):
                total = total + self.plane_got[e, line].astype(F32)
            self.line_out[line] = total.astype(BF16)
            return carry

        lax.fori_loop(0, place.lines, add, 0)
        for copy in self.line():
            copy.start()

    def to_sibling(self):
        place = self.place
        for copy in self.line():
            copy.wait()
        total = self.line_out[place.line].astype(F32)
        for d in range(place.lines - 1):
            total = total + self.line_got[d].astype(F32)
        self.result[place.core] = total
        self.last().start()

    def end(self):
        self.last().wait()


class TailScatter:
    def __init__(self, place, own, plane_got, line_out, line_got, mine, other, sems):
        self.place, self.own, self.plane_got, self.line_out = place, own, plane_got, line_out
        self.line_got, self.mine, self.other, self.sems = line_got, mine, other, sems

    def plane(self):
        place = self.place
        return [
            remote(
                self.own.at[place.spot_turn(e)],
                self.plane_got.at[e - 1],
                self.sems.at[0, e],
                self.sems.at[1, e],
                place.plane_peer(e),
            )
            for e in range(1, PLANE)
        ]

    def line(self):
        place = self.place
        return [
            remote(
                self.line_out.at[place.line_turn(d)],
                self.line_got.at[d - 1],
                self.sems.at[0, PLANE + d - 1],
                self.sems.at[1, PLANE + d - 1],
                place.line_peer(d),
            )
            for d in range(1, place.lines)
        ]

    def last(self):
        return remote(
            self.mine, self.other, self.sems.at[0, 0], self.sems.at[1, 0], self.place.sibling()
        )

    def begin(self):
        for copy in self.plane():
            copy.start()

    def to_line(self):
        place = self.place
        for copy in self.plane():
            copy.wait()
        total = self.own[place.spot]
        for e in range(PLANE - 1):
            total = total + self.plane_got[e]
        for line in range(place.lines):
            self.line_out[line, 0] = total[line]
            self.line_out[line, 1] = total[place.lines]
        for copy in self.line():
            copy.start()

    def to_sibling(self):
        place = self.place
        for copy in self.line():
            copy.wait()
        total = self.line_out[place.line]
        for d in range(place.lines - 1):
            total = total + self.line_got[d]
        self.mine[...] = total
        self.last().start()

    def end(self):
        self.last().wait()
        return self.mine[...] + self.other[...]


def hop_states(counts_ref, adjacency_ref, features_ref, stacked_ref):
    clusters, slots = adjacency_ref.shape[:2]
    per_cluster = slots // NODES_PER_TILE
    links = []
    states = []
    for cluster in range(clusters):
        count = counts_ref[cluster]
        links.append(link_of(adjacency_ref[cluster], count))
        states.append(
            features_ref[cluster * slots : (cluster + 1) * slots].astype(F32)
            * live_rows(count, 0, slots)
        )
    for index in range(HOP_TOKENS):
        for cluster in range(clusters):
            if index > 0:
                states[cluster] = hop(*links[cluster], states[cluster])
            rounded = states[cluster].astype(BF16)
            for part in range(per_cluster):
                stacked_ref[cluster * per_cluster + part, index] = rounded[
                    part * NODES_PER_TILE : (part + 1) * NODES_PER_TILE
                ]


def embed_tile(step, stacked_ref, embed, gain, shift, hidden_keep, normed_keep, hidden_ref, normed_ref):
    stacked = stacked_ref[step].reshape(TOKENS, stacked_ref.shape[-1])
    hidden = dot(stacked, embed)
    hidden_keep[step] = hidden
    hidden_ref[...] = hidden
    normal, _ = norm_stats(hidden)
    normed = (normal * gain + shift).astype(BF16)
    normed_keep[step] = normed
    normed_ref[...] = normed


def attend_tile(tile, hidden_keep, normed_keep, attend, merge_of, triple_ref, mixed_ref, second_ref):
    width = hidden_keep.shape[-1]
    triple_ref[...] = dot(normed_keep[tile], attend).astype(BF16).reshape(triple_ref.shape)
    first_half = head_masks()
    keep = same_node()

    def group_step(group, carry):
        for first in range(0, width, 2 * HEAD):
            queries = read_block(triple_ref, group, first)
            keys = pair_stack(read_block(triple_ref, group, width + first), first_half)
            values = pair_stack(read_block(triple_ref, group, 2 * width + first), first_half)
            probs = pair_probs(queries, keys, keep)
            rounded = jnp.concatenate([half.astype(BF16) for half in probs], axis=1)
            write_block(mixed_ref, group, first, dot(rounded, values).astype(BF16))
        return carry

    lax.fori_loop(0, NODES_PER_TILE // GROUP, group_step, 0)
    mixed = mixed_ref[...].reshape(TOKENS, width)
    second_ref[...] = hidden_keep[tile] + dot(mixed, merge_of())


def spread_vectors(small, owners, width):
    rows = small.shape[0]
    lane = lax.broadcasted_iota(jnp.int32, (128, width), 0)
    column = lax.broadcasted_iota(jnp.int32, (128, width), 1)
    row = lax.broadcasted_iota(jnp.int32, (rows, width), 0)
    place = lax.broadcasted_iota(jnp.int32, (rows, width), 1)
    piece = width // owners
    pieces = dot(small, jnp.where(lane == column % piece, 1.0, 0.0).astype(BF16))
    out = []
    for vector in range(4):
        mine = jnp.logical_and(row % 8 == vector, lax.div(row, 8) == lax.div(place, piece))
        out.append(jnp.sum(jnp.where(mine, pieces, 0.0), axis=0, keepdims=True))
    pieces = dot(small, jnp.where(lane == column % (2 * piece), 1.0, 0.0).astype(BF16))
    for first in (0, owners // 2):
        owner = lax.div(place, 2 * piece) + first
        mine = jnp.logical_and(row % 8 == 4, lax.div(row, 8) == owner)
        out.append(jnp.sum(jnp.where(mine, pieces, 0.0), axis=0, keepdims=True))
    return jnp.concatenate(out + [jnp.zeros((2, width), F32)], axis=0)


def forward_kernel(
    lines,
    counts_ref,
    adjacency_ref,
    features_ref,
    embed_shard,
    vector_a,
    vector_b,
    vector_c,
    vector_d,
    vector_e,
    attend_shard,
    merge_shard,
    expand_shard,
    reduce_shard,
    stacked_ref,
    hidden_ref,
    normed_ref,
    triple_ref,
    mixed_ref,
    second_ref,
    rows_ref,
    embed_ref,
    attend_out,
    merge_out,
    expand_slots,
    reduce_slots,
    small_keep,
    head_slots,
    attend_slots,
    merge_slots,
    hidden_keep,
    normed_keep,
    send,
    recv,
    pair,
    local,
):
    step = pl.program_id(0)
    tiles = hidden_keep.shape[0]
    owners = head_slots.shape[0]
    width = hidden_keep.shape[-1]
    place = Place(lines)
    core, owner = place.core, place.owner

    def half_of(shard):
        rows = shard.shape[0] // 2
        return shard.at[pl.ds(pl.multiple_of(core * rows, rows), rows)]

    def gather(index, slots, source, halves=True):
        return Gather(
            place, slots, source, send.at[index], recv.at[index], pair.at[index], halves
        )

    head = gather(0, head_slots, head_slots.at[owner], False)
    attend = gather(1, attend_slots, half_of(attend_shard))
    merge = gather(2, merge_slots, half_of(merge_shard))
    expand = gather(3, expand_slots, half_of(expand_shard))
    reducer = gather(4, reduce_slots, half_of(reduce_shard))
    own_copies = [
        pltpu.make_async_copy(half_of(shard), slots.at[owner, core], local.at[index])
        for index, (shard, slots) in enumerate(
            ((expand_shard, expand_slots), (reduce_shard, reduce_slots))
        )
    ]
    out_copies = [
        pltpu.make_async_copy(attend_slots, attend_out, local.at[2]),
        pltpu.make_async_copy(merge_slots, merge_out, local.at[3]),
    ]

    @pl.when(step == 0)
    def _():
        place.greet()
        small_keep[...] = jnp.zeros_like(small_keep)
        for index, vector in enumerate((vector_a, vector_b, vector_c, vector_d, vector_e)):
            length = vector.shape[0]
            small_keep[index : index + 1, 0:length] = vector[...].astype(F32).reshape(1, length)
        mine = embed_shard[...].astype(F32)
        half_width = width // 2
        packed = jnp.concatenate(
            [
                jnp.concatenate([mine[:, :half_width], small_keep[...]], axis=1),
                jnp.concatenate([mine[:, half_width:], jnp.zeros((8, 128), F32)], axis=1),
            ],
            axis=0,
        )
        head_slots[owner] = packed.astype(BF16)
        attend_slots[owner, core] = half_of(attend_shard)[...]
        merge_slots[owner, core] = half_of(merge_shard)[...]
        hop_states(counts_ref, adjacency_ref, features_ref, stacked_ref)
        place.greeted()
        head.start()
        attend.start()
        merge.start()
        for copy in own_copies:
            copy.start()
        head.forward()
        head.finish()
        whole_head = head_slots[...].astype(F32)
        top = whole_head[:, 0:8].reshape(owners * 8, half_width + 128)
        bottom = whole_head[:, 8:16].reshape(owners * 8, half_width + 128)
        embed_ref[:, :half_width] = top[:, :half_width].astype(BF16)
        embed_ref[:, half_width:] = bottom[:, :half_width].astype(BF16)
        rows_ref[...] = spread_vectors(top[:, half_width:].astype(BF16), owners, width)
        attend.forward()
        merge.forward()

    @pl.when(step < tiles)
    def _():
        embed_tile(
            step,
            stacked_ref,
            embed_ref[...],
            rows_ref[0:1],
            rows_ref[1:2],
            hidden_keep,
            normed_keep,
            hidden_ref,
            normed_ref,
        )

    @pl.when(step == tiles - 1)
    def _():
        attend.finish()
        attend.pair().start()
        merge.finish()
        merge.pair().start()
        for copy in own_copies:
            copy.wait()
        expand.start()
        reducer.start()
        attend.pair().wait()
        merge.pair().wait()
        for copy in out_copies:
            copy.start()

    @pl.when(step == tiles + 1)
    def _():
        expand.forward()
        reducer.forward()

    @pl.when(step == 2 * tiles - 2)
    def _():
        expand.finish()
        expand.pair().start()
        reducer.finish()
        reducer.pair().start()

    @pl.when(step >= tiles)
    def _():
        attend_tile(
            step - tiles,
            hidden_keep,
            normed_keep,
            attend_slots[...].reshape(width, 3 * width),
            lambda: merge_slots[...].reshape(width, width),
            triple_ref,
            mixed_ref,
            second_ref,
        )

    @pl.when(step == 2 * tiles - 1)
    def _():
        expand.pair().wait()
        reducer.pair().wait()
        for copy in out_copies:
            copy.wait()


def forward_alone_kernel(
    counts_ref,
    adjacency_ref,
    features_ref,
    rows_ref,
    embed_ref,
    attend_ref,
    merge_ref,
    stacked_ref,
    hidden_ref,
    normed_ref,
    triple_ref,
    mixed_ref,
    second_ref,
    hidden_keep,
    normed_keep,
):
    step = pl.program_id(0)
    tiles = hidden_keep.shape[0]
    width = hidden_keep.shape[-1]

    @pl.when(step == 0)
    def _():
        hop_states(counts_ref, adjacency_ref, features_ref, stacked_ref)

    @pl.when(step < tiles)
    def _():
        embed_tile(
            step,
            stacked_ref,
            embed_ref[...],
            rows_ref[0:1],
            rows_ref[1:2],
            hidden_keep,
            normed_keep,
            hidden_ref,
            normed_ref,
        )

    @pl.when(step >= tiles)
    def _():
        attend_tile(
            step - tiles,
            hidden_keep,
            normed_keep,
            attend_ref[...].reshape(width, 3 * width),
            lambda: merge_ref[...].reshape(width, width),
            triple_ref,
            mixed_ref,
            second_ref,
        )


def middle_kernel(
    counts_ref,
    second_ref,
    mixed_ref,
    cotangent_ref,
    rows_ref,
    expand_ref,
    reduce_ref,
    output_ref,
    grad_second_ref,
    terms_ref,
    rows_grad_ref,
    grad_merge_ref,
    grad_expand_ref,
    grad_reduce_ref,
):
    step = pl.program_id(0)
    width = second_ref.shape[-1]
    per_cluster = 128 // NODES_PER_TILE
    gain, shift = rows_ref[2:3], rows_ref[3:4]
    expand = expand_ref[...].reshape(width, expand_ref.shape[-1])
    reducer = reduce_ref[...].reshape(expand_ref.shape[-1], width)

    @pl.when(step == 0)
    def _():
        for ref in (rows_grad_ref, grad_merge_ref, grad_expand_ref, grad_reduce_ref):
            ref[...] = jnp.zeros_like(ref)

    second = second_ref[...]
    normal, inv = norm_stats(second)
    inner = (normal * gain + shift).astype(BF16)
    before = dot(inner, expand)
    square = before * before
    curve = jnp.tanh(GELU_A * before * (1.0 + GELU_B * square))
    after = (0.5 * before * (1.0 + curve)).astype(BF16)
    slope = 0.5 * (1.0 + curve) + (0.5 * GELU_A) * before * (1.0 - curve * curve) * (
        1.0 + (3.0 * GELU_B) * square
    )
    third = second + dot(after, reducer)
    shaped = third.reshape(HOP_TOKENS, NODES_PER_TILE, width)
    keep = live_rows(
        counts_ref[step // per_cluster], (step % per_cluster) * NODES_PER_TILE, NODES_PER_TILE
    )
    centre = shaped[0]
    row_node = rows_ref[4:5]
    row_hop = rows_ref[5:6]
    base = jnp.sum(centre * row_node, axis=-1, keepdims=True)
    logits = [
        base + jnp.sum(shaped[k] * row_hop, axis=-1, keepdims=True) for k in range(1, HOP_TOKENS)
    ]
    top = functools.reduce(jnp.maximum, logits)
    powers = [jnp.exp(logit - top) for logit in logits]
    scale = 1.0 / functools.reduce(jnp.add, powers)
    shares = [power * scale for power in powers]
    total = centre
    for k in range(1, HOP_TOKENS):
        total = total + shares[k - 1] * shaped[k]
    output_ref[...] = total * keep
    cotangent = cotangent_ref[...] * keep
    grad_shares = [
        jnp.sum(cotangent * shaped[k], axis=-1, keepdims=True) for k in range(1, HOP_TOKENS)
    ]
    mean_share = functools.reduce(jnp.add, [s * g for s, g in zip(shares, grad_shares)])
    grad_logits = [s * (g - mean_share) for s, g in zip(shares, grad_shares)]
    grad_base = functools.reduce(jnp.add, grad_logits)
    parts = [cotangent + grad_base * row_node]
    read_hop = jnp.zeros((NODES_PER_TILE, width), F32)
    for k in range(1, HOP_TOKENS):
        parts.append(shares[k - 1] * cotangent + grad_logits[k - 1] * row_hop)
        read_hop = read_hop + grad_logits[k - 1] * shaped[k]
    rows_grad_ref[4:5] += jnp.sum(grad_base * centre, axis=0, keepdims=True)
    rows_grad_ref[5:6] += jnp.sum(read_hop, axis=0, keepdims=True)
    grad_third = jnp.concatenate(parts, axis=0)
    grad_branch = grad_third.astype(BF16)
    grad_reduce_ref[...] += dot_lead(after, grad_branch)
    grad_before = (slope * dot_last(grad_branch, reducer)).astype(BF16)
    grad_expand_ref[...] += dot_lead(inner, grad_before)
    grad_inner = dot_last(grad_before, expand)
    rows_grad_ref[2:3] += jnp.sum(grad_inner * normal, axis=0, keepdims=True)
    rows_grad_ref[3:4] += jnp.sum(grad_inner, axis=0, keepdims=True)
    grad_normal = grad_inner * gain
    grad_second = grad_third + inv * (
        grad_normal
        - jnp.mean(grad_normal, axis=-1, keepdims=True)
        - normal * jnp.mean(grad_normal * normal, axis=-1, keepdims=True)
    )
    grad_second_ref[...] = grad_second
    grad_merge_ref[...] += dot_lead(mixed_ref[...].reshape(TOKENS, width), grad_second.astype(BF16))

    @pl.when(step == pl.num_programs(0) - 1)
    def _():
        spread = expand_ref.shape[-1]
        wide = grad_expand_ref[...].astype(BF16).reshape(PACK, 2, width // PACK // 2, spread)
        deep = grad_reduce_ref[...].astype(BF16).reshape(PACK, 2, spread // PACK // 2, width)
        square = grad_merge_ref[...].astype(BF16).reshape(PACK, 2, width // PACK // 2, width)
        terms_ref[:, :, 0:16] = wide[..., :width]
        terms_ref[:, :, 16:32] = wide[..., width:]
        terms_ref[:, :, 32:64] = deep
        terms_ref[:, :, 64:80] = square


def attend_back_tile(
    tile, triple_ref, normed_ref, grad_second_ref, merge, grad_mixed_ref, grad_triple_ref, grad_attend_ref
):
    width = normed_ref.shape[-1]
    grad_mixed = dot_last(grad_second_ref[...].astype(BF16), merge).astype(BF16)
    grad_mixed_ref[...] = grad_mixed.reshape(grad_mixed_ref.shape)
    first_half = head_masks()
    keep = same_node()
    span = GROUP * HOP_TOKENS
    out_ref = grad_triple_ref.at[tile]

    def group_step(group, carry):
        for first in range(0, width, 2 * HEAD):
            queries = read_block(triple_ref, group, first)
            keys = pair_stack(read_block(triple_ref, group, width + first), first_half)
            values = pair_stack(read_block(triple_ref, group, 2 * width + first), first_half)
            out_grad = read_block(grad_mixed_ref, group, first)
            probs = pair_probs(queries, keys, keep)
            grad_probs = dot_last(out_grad, values)
            grad_halves = []
            for half in range(2):
                part = grad_probs[:, half * span : (half + 1) * span]
                weighted = probs[half] * part
                grad_halves.append(
                    (weighted - probs[half] * jnp.sum(weighted, axis=-1, keepdims=True)).astype(
                        BF16
                    )
                )
            grad_scores = jnp.concatenate(grad_halves, axis=1)
            grad_query = dot(grad_scores, keys) * HEAD ** (-0.5)
            grad_key = dot_lead(
                jnp.concatenate(grad_halves, axis=0), pair_stack(queries, first_half)
            ) * HEAD ** (-0.5)
            grad_value = dot_lead(
                jnp.concatenate([half.astype(BF16) for half in probs], axis=0),
                pair_stack(out_grad, first_half),
            )
            write_block(out_ref, group, first, grad_query.astype(BF16))
            write_block(out_ref, group, width + first, grad_key.astype(BF16))
            write_block(out_ref, group, 2 * width + first, grad_value.astype(BF16))
        return carry

    lax.fori_loop(0, NODES_PER_TILE // GROUP, group_step, 0)
    grad_triple = out_ref[...].reshape(TOKENS, 3 * width)
    grad_attend_ref[...] += dot_lead(normed_ref[...], grad_triple)


def embed_back_tile(
    tile,
    hidden_ref,
    stacked_ref,
    grad_second_ref,
    grad_triple_ref,
    attend,
    embed,
    gain,
    rows_keep,
    grad_embed_ref,
    grad_stacked_ref,
):
    grad_triple = grad_triple_ref[tile].reshape(TOKENS, grad_triple_ref.shape[-1])
    grad_normed = dot_last(grad_triple, attend)
    normal, inv = norm_stats(hidden_ref[...])
    rows_keep[0:1] += jnp.sum(grad_normed * normal, axis=0, keepdims=True)
    rows_keep[1:2] += jnp.sum(grad_normed, axis=0, keepdims=True)
    grad_normal = grad_normed * gain
    grad_hidden = grad_second_ref[...] + inv * (
        grad_normal
        - jnp.mean(grad_normal, axis=-1, keepdims=True)
        - normal * jnp.mean(grad_normal * normal, axis=-1, keepdims=True)
    )
    grad_hidden = grad_hidden.astype(BF16)
    stacked = stacked_ref[...].reshape(TOKENS, stacked_ref.shape[-1])
    grad_embed_ref[...] += dot_lead(stacked, grad_hidden)
    grad_stacked_ref[tile] = dot_last(grad_hidden, embed).reshape(grad_stacked_ref.shape[1:])


def hop_back(counts_ref, adjacency_ref, grad_stacked_ref, grad_features_ref, between):
    clusters, slots = adjacency_ref.shape[:2]
    per_cluster = slots // NODES_PER_TILE
    links = []
    states = []

    def hop_grad(cluster, index):
        return jnp.concatenate(
            [grad_stacked_ref[cluster * per_cluster + p, index] for p in range(per_cluster)],
            axis=0,
        )

    for cluster in range(clusters):
        links.append(link_of(adjacency_ref[cluster], counts_ref[cluster]))
        states.append(hop_grad(cluster, HOPS))
    for index in range(HOPS - 1, -1, -1):
        for cluster in range(clusters):
            states[cluster] = hop_grad(cluster, index) + hop(*links[cluster], states[cluster])
        if index in between:
            between[index]()
    for cluster in range(clusters):
        grad_features_ref[cluster * slots : (cluster + 1) * slots] = states[cluster] * live_rows(
            counts_ref[cluster], 0, slots
        )


def backward_kernel(
    lines,
    counts_ref,
    adjacency_ref,
    triple_ref,
    normed_ref,
    grad_second_ref,
    hidden_ref,
    stacked_ref,
    embed_ref,
    rows_ref,
    attend_ref,
    merge_ref,
    terms_ref,
    rows_grad_ref,
    grad_features_ref,
    middle_share_ref,
    attend_share_ref,
    tail_share_ref,
    grad_mixed_ref,
    grad_triple_ref,
    grad_stacked_ref,
    grad_attend_ref,
    grad_embed_ref,
    rows_keep,
    middle_got,
    middle_chip,
    middle_plane,
    middle_line_out,
    middle_line,
    middle_result,
    attend_terms,
    attend_got,
    attend_chip,
    attend_plane,
    attend_line_out,
    attend_line,
    attend_result,
    tail_own,
    tail_plane,
    tail_line_out,
    tail_line,
    tail_mine,
    tail_other,
    middle_sems,
    attend_sems,
    tail_sems,
):
    step = pl.program_id(0)
    tiles = grad_triple_ref.shape[0]
    width = hidden_ref.shape[-1]
    place = Place(lines)
    middle = Scatter(
        place,
        terms_ref,
        middle_got,
        middle_chip,
        middle_plane,
        middle_line_out,
        middle_line,
        middle_result,
        middle_sems,
    )
    attend = Scatter(
        place,
        attend_terms,
        attend_got,
        attend_chip,
        attend_plane,
        attend_line_out,
        attend_line,
        attend_result,
        attend_sems,
    )
    tail = TailScatter(
        place, tail_own, tail_plane, tail_line_out, tail_line, tail_mine, tail_other, tail_sems
    )

    @pl.when(step == 0)
    def _():
        place.greet()
        rows_keep[...] = rows_grad_ref[...]
        grad_attend_ref[...] = jnp.zeros_like(grad_attend_ref)
        grad_embed_ref[...] = jnp.zeros_like(grad_embed_ref)

    @pl.when(step < tiles)
    def _():
        attend_back_tile(
            step,
            triple_ref,
            normed_ref,
            grad_second_ref,
            merge_ref[...].reshape(width, width),
            grad_mixed_ref,
            grad_triple_ref,
            grad_attend_ref,
        )

    @pl.when(step >= tiles)
    def _():
        embed_back_tile(
            step - tiles,
            hidden_ref,
            stacked_ref,
            grad_second_ref,
            grad_triple_ref,
            attend_ref[...].reshape(width, 3 * width),
            embed_ref[...],
            rows_ref[0:1],
            rows_keep,
            grad_embed_ref,
            grad_stacked_ref,
        )

    @pl.when(step == 0)
    def _():
        place.greeted()
        middle.begin()

    @pl.when(step == 1)
    def _():
        middle.to_plane()

    @pl.when(step == 3)
    def _():
        middle.to_line()

    @pl.when(step == 4)
    def _():
        middle.to_sibling()

    @pl.when(step == tiles - 1)
    def _():
        middle.end()
        attend_terms[...] = grad_attend_ref[...].astype(BF16).reshape(attend_terms.shape)
        attend.begin()

    @pl.when(step == tiles)
    def _():
        attend.to_plane()

    @pl.when(step == tiles + 2)
    def _():
        attend.to_line()

    @pl.when(step == tiles + 4)
    def _():
        attend.to_sibling()

    @pl.when(step == 2 * tiles - 1)
    def _():
        attend.end()
        own = grad_embed_ref[...].reshape(lines, PLANE, 8, width)
        for spot in range(PLANE):
            tail_own[spot, 0:lines] = own[:, spot]
            tail_own[spot, lines] = rows_keep[...]
        tail.begin()
        hop_back(
            counts_ref,
            adjacency_ref,
            grad_stacked_ref,
            grad_features_ref,
            {4: tail.to_line, 1: tail.to_sibling},
        )
        middle_share_ref[...] = middle_result[...]
        attend_share_ref[...] = attend_result[...]
        tail_share_ref[...] = tail.end()


def backward_alone_kernel(
    counts_ref,
    adjacency_ref,
    triple_ref,
    normed_ref,
    grad_second_ref,
    hidden_ref,
    stacked_ref,
    embed_ref,
    rows_ref,
    attend_ref,
    merge_ref,
    rows_grad_ref,
    grad_features_ref,
    grad_attend_ref,
    grad_embed_ref,
    rows_keep,
    grad_mixed_ref,
    grad_triple_ref,
    grad_stacked_ref,
):
    step = pl.program_id(0)
    tiles = grad_triple_ref.shape[0]
    width = hidden_ref.shape[-1]

    @pl.when(step == 0)
    def _():
        rows_keep[...] = rows_grad_ref[...]
        grad_attend_ref[...] = jnp.zeros_like(grad_attend_ref)
        grad_embed_ref[...] = jnp.zeros_like(grad_embed_ref)

    @pl.when(step < tiles)
    def _():
        attend_back_tile(
            step,
            triple_ref,
            normed_ref,
            grad_second_ref,
            merge_ref[...].reshape(width, width),
            grad_mixed_ref,
            grad_triple_ref,
            grad_attend_ref,
        )

    @pl.when(step >= tiles)
    def _():
        embed_back_tile(
            step - tiles,
            hidden_ref,
            stacked_ref,
            grad_second_ref,
            grad_triple_ref,
            attend_ref[...].reshape(width, 3 * width),
            embed_ref[...],
            rows_ref[0:1],
            rows_keep,
            grad_embed_ref,
            grad_stacked_ref,
        )

    @pl.when(step == 2 * tiles - 1)
    def _():
        hop_back(counts_ref, adjacency_ref, grad_stacked_ref, grad_features_ref, {})


def unpack_kernel(
    middle_ref,
    attend_ref,
    tail_ref,
    features_ref,
    grad_features_ref,
    grad_embed_ref,
    grad_gain_one,
    grad_shift_one,
    grad_attend,
    grad_merge,
    grad_gain_two,
    grad_shift_two,
    grad_expand,
    grad_reduce,
    grad_readout,
):
    owner = lax.axis_index("fsdp")
    width = middle_ref.shape[-1]
    grad_features_ref[...] = features_ref[...]
    for half in range(2):
        grad_attend[half * 16 : half * 16 + 16] = attend_ref[half]
        grad_expand[half * 16 : half * 16 + 16, 0:width] = middle_ref[half, 0:16]
        grad_expand[half * 16 : half * 16 + 16, width : 2 * width] = middle_ref[half, 16:32]
        grad_reduce[half * 32 : half * 32 + 32] = middle_ref[half, 32:64]
        grad_merge[half * 16 : half * 16 + 16] = middle_ref[half, 64:80]
    grad_embed_ref[...] = tail_ref[0]
    rows = tail_ref[1]
    length = grad_gain_one.shape[0]
    turned = pltpu.roll(rows, lax.rem(width - owner * length, width), 1)
    for index, ref in enumerate((grad_gain_one, grad_shift_one, grad_gain_two, grad_shift_two)):
        ref[...] = turned[index : index + 1, 0:length].reshape(length)
    length = grad_readout.shape[0]
    first = owner * length
    turned = pltpu.roll(rows, lax.rem(2 * width - first, width), 1)
    row = jnp.where(first < width, turned[4:5, 0:length], turned[5:6, 0:length])
    grad_readout[...] = row.reshape(length)


def whole(shape):
    return pl.BlockSpec(shape, lambda t: (0,) * len(shape), pipeline_mode=pl.Buffered(1))


def kept(shape):
    return pl.BlockSpec(shape, lambda t: (0,) * len(shape))


def tiled(*shape, at=lambda t: t):
    return pl.BlockSpec((None,) + shape, lambda t: (at(t),) + (0,) * len(shape))


def rows_of(*shape, at=lambda t: t):
    return pl.BlockSpec(shape, lambda t: (at(t),) + (0,) * (len(shape) - 1))


def sds(shape, dtype):
    return jax.ShapeDtypeStruct(shape, dtype)


SMEM_SPEC = pl.BlockSpec(memory_space=pltpu.SMEM)


VMEM_SPEC = pl.BlockSpec(memory_space=pltpu.VMEM)
ANY_SPEC = pl.BlockSpec(memory_space=pl.ANY)


def params(collective=None):
    more = {} if collective is None else {"collective_id": collective, "has_side_effects": True}
    return pltpu.CompilerParams(
        vmem_limit_bytes=56 * MIB, dimension_semantics=("arbitrary",), **more
    )


def forward_outs(tiles, feat, width):
    hops, per = HOP_TOKENS, NODES_PER_TILE
    early = lambda t: jnp.minimum(t, tiles - 1)
    late = lambda t: jnp.maximum(t - tiles, 0)
    out_specs = [
        kept((tiles, hops, per, feat)),
        tiled(TOKENS, width, at=early),
        tiled(TOKENS, width, at=early),
        rows_of(hops, per, 3 * width, at=late),
        rows_of(hops, per, width, at=late),
        tiled(TOKENS, width, at=late),
    ]
    out_shape = [
        sds((tiles, hops, per, feat), BF16),
        sds((tiles, TOKENS, width), F32),
        sds((tiles, TOKENS, width), BF16),
        sds((tiles * hops, per, 3 * width), BF16),
        sds((tiles * hops, per, width), BF16),
        sds((tiles, TOKENS, width), F32),
    ]
    keep = [pltpu.VMEM((tiles, TOKENS, width), F32), pltpu.VMEM((tiles, TOKENS, width), BF16)]
    return out_specs, out_shape, keep


def forward_part(
    lines, counts, adjacency, features, embed, vectors, attend, merge, expand, reducer
):
    nodes, feat = features.shape
    owners = lines * PLANE
    width = merge.shape[1]
    tiles = nodes // NODES_PER_TILE
    out_specs, out_shape, keep = forward_outs(tiles, feat, width)
    half = lambda shard: (owners, 2, shard.shape[0] // 2, shard.shape[1])
    copies = lines + PLANE - 2 + (lines - 1) * (PLANE - 1)
    return pl.pallas_call(
        functools.partial(forward_kernel, lines),
        grid=(2 * tiles,),
        in_specs=[SMEM_SPEC, whole(adjacency.shape), whole(features.shape)]
        + [VMEM_SPEC] * 6
        + [whole(attend.shape), whole(merge.shape), ANY_SPEC, ANY_SPEC],
        out_specs=out_specs + [kept((8, width)), kept((feat, width))] + [ANY_SPEC] * 4,
        out_shape=out_shape
        + [sds((8, width), F32), sds((feat, width), BF16)]
        + [sds(half(shard), BF16) for shard in (attend, merge, expand, reducer)],
        scratch_shapes=[
            pltpu.VMEM((8, 128), F32),
            pltpu.VMEM((owners, 16, width // 2 + 128), BF16),
            pltpu.VMEM(half(attend), BF16),
            pltpu.VMEM(half(merge), BF16),
        ]
        + keep
        + [
            pltpu.SemaphoreType.DMA((5, copies)),
            pltpu.SemaphoreType.DMA((5, owners)),
            pltpu.SemaphoreType.DMA((5, 2)),
            pltpu.SemaphoreType.DMA((4,)),
        ],
        compiler_params=params(0),
        name="hops_attention",
    )(counts, adjacency, features, embed, *vectors, attend, merge, expand, reducer)


def forward_alone_part(counts, adjacency, features, rows, embed, attend, merge):
    nodes, feat = features.shape
    width = merge.shape[-1]
    tiles = nodes // NODES_PER_TILE
    out_specs, out_shape, keep = forward_outs(tiles, feat, width)
    return pl.pallas_call(
        forward_alone_kernel,
        grid=(2 * tiles,),
        in_specs=[SMEM_SPEC]
        + [whole(a.shape) for a in (adjacency, features, rows, embed, attend, merge)],
        out_specs=out_specs,
        out_shape=out_shape,
        scratch_shapes=keep,
        compiler_params=params(),
        name="hops_attention_alone",
    )(counts, adjacency, features, rows, embed, attend, merge)


def middle_part(counts, second, mixed, cotangent, rows, expand, reducer):
    tiles, _, width = second.shape
    hops, per = HOP_TOKENS, NODES_PER_TILE
    spread = expand.shape[-1]
    terms = (PACK, 2, 80, width)
    return pl.pallas_call(
        middle_kernel,
        grid=(tiles,),
        in_specs=[
            SMEM_SPEC,
            tiled(TOKENS, width),
            rows_of(hops, per, width),
            rows_of(per, width),
            whole(rows.shape),
            whole(expand.shape),
            whole(reducer.shape),
        ],
        out_specs=[
            rows_of(per, width),
            tiled(TOKENS, width),
            kept(terms),
            kept(rows.shape),
        ],
        out_shape=[
            sds(cotangent.shape, F32),
            sds(second.shape, F32),
            sds(terms, BF16),
            sds(rows.shape, F32),
        ],
        scratch_shapes=[
            pltpu.VMEM((width, width), F32),
            pltpu.VMEM((width, spread), F32),
            pltpu.VMEM((spread, width), F32),
        ],
        compiler_params=params(),
        name="feed_forward",
    )(counts, second, mixed, cotangent, rows, expand, reducer)


def backward_ins(tiles, feat, width, arrays):
    hops, per = HOP_TOKENS, NODES_PER_TILE
    early = lambda t: jnp.minimum(t, tiles - 1)
    late = lambda t: jnp.maximum(t - tiles, 0)
    both = lambda t: lax.rem(t, tiles)
    return [
        SMEM_SPEC,
        whole(arrays[1].shape),
        rows_of(hops, per, 3 * width, at=early),
        tiled(TOKENS, width, at=early),
        tiled(TOKENS, width, at=both),
        tiled(TOKENS, width, at=late),
        tiled(hops, per, feat, at=late),
    ] + [whole(a.shape) for a in arrays[7:]]


def backward_part(lines, *arrays):
    tiles, _, width = arrays[3].shape
    hops, per, feat = arrays[6].shape[1:]
    owners = lines * PLANE
    rest = (80, width)
    wide = (width // owners // 2, 3 * width)

    def buffers(shape):
        return [
            pltpu.VMEM((owners,) + shape, BF16),
            pltpu.VMEM((lines, PLANE) + shape, BF16),
            pltpu.VMEM((PLANE - 1, lines) + shape, BF16),
            pltpu.VMEM((lines,) + shape, BF16),
            pltpu.VMEM((lines - 1,) + shape, BF16),
            pltpu.VMEM((2,) + shape, F32),
        ]

    sems = pltpu.SemaphoreType.DMA((2, PLANE + lines))
    outs = [(tiles * per, feat), (2,) + rest, (2,) + wide, (2, 8, width)]
    return pl.pallas_call(
        functools.partial(backward_kernel, lines),
        grid=(2 * tiles,),
        in_specs=backward_ins(tiles, feat, width, arrays),
        out_specs=[kept(shape) for shape in outs],
        out_shape=[sds(shape, F32) for shape in outs],
        scratch_shapes=[
            pltpu.VMEM((hops, per, width), BF16),
            pltpu.VMEM((tiles, hops, per, 3 * width), BF16),
            pltpu.VMEM((tiles, hops, per, feat), F32),
            pltpu.VMEM((width, 3 * width), F32),
            pltpu.VMEM((feat, width), F32),
            pltpu.VMEM((8, width), F32),
        ]
        + buffers(rest)
        + [pltpu.VMEM((owners, 2) + wide, BF16)]
        + buffers(wide)
        + [
            pltpu.VMEM((PLANE, lines + 1, 8, width), F32),
            pltpu.VMEM((PLANE - 1, lines + 1, 8, width), F32),
            pltpu.VMEM((lines, 2, 8, width), F32),
            pltpu.VMEM((lines - 1, 2, 8, width), F32),
            pltpu.VMEM((2, 8, width), F32),
            pltpu.VMEM((2, 8, width), F32),
        ]
        + [sems] * 3,
        compiler_params=params(1),
        name="attention_backward",
    )(*arrays)


def backward_alone_part(*arrays):
    tiles, _, width = arrays[3].shape
    hops, per, feat = arrays[6].shape[1:]
    outs = [(tiles * per, feat), (width, 3 * width), (feat, width), (8, width)]
    return pl.pallas_call(
        backward_alone_kernel,
        grid=(2 * tiles,),
        in_specs=backward_ins(tiles, feat, width, arrays),
        out_specs=[kept(shape) for shape in outs],
        out_shape=[sds(shape, F32) for shape in outs],
        scratch_shapes=[
            pltpu.VMEM((hops, per, width), BF16),
            pltpu.VMEM((tiles, hops, per, 3 * width), BF16),
            pltpu.VMEM((tiles, hops, per, feat), F32),
        ],
        compiler_params=params(),
        name="attention_backward_alone",
    )(*arrays)


def unpack_part(middle, attend, tail, features, shapes):
    return pl.pallas_call(
        unpack_kernel,
        in_specs=[VMEM_SPEC] * 4,
        out_specs=[VMEM_SPEC] * 11,
        out_shape=[sds(features.shape, F32)] + [sds(shape, F32) for shape in shapes],
        compiler_params=pltpu.CompilerParams(vmem_limit_bytes=24 * MIB),
        name="unpack_shares",
    )(middle, attend, tail, features)


def gather(block):
    return lax.all_gather(block, "fsdp", axis=0, tiled=True)


def share(term):
    part = lax.psum_scatter(term.astype(BF16), "fsdp", scatter_dimension=0, tiled=True)
    return lax.psum(part.astype(F32), "grp")


def body(
    features,
    adjacency,
    counts,
    input_weight,
    first_gain,
    first_shift,
    attend_weight,
    merge_weight,
    second_gain,
    second_shift,
    expand_weight,
    reduce_weight,
    readout_weight,
    cotangent,
):
    vectors = (first_gain, first_shift, second_gain, second_shift, readout_weight)
    owners = lax.axis_size("fsdp")
    if owners % PLANE == 0 and input_weight.shape[0] == 8 and attend_weight.shape[0] == 32:
        lines = owners // PLANE
        (
            stacked,
            hidden,
            normed,
            triple,
            mixed,
            second,
            rows,
            embed,
            attend,
            merge,
            expand,
            reducer,
        ) = forward_part(
            lines,
            counts,
            adjacency,
            features,
            input_weight,
            vectors,
            attend_weight,
            merge_weight,
            expand_weight,
            reduce_weight,
        )
        output, grad_second, terms, rows_grad = middle_part(
            counts, second, mixed, cotangent, rows, expand, reducer
        )
        grad_features, *shares = backward_part(
            lines,
            counts,
            adjacency,
            triple,
            normed,
            grad_second,
            hidden,
            stacked,
            embed,
            rows,
            attend,
            merge,
            terms,
            rows_grad,
        )
        shapes = [
            weight.shape
            for weight in (
                input_weight,
                first_gain,
                first_shift,
                attend_weight,
                merge_weight,
                second_gain,
                second_shift,
                expand_weight,
                reduce_weight,
                readout_weight,
            )
        ]
        return (output, *unpack_part(*shares, grad_features, shapes))
    return body_apart(
        features,
        adjacency,
        counts,
        input_weight,
        vectors,
        attend_weight,
        merge_weight,
        expand_weight,
        reduce_weight,
        cotangent,
    )


def body_apart(
    features,
    adjacency,
    counts,
    input_weight,
    vectors,
    attend_weight,
    merge_weight,
    expand_weight,
    reduce_weight,
    cotangent,
):
    lengths = [v.shape[0] for v in vectors]
    places = [sum(lengths[:i]) for i in range(len(lengths) + 1)]
    packed = lax.all_gather(jnp.concatenate(vectors), "fsdp", axis=0, tiled=False)
    width = merge_weight.shape[1]
    full = [
        packed[:, places[i] : places[i + 1]].astype(F32).reshape(-1, width)
        for i in range(len(lengths))
    ]
    rows = jnp.concatenate(full + [jnp.zeros((2, width), F32)], axis=0)
    embed, attend, merge, expand, reducer = map(
        gather, (input_weight, attend_weight, merge_weight, expand_weight, reduce_weight)
    )
    stacked, hidden, normed, triple, mixed, second = forward_alone_part(
        counts, adjacency, features, rows, embed, attend, merge
    )
    output, grad_second, terms, rows_grad = middle_part(
        counts, second, mixed, cotangent, rows, expand, reducer
    )
    grad_features, grad_attend, grad_embed, rows_grad = backward_alone_part(
        counts,
        adjacency,
        triple,
        normed,
        grad_second,
        hidden,
        stacked,
        embed,
        rows,
        attend,
        merge,
        rows_grad,
    )
    spread = expand.shape[1]
    grad_expand = jnp.concatenate([terms[:, :, 0:16], terms[:, :, 16:32]], axis=-1)
    parts = lax.axis_size("fsdp")
    pieces = [rows_grad[i] for i in range(4)] + [rows_grad[4:6]]
    packed_grad = jnp.concatenate([piece.reshape(parts, -1) for piece in pieces], axis=1)
    packed_grad = lax.psum(
        lax.psum_scatter(packed_grad, "fsdp", scatter_dimension=0, tiled=True), "grp"
    ).reshape(-1)
    small = [packed_grad[places[i] : places[i + 1]] for i in range(len(lengths))]
    return (
        output,
        grad_features,
        share(grad_embed),
        small[0],
        small[1],
        share(grad_attend),
        share(terms[:, :, 64:80].reshape(width, width)),
        small[2],
        small[3],
        share(grad_expand.reshape(width, spread)),
        share(terms[:, :, 32:64].reshape(spread, width)),
        small[4],
    )


def solution(mesh):
    nodes = ("grp", "fsdp")
    rows = P("fsdp", None)
    vector = P("fsdp")
    in_specs = (
        P(nodes, None),
        P(nodes, None, None),
        P(nodes),
        rows,
        vector,
        vector,
        rows,
        rows,
        vector,
        vector,
        rows,
        rows,
        vector,
        P(nodes, None),
    )
    out_specs = (
        P(nodes, None),
        P(nodes, None),
        rows,
        vector,
        vector,
        rows,
        rows,
        vector,
        vector,
        rows,
        rows,
        vector,
    )
    return jax.shard_map(body, mesh=mesh, in_specs=in_specs, out_specs=out_specs, check_vma=False)
```

```python
import functools

import jax
import jax.numpy as jnp
from jax import lax
from jax.experimental import pallas as pl
from jax.experimental.pallas import tpu as pltpu
from jax.sharding import PartitionSpec as P

HEADS = 8
HEAD = 64
HOPS = 7
HOP_TOKENS = HOPS + 1
NODES_PER_TILE = 64
TOKENS = NODES_PER_TILE * HOP_TOKENS
GROUP = 8
GROUPS = NODES_PER_TILE // GROUP
HOP_PAIRS = HOP_TOKENS // 2
QUAD = 4 * HEAD
MIB = 1 << 20
F32 = jnp.float32
BF16 = jnp.bfloat16
GELU_A = 0.7978845608028654
GELU_B = 0.044715
PLANE = 4
PACK = 16
MESH = pl.DeviceIdType.MESH


def dot(left, right):
    return jnp.dot(left, right, preferred_element_type=F32)


def dot_lead(left, right):
    return lax.dot_general(left, right, (((0,), (0,)), ((), ())), preferred_element_type=F32)


def dot_last(left, right):
    return lax.dot_general(left, right, (((1,), (1,)), ((), ())), preferred_element_type=F32)


def link_of(adjacency, count):
    slots = adjacency.shape[0]
    rows = lax.broadcasted_iota(jnp.int32, (slots, slots), 0)
    cols = lax.broadcasted_iota(jnp.int32, (slots, slots), 1)
    live = jnp.logical_and(rows < count, cols < count)
    link = jnp.where(live, adjacency, 0) + jnp.where(rows == cols, 1, 0)
    link = link.astype(F32)
    root = lax.rsqrt(jnp.sum(link, axis=-1, keepdims=True))
    return link.astype(BF16), root


def hop(link, root, state):
    width = state.shape[1]
    scaled = state * root
    high = scaled.astype(BF16)
    rest = scaled - high.astype(F32)
    middle = rest.astype(BF16)
    low = (rest - middle.astype(F32)).astype(BF16)
    spread = dot(link, jnp.concatenate([high, middle, low], axis=1))
    return (spread[:, :width] + (spread[:, width : 2 * width] + spread[:, 2 * width :])) * root


def live_rows(count, first, rows):
    index = lax.broadcasted_iota(jnp.int32, (rows, 1), 0) + first
    return jnp.where(index < count, 1.0, 0.0).astype(F32)


def norm_stats(values):
    mean = jnp.mean(values, axis=-1, keepdims=True)
    centred = values - mean
    var = jnp.mean(centred * centred, axis=-1, keepdims=True)
    inv = lax.rsqrt(var + 1e-05)
    return centred * inv, inv


def quad_stack(block):
    head = lax.broadcasted_iota(jnp.int32, block.shape, 1) // HEAD
    return jnp.concatenate(
        [jnp.where(head == h, block, jnp.zeros_like(block)) for h in range(4)], axis=0
    )


def grad_softmax(probs, grad_probs):
    tokens, columns = probs.shape
    weighted = (probs * grad_probs).reshape(HOP_TOKENS, GROUP, columns)
    total = jnp.sum(weighted, axis=0)
    shaped = probs.reshape(HOP_TOKENS, GROUP, columns)
    return (weighted - shaped * total[None]).reshape(tokens, columns).astype(BF16)


def quad_probs(scores):
    tokens, columns = scores.shape
    scores = scores.reshape(HOP_TOKENS, GROUP, columns)
    top = jnp.max(scores, axis=0)
    power = jnp.exp((scores - top[None]) * HEAD ** (-0.5))
    row = lax.broadcasted_iota(jnp.int32, (GROUP, columns), 0)
    col = lax.broadcasted_iota(jnp.int32, (GROUP, columns), 1) % GROUP
    share = jnp.where(row == col, 1.0 / jnp.sum(power, axis=0), 0.0)
    return (power * share[None]).reshape(tokens, columns)


VARIANT = "A"
BATCH_A = 8
BATCH_B = 8


def queries_from(weights, block, stack):
    if VARIANT == "A":
        tokens = block.shape[0]
        out = []
        lane = lax.broadcasted_iota(jnp.int32, (tokens, 2 * HEAD), 1)
        for first in (0, 2 * HEAD):
            both = dot_lead(weights[:, first : first + 2 * HEAD], block[:, first : first + 2 * HEAD])
            out.append(jnp.where(lane < HEAD, both[:tokens], both[tokens:]))
        return jnp.concatenate(out, axis=1)
    turned = []
    for first in (0, 2 * HEAD):
        part = weights[:, first : first + 2 * HEAD].T
        turned += [part[:HEAD], part[HEAD:]]
    return dot(jnp.concatenate(turned, axis=1), stack())


def read_block(ref, group, first):
    return ref[:, group, :, first : first + QUAD].reshape(GROUP * HOP_TOKENS, QUAD)


def write_block(ref, group, first, block):
    ref[:, group, :, first : first + QUAD] = block.reshape(HOP_PAIRS, 2 * GROUP, QUAD)


def hop_rows(values, index):
    shaped = values.reshape(HOP_PAIRS, GROUPS, 2, GROUP, values.shape[-1])
    return shaped[index // 2, :, index % 2].reshape(NODES_PER_TILE, values.shape[-1])


def hop_join(parts):
    width = parts[0].shape[-1]
    blocks = []
    for pair in range(HOP_PAIRS):
        both = [parts[2 * pair + k].reshape(GROUPS, 1, GROUP, width) for k in range(2)]
        blocks.append(jnp.concatenate(both, axis=1))
    return jnp.concatenate(blocks, axis=0).reshape(TOKENS, width)


class Place:
    def __init__(self, lines):
        self.lines = lines
        self.core = lax.axis_index("grp")
        self.owner = lax.axis_index("fsdp")
        self.line = lax.div(self.owner, PLANE)
        self.spot = lax.rem(self.owner, PLANE)

    def line_turn(self, ahead):
        return lax.rem(self.line + ahead + self.lines, self.lines)

    def spot_turn(self, ahead):
        return lax.rem(self.spot + ahead + PLANE, PLANE)

    def line_peer(self, ahead):
        return (self.core, self.line_turn(ahead) * PLANE + self.spot)

    def plane_peer(self, ahead):
        return (self.core, self.line * PLANE + self.spot_turn(ahead))

    def sibling(self):
        return (1 - self.core, self.owner)

    def peers(self):
        return (
            [self.line_peer(d) for d in range(1, self.lines)]
            + [self.plane_peer(e) for e in range(1, PLANE)]
            + [self.sibling()]
        )

    def greet(self):
        barrier = pltpu.get_barrier_semaphore()
        for peer in self.peers():
            pl.semaphore_signal(barrier, inc=1, device_id=peer, device_id_type=MESH)

    def greeted(self):
        pl.semaphore_wait(pltpu.get_barrier_semaphore(), self.lines + PLANE - 1)


def remote(source, target, send, recv, device):
    return pltpu.make_async_remote_copy(
        src_ref=source,
        dst_ref=target,
        send_sem=send,
        recv_sem=recv,
        device_id=device,
        device_id_type=MESH,
    )


class Gather:
    def __init__(self, place, slots, source, send, recv, pair, halves=True):
        self.place, self.slots, self.source = place, slots, source
        self.send, self.recv, self.pair_sems, self.halves = send, recv, pair, halves

    def slot(self, owner):
        return self.slots.at[owner, self.place.core] if self.halves else self.slots.at[owner]

    def own_copies(self):
        place = self.place
        peers = [place.line_peer(d) for d in range(1, place.lines)]
        peers += [place.plane_peer(e) for e in range(1, PLANE)]
        return [
            remote(
                self.source, self.slot(place.owner), self.send.at[i], self.recv.at[place.owner], peer
            )
            for i, peer in enumerate(peers)
        ]

    def onward(self, d):
        place = self.place
        owner = place.line_turn(-d) * PLANE + place.spot
        first = place.lines + PLANE - 2 + (d - 1) * (PLANE - 1)
        return [
            remote(
                self.slot(owner),
                self.slot(owner),
                self.send.at[first + e - 1],
                self.recv.at[owner],
                place.plane_peer(e),
            )
            for e in range(1, PLANE)
        ]

    def start(self):
        for copy in self.own_copies():
            copy.start()

    def forward(self):
        for d in range(1, self.place.lines):
            copies = self.onward(d)
            copies[0].wait_recv()
            for copy in copies:
                copy.start()

    def finish(self):
        place = self.place
        for d in range(place.lines):
            for e in range(1, PLANE):
                owner = place.line_turn(d) * PLANE + place.spot_turn(-e)
                remote(
                    self.slot(owner),
                    self.slot(owner),
                    self.send.at[0],
                    self.recv.at[owner],
                    place.plane_peer(e),
                ).wait_recv()
        for copy in self.own_copies():
            copy.wait_send()
        for d in range(1, place.lines):
            for copy in self.onward(d):
                copy.wait_send()

    def pair(self):
        half = self.slots.at[:, self.place.core]
        return remote(half, half, self.pair_sems.at[0], self.pair_sems.at[1], self.place.sibling())


class Scatter:
    def __init__(self, place, terms, got, chip, plane_got, line_out, line_got, result, sems):
        self.place, self.terms, self.got, self.chip = place, terms, got, chip
        self.plane_got, self.line_out, self.line_got = plane_got, line_out, line_got
        self.result, self.sems = result, sems

    def pair(self):
        place = self.place
        return remote(
            self.terms.at[:, 1 - place.core],
            self.got,
            self.sems.at[0, 0],
            self.sems.at[1, 0],
            place.sibling(),
        )

    def plane(self):
        place = self.place
        return [
            remote(
                self.chip.at[:, place.spot_turn(e)],
                self.plane_got.at[e - 1],
                self.sems.at[0, e],
                self.sems.at[1, e],
                place.plane_peer(e),
            )
            for e in range(1, PLANE)
        ]

    def line(self):
        place = self.place
        return [
            remote(
                self.line_out.at[place.line_turn(d)],
                self.line_got.at[d - 1],
                self.sems.at[0, PLANE + d - 1],
                self.sems.at[1, PLANE + d - 1],
                place.line_peer(d),
            )
            for d in range(1, place.lines)
        ]

    def last(self):
        place = self.place
        half = self.result.at[place.core]
        k = PLANE + place.lines - 1
        return remote(half, half, self.sems.at[0, k], self.sems.at[1, k], place.sibling())

    def begin(self):
        self.pair().start()

    def to_plane(self):
        place = self.place
        self.pair().wait()

        def add(line, carry):
            for spot in range(PLANE):
                owner = line * PLANE + spot
                both = self.terms[owner, place.core].astype(F32) + self.got[owner].astype(F32)
                self.chip[line, spot] = both.astype(BF16)
            return carry

        lax.fori_loop(0, place.lines, add, 0)
        for copy in self.plane():
            copy.start()

    def to_line(self):
        place = self.place
        for copy in self.plane():
            copy.wait()

        def add(line, carry):
            total = self.chip[line, place.spot].astype(F32)
            for e in range(PLANE - 1):
                total = total + self.plane_got[e, line].astype(F32)
            self.line_out[line] = total.astype(BF16)
            return carry

        lax.fori_loop(0, place.lines, add, 0)
        for copy in self.line():
            copy.start()

    def to_sibling(self):
        place = self.place
        for copy in self.line():
            copy.wait()
        total = self.line_out[place.line].astype(F32)
        for d in range(place.lines - 1):
            total = total + self.line_got[d].astype(F32)
        self.result[place.core] = total
        self.last().start()

    def end(self):
        self.last().wait()


class TailScatter:
    def __init__(self, place, own, plane_got, line_out, line_got, mine, other, sems):
        self.place, self.own, self.plane_got, self.line_out = place, own, plane_got, line_out
        self.line_got, self.mine, self.other, self.sems = line_got, mine, other, sems

    def plane(self):
        place = self.place
        return [
            remote(
                self.own.at[place.spot_turn(e)],
                self.plane_got.at[e - 1],
                self.sems.at[0, e],
                self.sems.at[1, e],
                place.plane_peer(e),
            )
            for e in range(1, PLANE)
        ]

    def line(self):
        place = self.place
        return [
            remote(
                self.line_out.at[place.line_turn(d)],
                self.line_got.at[d - 1],
                self.sems.at[0, PLANE + d - 1],
                self.sems.at[1, PLANE + d - 1],
                place.line_peer(d),
            )
            for d in range(1, place.lines)
        ]

    def last(self):
        return remote(
            self.mine, self.other, self.sems.at[0, 0], self.sems.at[1, 0], self.place.sibling()
        )

    def begin(self):
        for copy in self.plane():
            copy.start()

    def to_line(self):
        place = self.place
        for copy in self.plane():
            copy.wait()
        total = self.own[place.spot]
        for e in range(PLANE - 1):
            total = total + self.plane_got[e]
        for line in range(place.lines):
            self.line_out[line, 0] = total[line]
            self.line_out[line, 1] = total[place.lines]
        for copy in self.line():
            copy.start()

    def to_sibling(self):
        place = self.place
        for copy in self.line():
            copy.wait()
        total = self.line_out[place.line]
        for d in range(place.lines - 1):
            total = total + self.line_got[d]
        self.mine[...] = total
        self.last().start()

    def end(self):
        self.last().wait()
        return self.mine[...] + self.other[...]


def hop_states(counts_ref, adjacency_ref, features_ref, stacked_ref):
    clusters, slots = adjacency_ref.shape[:2]
    per_cluster = slots // NODES_PER_TILE
    links = []
    states = []
    for cluster in range(clusters):
        count = counts_ref[cluster]
        links.append(link_of(adjacency_ref[cluster], count))
        states.append(
            features_ref[cluster * slots : (cluster + 1) * slots].astype(F32)
            * live_rows(count, 0, slots)
        )
    earlier = [None] * clusters
    for index in range(HOP_TOKENS):
        for cluster in range(clusters):
            if index > 0:
                states[cluster] = hop(*links[cluster], states[cluster])
            if index % 2 == 0:
                earlier[cluster] = states[cluster]
                continue
            for part in range(per_cluster):
                rows = slice(part * NODES_PER_TILE, (part + 1) * NODES_PER_TILE)
                both = [
                    state[rows].reshape(GROUPS, GROUP, state.shape[-1])
                    for state in (earlier[cluster], states[cluster])
                ]
                stacked_ref[cluster * per_cluster + part, index // 2] = jnp.concatenate(
                    both, axis=1
                ).astype(BF16)


def embed_tile(step, stacked_ref, embed, gain, shift, hidden_keep, normed_keep, hidden_ref, normed_ref):
    stacked = stacked_ref[step].reshape(TOKENS, stacked_ref.shape[-1])
    hidden = dot(stacked, embed)
    hidden_keep[step] = hidden
    hidden_ref[...] = hidden
    normal, _ = norm_stats(hidden)
    normed = (normal * gain + shift).astype(BF16)
    normed_keep[step] = normed
    normed_ref[...] = normed


def attend_tile(tile, hidden_keep, normed_keep, attend, merge_of, triple_ref, mixed_ref, second_ref):
    width = hidden_keep.shape[-1]
    triple_ref[...] = dot(normed_keep[tile], attend).astype(BF16).reshape(triple_ref.shape)

    def group_step(index, carry):
        places = [
            (index * BATCH_A + g, first) for g in range(BATCH_A) for first in range(0, width, QUAD)
        ]
        keys = [read_block(triple_ref, g, width + first) for g, first in places]
        queries = [quad_stack(read_block(triple_ref, g, first)) for g, first in places]
        scores = [dot_last(k, q) for k, q in zip(keys, queries)]
        probs = [quad_probs(score).astype(BF16) for score in scores]
        values = [read_block(triple_ref, g, 2 * width + first) for g, first in places]
        mixed = [queries_from(p, v, lambda v=v: quad_stack(v)) for p, v in zip(probs, values)]
        for (g, first), block in zip(places, mixed):
            write_block(mixed_ref, g, first, block.astype(BF16))
        return carry

    lax.fori_loop(0, GROUPS // BATCH_A, group_step, 0)
    mixed = mixed_ref[...].reshape(TOKENS, width)
    second_ref[...] = hidden_keep[tile] + dot(mixed, merge_of())


def spread_vectors(small, owners, width):
    rows = small.shape[0]
    lane = lax.broadcasted_iota(jnp.int32, (128, width), 0)
    column = lax.broadcasted_iota(jnp.int32, (128, width), 1)
    row = lax.broadcasted_iota(jnp.int32, (rows, width), 0)
    place = lax.broadcasted_iota(jnp.int32, (rows, width), 1)
    piece = width // owners
    pieces = dot(small, jnp.where(lane == column % piece, 1.0, 0.0).astype(BF16))
    out = []
    for vector in range(4):
        mine = jnp.logical_and(row % 8 == vector, lax.div(row, 8) == lax.div(place, piece))
        out.append(jnp.sum(jnp.where(mine, pieces, 0.0), axis=0, keepdims=True))
    pieces = dot(small, jnp.where(lane == column % (2 * piece), 1.0, 0.0).astype(BF16))
    for first in (0, owners // 2):
        owner = lax.div(place, 2 * piece) + first
        mine = jnp.logical_and(row % 8 == 4, lax.div(row, 8) == owner)
        out.append(jnp.sum(jnp.where(mine, pieces, 0.0), axis=0, keepdims=True))
    return jnp.concatenate(out + [jnp.zeros((2, width), F32)], axis=0)


def forward_kernel(
    lines,
    counts_ref,
    adjacency_ref,
    features_ref,
    embed_shard,
    vector_a,
    vector_b,
    vector_c,
    vector_d,
    vector_e,
    attend_shard,
    merge_shard,
    expand_shard,
    reduce_shard,
    stacked_ref,
    hidden_ref,
    normed_ref,
    triple_ref,
    mixed_ref,
    second_ref,
    rows_ref,
    embed_ref,
    attend_out,
    merge_out,
    expand_slots,
    reduce_slots,
    small_keep,
    head_slots,
    attend_slots,
    merge_slots,
    hidden_keep,
    normed_keep,
    send,
    recv,
    pair,
    local,
):
    step = pl.program_id(0)
    tiles = hidden_keep.shape[0]
    owners = head_slots.shape[0]
    width = hidden_keep.shape[-1]
    place = Place(lines)
    core, owner = place.core, place.owner

    def half_of(shard):
        rows = shard.shape[0] // 2
        return shard.at[pl.ds(pl.multiple_of(core * rows, rows), rows)]

    def gather(index, slots, source, halves=True):
        return Gather(
            place, slots, source, send.at[index], recv.at[index], pair.at[index], halves
        )

    head = gather(0, head_slots, head_slots.at[owner], False)
    attend = gather(1, attend_slots, half_of(attend_shard))
    merge = gather(2, merge_slots, half_of(merge_shard))
    expand = gather(3, expand_slots, half_of(expand_shard))
    reducer = gather(4, reduce_slots, half_of(reduce_shard))
    own_copies = [
        pltpu.make_async_copy(half_of(shard), slots.at[owner, core], local.at[index])
        for index, (shard, slots) in enumerate(
            ((expand_shard, expand_slots), (reduce_shard, reduce_slots))
        )
    ]
    out_copies = [
        pltpu.make_async_copy(attend_slots, attend_out, local.at[2]),
        pltpu.make_async_copy(merge_slots, merge_out, local.at[3]),
    ]

    @pl.when(step == 0)
    def _():
        place.greet()
        small_keep[...] = jnp.zeros_like(small_keep)
        for index, vector in enumerate((vector_a, vector_b, vector_c, vector_d, vector_e)):
            length = vector.shape[0]
            small_keep[index : index + 1, 0:length] = vector[...].astype(F32).reshape(1, length)
        mine = embed_shard[...].astype(F32)
        half_width = width // 2
        packed = jnp.concatenate(
            [
                jnp.concatenate([mine[:, :half_width], small_keep[...]], axis=1),
                jnp.concatenate([mine[:, half_width:], jnp.zeros((8, 128), F32)], axis=1),
            ],
            axis=0,
        )
        head_slots[owner] = packed.astype(BF16)
        attend_slots[owner, core] = half_of(attend_shard)[...]
        merge_slots[owner, core] = half_of(merge_shard)[...]
        hop_states(counts_ref, adjacency_ref, features_ref, stacked_ref)
        place.greeted()
        head.start()
        attend.start()
        merge.start()
        for copy in own_copies:
            copy.start()
        head.forward()
        head.finish()
        whole_head = head_slots[...].astype(F32)
        top = whole_head[:, 0:8].reshape(owners * 8, half_width + 128)
        bottom = whole_head[:, 8:16].reshape(owners * 8, half_width + 128)
        embed_ref[:, :half_width] = top[:, :half_width].astype(BF16)
        embed_ref[:, half_width:] = bottom[:, :half_width].astype(BF16)
        rows_ref[...] = spread_vectors(top[:, half_width:].astype(BF16), owners, width)
        attend.forward()
        merge.forward()

    @pl.when(step < tiles)
    def _():
        embed_tile(
            step,
            stacked_ref,
            embed_ref[...],
            rows_ref[0:1],
            rows_ref[1:2],
            hidden_keep,
            normed_keep,
            hidden_ref,
            normed_ref,
        )

    @pl.when(step == tiles - 1)
    def _():
        attend.finish()
        attend.pair().start()
        merge.finish()
        merge.pair().start()
        for copy in own_copies:
            copy.wait()
        expand.start()
        reducer.start()
        attend.pair().wait()
        merge.pair().wait()
        for copy in out_copies:
            copy.start()

    @pl.when(step == tiles + 1)
    def _():
        expand.forward()
        reducer.forward()

    @pl.when(step == 2 * tiles - 2)
    def _():
        expand.finish()
        expand.pair().start()
        reducer.finish()
        reducer.pair().start()

    @pl.when(step >= tiles)
    def _():
        attend_tile(
            step - tiles,
            hidden_keep,
            normed_keep,
            attend_slots[...].reshape(width, 3 * width),
            lambda: merge_slots[...].reshape(width, width),
            triple_ref,
            mixed_ref,
            second_ref,
        )

    @pl.when(step == 2 * tiles - 1)
    def _():
        expand.pair().wait()
        reducer.pair().wait()
        for copy in out_copies:
            copy.wait()


def forward_alone_kernel(
    counts_ref,
    adjacency_ref,
    features_ref,
    rows_ref,
    embed_ref,
    attend_ref,
    merge_ref,
    stacked_ref,
    hidden_ref,
    normed_ref,
    triple_ref,
    mixed_ref,
    second_ref,
    hidden_keep,
    normed_keep,
):
    step = pl.program_id(0)
    tiles = hidden_keep.shape[0]
    width = hidden_keep.shape[-1]

    @pl.when(step == 0)
    def _():
        hop_states(counts_ref, adjacency_ref, features_ref, stacked_ref)

    @pl.when(step < tiles)
    def _():
        embed_tile(
            step,
            stacked_ref,
            embed_ref[...],
            rows_ref[0:1],
            rows_ref[1:2],
            hidden_keep,
            normed_keep,
            hidden_ref,
            normed_ref,
        )

    @pl.when(step >= tiles)
    def _():
        attend_tile(
            step - tiles,
            hidden_keep,
            normed_keep,
            attend_ref[...].reshape(width, 3 * width),
            lambda: merge_ref[...].reshape(width, width),
            triple_ref,
            mixed_ref,
            second_ref,
        )


def middle_kernel(
    counts_ref,
    second_ref,
    mixed_ref,
    cotangent_ref,
    rows_ref,
    expand_ref,
    reduce_ref,
    output_ref,
    grad_second_ref,
    terms_ref,
    rows_grad_ref,
    grad_merge_ref,
    grad_expand_ref,
    grad_reduce_ref,
):
    step = pl.program_id(0)
    width = second_ref.shape[-1]
    per_cluster = 128 // NODES_PER_TILE
    gain, shift = rows_ref[2:3], rows_ref[3:4]
    expand = expand_ref[...].reshape(width, expand_ref.shape[-1])
    reducer = reduce_ref[...].reshape(expand_ref.shape[-1], width)

    @pl.when(step == 0)
    def _():
        for ref in (rows_grad_ref, grad_merge_ref, grad_expand_ref, grad_reduce_ref):
            ref[...] = jnp.zeros_like(ref)

    second = second_ref[...]
    normal, inv = norm_stats(second)
    inner = (normal * gain + shift).astype(BF16)
    before = dot(inner, expand)
    square = before * before
    curve = jnp.tanh(GELU_A * before * (1.0 + GELU_B * square))
    after = (0.5 * before * (1.0 + curve)).astype(BF16)
    slope = 0.5 * (1.0 + curve) + (0.5 * GELU_A) * before * (1.0 - curve * curve) * (
        1.0 + (3.0 * GELU_B) * square
    )
    third = second + dot(after, reducer)
    shaped = [hop_rows(third, k) for k in range(HOP_TOKENS)]
    keep = live_rows(
        counts_ref[step // per_cluster], (step % per_cluster) * NODES_PER_TILE, NODES_PER_TILE
    )
    centre = shaped[0]
    row_node = rows_ref[4:5]
    row_hop = rows_ref[5:6]
    base = jnp.sum(centre * row_node, axis=-1, keepdims=True)
    logits = [
        base + jnp.sum(shaped[k] * row_hop, axis=-1, keepdims=True) for k in range(1, HOP_TOKENS)
    ]
    top = functools.reduce(jnp.maximum, logits)
    powers = [jnp.exp(logit - top) for logit in logits]
    scale = 1.0 / functools.reduce(jnp.add, powers)
    shares = [power * scale for power in powers]
    total = centre
    for k in range(1, HOP_TOKENS):
        total = total + shares[k - 1] * shaped[k]
    output_ref[...] = total * keep
    cotangent = cotangent_ref[...] * keep
    grad_shares = [
        jnp.sum(cotangent * shaped[k], axis=-1, keepdims=True) for k in range(1, HOP_TOKENS)
    ]
    mean_share = functools.reduce(jnp.add, [s * g for s, g in zip(shares, grad_shares)])
    grad_logits = [s * (g - mean_share) for s, g in zip(shares, grad_shares)]
    grad_base = functools.reduce(jnp.add, grad_logits)
    parts = [cotangent + grad_base * row_node]
    read_hop = jnp.zeros((NODES_PER_TILE, width), F32)
    for k in range(1, HOP_TOKENS):
        parts.append(shares[k - 1] * cotangent + grad_logits[k - 1] * row_hop)
        read_hop = read_hop + grad_logits[k - 1] * shaped[k]
    rows_grad_ref[4:5] += jnp.sum(grad_base * centre, axis=0, keepdims=True)
    rows_grad_ref[5:6] += jnp.sum(read_hop, axis=0, keepdims=True)
    grad_third = hop_join(parts)
    grad_branch = grad_third.astype(BF16)
    grad_reduce_ref[...] += dot_lead(after, grad_branch)
    grad_before = (slope * dot_last(grad_branch, reducer)).astype(BF16)
    grad_expand_ref[...] += dot_lead(inner, grad_before)
    grad_inner = dot_last(grad_before, expand)
    rows_grad_ref[2:3] += jnp.sum(grad_inner * normal, axis=0, keepdims=True)
    rows_grad_ref[3:4] += jnp.sum(grad_inner, axis=0, keepdims=True)
    grad_normal = grad_inner * gain
    grad_second = grad_third + inv * (
        grad_normal
        - jnp.mean(grad_normal, axis=-1, keepdims=True)
        - normal * jnp.mean(grad_normal * normal, axis=-1, keepdims=True)
    )
    grad_second_ref[...] = grad_second
    grad_merge_ref[...] += dot_lead(mixed_ref[...].reshape(TOKENS, width), grad_second.astype(BF16))

    @pl.when(step == pl.num_programs(0) - 1)
    def _():
        spread = expand_ref.shape[-1]
        wide = grad_expand_ref[...].astype(BF16).reshape(PACK, 2, width // PACK // 2, spread)
        deep = grad_reduce_ref[...].astype(BF16).reshape(PACK, 2, spread // PACK // 2, width)
        square = grad_merge_ref[...].astype(BF16).reshape(PACK, 2, width // PACK // 2, width)
        terms_ref[:, :, 0:16] = wide[..., :width]
        terms_ref[:, :, 16:32] = wide[..., width:]
        terms_ref[:, :, 32:64] = deep
        terms_ref[:, :, 64:80] = square


def attend_back_tile(
    tile, triple_ref, normed_ref, grad_second_ref, merge, grad_mixed_ref, grad_triple_ref, grad_attend_ref
):
    width = normed_ref.shape[-1]
    grad_mixed = dot_last(grad_second_ref[...].astype(BF16), merge).astype(BF16)
    grad_mixed_ref[...] = grad_mixed.reshape(grad_mixed_ref.shape)
    out_ref = grad_triple_ref.at[tile]

    def group_step(index, carry):
        places = [
            (index * BATCH_B + g, first) for g in range(BATCH_B) for first in range(0, width, QUAD)
        ]
        scale = HEAD ** (-0.5)
        keys = [read_block(triple_ref, g, width + first) for g, first in places]
        queries = [quad_stack(read_block(triple_ref, g, first)) for g, first in places]
        scores = [dot_last(k, q) for k, q in zip(keys, queries)]
        values = [read_block(triple_ref, g, 2 * width + first) for g, first in places]
        out_grads = [quad_stack(read_block(grad_mixed_ref, g, first)) for g, first in places]
        grad_probs = [dot_last(v, o) for v, o in zip(values, out_grads)]
        probs = [quad_probs(score) for score in scores]
        grad_scores = [grad_softmax(p, g) for p, g in zip(probs, grad_probs)]
        grad_values = [dot(p.astype(BF16), o) for p, o in zip(probs, out_grads)]
        grad_keys = [dot(s, q) for s, q in zip(grad_scores, queries)]
        grad_queries = [
            queries_from(s, k, lambda k=k: quad_stack(k)) for s, k in zip(grad_scores, keys)
        ]
        for (g, first), a, b, c in zip(places, grad_queries, grad_keys, grad_values):
            write_block(out_ref, g, first, (a * scale).astype(BF16))
            write_block(out_ref, g, width + first, (b * scale).astype(BF16))
            write_block(out_ref, g, 2 * width + first, c.astype(BF16))
        return carry

    lax.fori_loop(0, GROUPS // BATCH_B, group_step, 0)
    grad_triple = out_ref[...].reshape(TOKENS, 3 * width)
    grad_attend_ref[...] += dot_lead(normed_ref[...], grad_triple)


def embed_back_tile(
    tile,
    hidden_ref,
    stacked_ref,
    grad_second_ref,
    grad_triple_ref,
    attend,
    embed,
    gain,
    rows_keep,
    grad_embed_ref,
    grad_stacked_ref,
):
    grad_triple = grad_triple_ref[tile].reshape(TOKENS, grad_triple_ref.shape[-1])
    grad_normed = dot_last(grad_triple, attend)
    normal, inv = norm_stats(hidden_ref[...])
    rows_keep[0:1] += jnp.sum(grad_normed * normal, axis=0, keepdims=True)
    rows_keep[1:2] += jnp.sum(grad_normed, axis=0, keepdims=True)
    grad_normal = grad_normed * gain
    grad_hidden = grad_second_ref[...] + inv * (
        grad_normal
        - jnp.mean(grad_normal, axis=-1, keepdims=True)
        - normal * jnp.mean(grad_normal * normal, axis=-1, keepdims=True)
    )
    grad_hidden = grad_hidden.astype(BF16)
    stacked = stacked_ref[...].reshape(TOKENS, stacked_ref.shape[-1])
    grad_embed_ref[...] += dot_lead(stacked, grad_hidden)
    grad_stacked_ref[tile] = dot_last(grad_hidden, embed).reshape(grad_stacked_ref.shape[1:])


def hop_back(counts_ref, adjacency_ref, grad_stacked_ref, grad_features_ref, between):
    clusters, slots = adjacency_ref.shape[:2]
    per_cluster = slots // NODES_PER_TILE
    links = []
    states = []

    def hop_grad(cluster, index):
        return jnp.concatenate(
            [
                grad_stacked_ref[cluster * per_cluster + p, index // 2, :, index % 2].reshape(
                    NODES_PER_TILE, grad_stacked_ref.shape[-1]
                )
                for p in range(per_cluster)
            ],
            axis=0,
        )

    for cluster in range(clusters):
        links.append(link_of(adjacency_ref[cluster], counts_ref[cluster]))
        states.append(hop_grad(cluster, HOPS))
    for index in range(HOPS - 1, -1, -1):
        for cluster in range(clusters):
            states[cluster] = hop_grad(cluster, index) + hop(*links[cluster], states[cluster])
        if index in between:
            between[index]()
    for cluster in range(clusters):
        grad_features_ref[cluster * slots : (cluster + 1) * slots] = states[cluster] * live_rows(
            counts_ref[cluster], 0, slots
        )


def backward_kernel(
    lines,
    counts_ref,
    adjacency_ref,
    triple_ref,
    normed_ref,
    grad_second_ref,
    hidden_ref,
    stacked_ref,
    embed_ref,
    rows_ref,
    attend_ref,
    merge_ref,
    terms_ref,
    rows_grad_ref,
    grad_features_ref,
    middle_share_ref,
    attend_share_ref,
    tail_share_ref,
    grad_mixed_ref,
    grad_triple_ref,
    grad_stacked_ref,
    grad_attend_ref,
    grad_embed_ref,
    rows_keep,
    middle_got,
    middle_chip,
    middle_plane,
    middle_line_out,
    middle_line,
    middle_result,
    attend_terms,
    attend_got,
    attend_chip,
    attend_plane,
    attend_line_out,
    attend_line,
    attend_result,
    tail_own,
    tail_plane,
    tail_line_out,
    tail_line,
    tail_mine,
    tail_other,
    middle_sems,
    attend_sems,
    tail_sems,
):
    step = pl.program_id(0)
    tiles = grad_triple_ref.shape[0]
    width = hidden_ref.shape[-1]
    place = Place(lines)
    middle = Scatter(
        place,
        terms_ref,
        middle_got,
        middle_chip,
        middle_plane,
        middle_line_out,
        middle_line,
        middle_result,
        middle_sems,
    )
    attend = Scatter(
        place,
        attend_terms,
        attend_got,
        attend_chip,
        attend_plane,
        attend_line_out,
        attend_line,
        attend_result,
        attend_sems,
    )
    tail = TailScatter(
        place, tail_own, tail_plane, tail_line_out, tail_line, tail_mine, tail_other, tail_sems
    )

    @pl.when(step == 0)
    def _():
        place.greet()
        rows_keep[...] = rows_grad_ref[...]
        grad_attend_ref[...] = jnp.zeros_like(grad_attend_ref)
        grad_embed_ref[...] = jnp.zeros_like(grad_embed_ref)

    @pl.when(step < tiles)
    def _():
        attend_back_tile(
            step,
            triple_ref,
            normed_ref,
            grad_second_ref,
            merge_ref[...].reshape(width, width),
            grad_mixed_ref,
            grad_triple_ref,
            grad_attend_ref,
        )

    @pl.when(step >= tiles)
    def _():
        embed_back_tile(
            step - tiles,
            hidden_ref,
            stacked_ref,
            grad_second_ref,
            grad_triple_ref,
            attend_ref[...].reshape(width, 3 * width),
            embed_ref[...],
            rows_ref[0:1],
            rows_keep,
            grad_embed_ref,
            grad_stacked_ref,
        )

    @pl.when(step == 0)
    def _():
        place.greeted()
        middle.begin()

    @pl.when(step == 1)
    def _():
        middle.to_plane()

    @pl.when(step == 3)
    def _():
        middle.to_line()

    @pl.when(step == 4)
    def _():
        middle.to_sibling()

    @pl.when(step == tiles - 1)
    def _():
        middle.end()
        attend_terms[...] = grad_attend_ref[...].astype(BF16).reshape(attend_terms.shape)
        attend.begin()

    @pl.when(step == tiles)
    def _():
        attend.to_plane()

    @pl.when(step == tiles + 2)
    def _():
        attend.to_line()

    @pl.when(step == tiles + 4)
    def _():
        attend.to_sibling()

    @pl.when(step == 2 * tiles - 1)
    def _():
        attend.end()
        own = grad_embed_ref[...].reshape(lines, PLANE, 8, width)
        for spot in range(PLANE):
            tail_own[spot, 0:lines] = own[:, spot]
            tail_own[spot, lines] = rows_keep[...]
        tail.begin()
        hop_back(
            counts_ref,
            adjacency_ref,
            grad_stacked_ref,
            grad_features_ref,
            {4: tail.to_line, 1: tail.to_sibling},
        )
        middle_share_ref[...] = middle_result[...]
        attend_share_ref[...] = attend_result[...]
        tail_share_ref[...] = tail.end()


def backward_alone_kernel(
    counts_ref,
    adjacency_ref,
    triple_ref,
    normed_ref,
    grad_second_ref,
    hidden_ref,
    stacked_ref,
    embed_ref,
    rows_ref,
    attend_ref,
    merge_ref,
    rows_grad_ref,
    grad_features_ref,
    grad_attend_ref,
    grad_embed_ref,
    rows_keep,
    grad_mixed_ref,
    grad_triple_ref,
    grad_stacked_ref,
):
    step = pl.program_id(0)
    tiles = grad_triple_ref.shape[0]
    width = hidden_ref.shape[-1]

    @pl.when(step == 0)
    def _():
        rows_keep[...] = rows_grad_ref[...]
        grad_attend_ref[...] = jnp.zeros_like(grad_attend_ref)
        grad_embed_ref[...] = jnp.zeros_like(grad_embed_ref)

    @pl.when(step < tiles)
    def _():
        attend_back_tile(
            step,
            triple_ref,
            normed_ref,
            grad_second_ref,
            merge_ref[...].reshape(width, width),
            grad_mixed_ref,
            grad_triple_ref,
            grad_attend_ref,
        )

    @pl.when(step >= tiles)
    def _():
        embed_back_tile(
            step - tiles,
            hidden_ref,
            stacked_ref,
            grad_second_ref,
            grad_triple_ref,
            attend_ref[...].reshape(width, 3 * width),
            embed_ref[...],
            rows_ref[0:1],
            rows_keep,
            grad_embed_ref,
            grad_stacked_ref,
        )

    @pl.when(step == 2 * tiles - 1)
    def _():
        hop_back(counts_ref, adjacency_ref, grad_stacked_ref, grad_features_ref, {})


def unpack_kernel(
    middle_ref,
    attend_ref,
    tail_ref,
    features_ref,
    grad_features_ref,
    grad_embed_ref,
    grad_gain_one,
    grad_shift_one,
    grad_attend,
    grad_merge,
    grad_gain_two,
    grad_shift_two,
    grad_expand,
    grad_reduce,
    grad_readout,
):
    owner = lax.axis_index("fsdp")
    width = middle_ref.shape[-1]
    grad_features_ref[...] = features_ref[...]
    for half in range(2):
        grad_attend[half * 16 : half * 16 + 16] = attend_ref[half]
        grad_expand[half * 16 : half * 16 + 16, 0:width] = middle_ref[half, 0:16]
        grad_expand[half * 16 : half * 16 + 16, width : 2 * width] = middle_ref[half, 16:32]
        grad_reduce[half * 32 : half * 32 + 32] = middle_ref[half, 32:64]
        grad_merge[half * 16 : half * 16 + 16] = middle_ref[half, 64:80]
    grad_embed_ref[...] = tail_ref[0]
    rows = tail_ref[1]
    length = grad_gain_one.shape[0]
    turned = pltpu.roll(rows, lax.rem(width - owner * length, width), 1)
    for index, ref in enumerate((grad_gain_one, grad_shift_one, grad_gain_two, grad_shift_two)):
        ref[...] = turned[index : index + 1, 0:length].reshape(length)
    length = grad_readout.shape[0]
    first = owner * length
    turned = pltpu.roll(rows, lax.rem(2 * width - first, width), 1)
    row = jnp.where(first < width, turned[4:5, 0:length], turned[5:6, 0:length])
    grad_readout[...] = row.reshape(length)


def whole(shape):
    return pl.BlockSpec(shape, lambda t: (0,) * len(shape), pipeline_mode=pl.Buffered(1))


def kept(shape):
    return pl.BlockSpec(shape, lambda t: (0,) * len(shape))


def tiled(*shape, at=lambda t: t):
    return pl.BlockSpec((None,) + shape, lambda t: (at(t),) + (0,) * len(shape))


def rows_of(*shape, at=lambda t: t):
    return pl.BlockSpec(shape, lambda t: (at(t),) + (0,) * (len(shape) - 1))


def sds(shape, dtype):
    return jax.ShapeDtypeStruct(shape, dtype)


SMEM_SPEC = pl.BlockSpec(memory_space=pltpu.SMEM)


VMEM_SPEC = pl.BlockSpec(memory_space=pltpu.VMEM)
ANY_SPEC = pl.BlockSpec(memory_space=pl.ANY)


def params(collective=None):
    more = {} if collective is None else {"collective_id": collective, "has_side_effects": True}
    return pltpu.CompilerParams(
        vmem_limit_bytes=56 * MIB, dimension_semantics=("arbitrary",), **more
    )


def forward_outs(tiles, feat, width):
    hops, per = HOP_PAIRS, (GROUPS, 2 * GROUP)
    early = lambda t: jnp.minimum(t, tiles - 1)
    late = lambda t: jnp.maximum(t - tiles, 0)
    out_specs = [
        kept((tiles, hops, *per, feat)),
        tiled(TOKENS, width, at=early),
        tiled(TOKENS, width, at=early),
        rows_of(hops, *per, 3 * width, at=late),
        rows_of(hops, *per, width, at=late),
        tiled(TOKENS, width, at=late),
    ]
    out_shape = [
        sds((tiles, hops, *per, feat), BF16),
        sds((tiles, TOKENS, width), F32),
        sds((tiles, TOKENS, width), BF16),
        sds((tiles * hops, *per, 3 * width), BF16),
        sds((tiles * hops, *per, width), BF16),
        sds((tiles, TOKENS, width), F32),
    ]
    keep = [pltpu.VMEM((tiles, TOKENS, width), F32), pltpu.VMEM((tiles, TOKENS, width), BF16)]
    return out_specs, out_shape, keep


def forward_part(
    lines, counts, adjacency, features, embed, vectors, attend, merge, expand, reducer
):
    nodes, feat = features.shape
    owners = lines * PLANE
    width = merge.shape[1]
    tiles = nodes // NODES_PER_TILE
    out_specs, out_shape, keep = forward_outs(tiles, feat, width)
    half = lambda shard: (owners, 2, shard.shape[0] // 2, shard.shape[1])
    copies = lines + PLANE - 2 + (lines - 1) * (PLANE - 1)
    return pl.pallas_call(
        functools.partial(forward_kernel, lines),
        grid=(2 * tiles,),
        in_specs=[SMEM_SPEC, whole(adjacency.shape), whole(features.shape)]
        + [VMEM_SPEC] * 6
        + [whole(attend.shape), whole(merge.shape), ANY_SPEC, ANY_SPEC],
        out_specs=out_specs + [kept((8, width)), kept((feat, width))] + [ANY_SPEC] * 4,
        out_shape=out_shape
        + [sds((8, width), F32), sds((feat, width), BF16)]
        + [sds(half(shard), BF16) for shard in (attend, merge, expand, reducer)],
        scratch_shapes=[
            pltpu.VMEM((8, 128), F32),
            pltpu.VMEM((owners, 16, width // 2 + 128), BF16),
            pltpu.VMEM(half(attend), BF16),
            pltpu.VMEM(half(merge), BF16),
        ]
        + keep
        + [
            pltpu.SemaphoreType.DMA((5, copies)),
            pltpu.SemaphoreType.DMA((5, owners)),
            pltpu.SemaphoreType.DMA((5, 2)),
            pltpu.SemaphoreType.DMA((4,)),
        ],
        compiler_params=params(0),
        name="hops_attention",
    )(counts, adjacency, features, embed, *vectors, attend, merge, expand, reducer)


def forward_alone_part(counts, adjacency, features, rows, embed, attend, merge):
    nodes, feat = features.shape
    width = merge.shape[-1]
    tiles = nodes // NODES_PER_TILE
    out_specs, out_shape, keep = forward_outs(tiles, feat, width)
    return pl.pallas_call(
        forward_alone_kernel,
        grid=(2 * tiles,),
        in_specs=[SMEM_SPEC]
        + [whole(a.shape) for a in (adjacency, features, rows, embed, attend, merge)],
        out_specs=out_specs,
        out_shape=out_shape,
        scratch_shapes=keep,
        compiler_params=params(),
        name="hops_attention_alone",
    )(counts, adjacency, features, rows, embed, attend, merge)


def middle_part(counts, second, mixed, cotangent, rows, expand, reducer):
    tiles, _, width = second.shape
    hops, per = HOP_PAIRS, (GROUPS, 2 * GROUP)
    spread = expand.shape[-1]
    terms = (PACK, 2, 80, width)
    return pl.pallas_call(
        middle_kernel,
        grid=(tiles,),
        in_specs=[
            SMEM_SPEC,
            tiled(TOKENS, width),
            rows_of(hops, *per, width),
            rows_of(NODES_PER_TILE, width),
            whole(rows.shape),
            whole(expand.shape),
            whole(reducer.shape),
        ],
        out_specs=[
            rows_of(NODES_PER_TILE, width),
            tiled(TOKENS, width),
            kept(terms),
            kept(rows.shape),
        ],
        out_shape=[
            sds(cotangent.shape, F32),
            sds(second.shape, F32),
            sds(terms, BF16),
            sds(rows.shape, F32),
        ],
        scratch_shapes=[
            pltpu.VMEM((width, width), F32),
            pltpu.VMEM((width, spread), F32),
            pltpu.VMEM((spread, width), F32),
        ],
        compiler_params=params(),
        name="feed_forward",
    )(counts, second, mixed, cotangent, rows, expand, reducer)


def backward_ins(tiles, feat, width, arrays):
    hops, per = HOP_PAIRS, (GROUPS, 2 * GROUP)
    early = lambda t: jnp.minimum(t, tiles - 1)
    late = lambda t: jnp.maximum(t - tiles, 0)
    both = lambda t: lax.rem(t, tiles)
    return [
        SMEM_SPEC,
        whole(arrays[1].shape),
        rows_of(hops, *per, 3 * width, at=early),
        tiled(TOKENS, width, at=early),
        tiled(TOKENS, width, at=both),
        tiled(TOKENS, width, at=late),
        tiled(hops, *per, feat, at=late),
    ] + [whole(a.shape) for a in arrays[7:]]


def backward_part(lines, *arrays):
    tiles, _, width = arrays[3].shape
    hops, per, feat = HOP_PAIRS, (GROUPS, 2 * GROUP), arrays[6].shape[-1]
    owners = lines * PLANE
    rest = (80, width)
    wide = (width // owners // 2, 3 * width)

    def buffers(shape):
        return [
            pltpu.VMEM((owners,) + shape, BF16),
            pltpu.VMEM((lines, PLANE) + shape, BF16),
            pltpu.VMEM((PLANE - 1, lines) + shape, BF16),
            pltpu.VMEM((lines,) + shape, BF16),
            pltpu.VMEM((lines - 1,) + shape, BF16),
            pltpu.VMEM((2,) + shape, F32),
        ]

    sems = pltpu.SemaphoreType.DMA((2, PLANE + lines))
    outs = [(tiles * NODES_PER_TILE, feat), (2,) + rest, (2,) + wide, (2, 8, width)]
    return pl.pallas_call(
        functools.partial(backward_kernel, lines),
        grid=(2 * tiles,),
        in_specs=backward_ins(tiles, feat, width, arrays),
        out_specs=[kept(shape) for shape in outs],
        out_shape=[sds(shape, F32) for shape in outs],
        scratch_shapes=[
            pltpu.VMEM((hops, *per, width), BF16),
            pltpu.VMEM((tiles, hops, *per, 3 * width), BF16),
            pltpu.VMEM((tiles, hops, GROUPS, 2, GROUP, feat), F32),
            pltpu.VMEM((width, 3 * width), F32),
            pltpu.VMEM((feat, width), F32),
            pltpu.VMEM((8, width), F32),
        ]
        + buffers(rest)
        + [pltpu.VMEM((owners, 2) + wide, BF16)]
        + buffers(wide)
        + [
            pltpu.VMEM((PLANE, lines + 1, 8, width), F32),
            pltpu.VMEM((PLANE - 1, lines + 1, 8, width), F32),
            pltpu.VMEM((lines, 2, 8, width), F32),
            pltpu.VMEM((lines - 1, 2, 8, width), F32),
            pltpu.VMEM((2, 8, width), F32),
            pltpu.VMEM((2, 8, width), F32),
        ]
        + [sems] * 3,
        compiler_params=params(1),
        name="attention_backward",
    )(*arrays)


def backward_alone_part(*arrays):
    tiles, _, width = arrays[3].shape
    hops, per, feat = HOP_PAIRS, (GROUPS, 2 * GROUP), arrays[6].shape[-1]
    outs = [(tiles * NODES_PER_TILE, feat), (width, 3 * width), (feat, width), (8, width)]
    return pl.pallas_call(
        backward_alone_kernel,
        grid=(2 * tiles,),
        in_specs=backward_ins(tiles, feat, width, arrays),
        out_specs=[kept(shape) for shape in outs],
        out_shape=[sds(shape, F32) for shape in outs],
        scratch_shapes=[
            pltpu.VMEM((hops, *per, width), BF16),
            pltpu.VMEM((tiles, hops, *per, 3 * width), BF16),
            pltpu.VMEM((tiles, hops, GROUPS, 2, GROUP, feat), F32),
        ],
        compiler_params=params(),
        name="attention_backward_alone",
    )(*arrays)


def unpack_part(middle, attend, tail, features, shapes):
    return pl.pallas_call(
        unpack_kernel,
        in_specs=[VMEM_SPEC] * 4,
        out_specs=[VMEM_SPEC] * 11,
        out_shape=[sds(features.shape, F32)] + [sds(shape, F32) for shape in shapes],
        compiler_params=pltpu.CompilerParams(vmem_limit_bytes=24 * MIB),
        name="unpack_shares",
    )(middle, attend, tail, features)


def gather(block):
    return lax.all_gather(block, "fsdp", axis=0, tiled=True)


def share(term):
    part = lax.psum_scatter(term.astype(BF16), "fsdp", scatter_dimension=0, tiled=True)
    return lax.psum(part.astype(F32), "grp")


def body(
    features,
    adjacency,
    counts,
    input_weight,
    first_gain,
    first_shift,
    attend_weight,
    merge_weight,
    second_gain,
    second_shift,
    expand_weight,
    reduce_weight,
    readout_weight,
    cotangent,
):
    vectors = (first_gain, first_shift, second_gain, second_shift, readout_weight)
    owners = lax.axis_size("fsdp")
    if owners % PLANE == 0 and input_weight.shape[0] == 8 and attend_weight.shape[0] == 32:
        lines = owners // PLANE
        (
            stacked,
            hidden,
            normed,
            triple,
            mixed,
            second,
            rows,
            embed,
            attend,
            merge,
            expand,
            reducer,
        ) = forward_part(
            lines,
            counts,
            adjacency,
            features,
            input_weight,
            vectors,
            attend_weight,
            merge_weight,
            expand_weight,
            reduce_weight,
        )
        output, grad_second, terms, rows_grad = middle_part(
            counts, second, mixed, cotangent, rows, expand, reducer
        )
        grad_features, *shares = backward_part(
            lines,
            counts,
            adjacency,
            triple,
            normed,
            grad_second,
            hidden,
            stacked,
            embed,
            rows,
            attend,
            merge,
            terms,
            rows_grad,
        )
        shapes = [
            weight.shape
            for weight in (
                input_weight,
                first_gain,
                first_shift,
                attend_weight,
                merge_weight,
                second_gain,
                second_shift,
                expand_weight,
                reduce_weight,
                readout_weight,
            )
        ]
        return (output, *unpack_part(*shares, grad_features, shapes))
    return body_apart(
        features,
        adjacency,
        counts,
        input_weight,
        vectors,
        attend_weight,
        merge_weight,
        expand_weight,
        reduce_weight,
        cotangent,
    )


def body_apart(
    features,
    adjacency,
    counts,
    input_weight,
    vectors,
    attend_weight,
    merge_weight,
    expand_weight,
    reduce_weight,
    cotangent,
):
    lengths = [v.shape[0] for v in vectors]
    places = [sum(lengths[:i]) for i in range(len(lengths) + 1)]
    packed = lax.all_gather(jnp.concatenate(vectors), "fsdp", axis=0, tiled=False)
    width = merge_weight.shape[1]
    full = [
        packed[:, places[i] : places[i + 1]].astype(F32).reshape(-1, width)
        for i in range(len(lengths))
    ]
    rows = jnp.concatenate(full + [jnp.zeros((2, width), F32)], axis=0)
    embed, attend, merge, expand, reducer = map(
        gather, (input_weight, attend_weight, merge_weight, expand_weight, reduce_weight)
    )
    stacked, hidden, normed, triple, mixed, second = forward_alone_part(
        counts, adjacency, features, rows, embed, attend, merge
    )
    output, grad_second, terms, rows_grad = middle_part(
        counts, second, mixed, cotangent, rows, expand, reducer
    )
    grad_features, grad_attend, grad_embed, rows_grad = backward_alone_part(
        counts,
        adjacency,
        triple,
        normed,
        grad_second,
        hidden,
        stacked,
        embed,
        rows,
        attend,
        merge,
        rows_grad,
    )
    spread = expand.shape[1]
    grad_expand = jnp.concatenate([terms[:, :, 0:16], terms[:, :, 16:32]], axis=-1)
    parts = lax.axis_size("fsdp")
    pieces = [rows_grad[i] for i in range(4)] + [rows_grad[4:6]]
    packed_grad = jnp.concatenate([piece.reshape(parts, -1) for piece in pieces], axis=1)
    packed_grad = lax.psum(
        lax.psum_scatter(packed_grad, "fsdp", scatter_dimension=0, tiled=True), "grp"
    ).reshape(-1)
    small = [packed_grad[places[i] : places[i + 1]] for i in range(len(lengths))]
    return (
        output,
        grad_features,
        share(grad_embed),
        small[0],
        small[1],
        share(grad_attend),
        share(terms[:, :, 64:80].reshape(width, width)),
        small[2],
        small[3],
        share(grad_expand.reshape(width, spread)),
        share(terms[:, :, 32:64].reshape(spread, width)),
        small[4],
    )


def solution(mesh):
    nodes = ("grp", "fsdp")
    rows = P("fsdp", None)
    vector = P("fsdp")
    in_specs = (
        P(nodes, None),
        P(nodes, None, None),
        P(nodes),
        rows,
        vector,
        vector,
        rows,
        rows,
        vector,
        vector,
        rows,
        rows,
        vector,
        P(nodes, None),
    )
    out_specs = (
        P(nodes, None),
        P(nodes, None),
        rows,
        vector,
        vector,
        rows,
        rows,
        vector,
        vector,
        rows,
        rows,
        vector,
    )
    return jax.shard_map(body, mesh=mesh, in_specs=in_specs, out_specs=out_specs, check_vma=False)
```

```python
import functools

import jax
import jax.numpy as jnp
from jax import lax
from jax.experimental import pallas as pl
from jax.experimental.pallas import tpu as pltpu
from jax.sharding import PartitionSpec as P

HEADS = 8
HEAD = 64
HOPS = 7
HOP_TOKENS = HOPS + 1
NODES_PER_TILE = 64
TOKENS = NODES_PER_TILE * HOP_TOKENS
GROUP = 8
STREAMS = 2
FEEDS = 1
SKEW = 1
GROUPS = NODES_PER_TILE // GROUP
HOP_PAIRS = HOP_TOKENS // 2
QUAD = 4 * HEAD
MIB = 1 << 20
VMEM_GRANT = 62 * MIB
F32 = jnp.float32
BF16 = jnp.bfloat16
GELU_A = 0.7978845608028654
GELU_B = 0.044715
PLANE = 4
PACK = 16
MESH = pl.DeviceIdType.MESH


def dot(left, right):
    return jnp.dot(left, right, preferred_element_type=F32)


def dot_lead(left, right):
    return lax.dot_general(left, right, (((0,), (0,)), ((), ())), preferred_element_type=F32)


def dot_last(left, right):
    return lax.dot_general(left, right, (((1,), (1,)), ((), ())), preferred_element_type=F32)


def link_of(adjacency, count):
    slots = adjacency.shape[0]
    rows = lax.broadcasted_iota(jnp.int32, (slots, slots), 0)
    cols = lax.broadcasted_iota(jnp.int32, (slots, slots), 1)
    live = jnp.logical_and(rows < count, cols < count)
    link = jnp.where(live, adjacency, 0) + jnp.where(rows == cols, 1, 0)
    link = link.astype(F32)
    root = lax.rsqrt(jnp.sum(link, axis=-1, keepdims=True))
    return link.astype(BF16), root


def hop(link, root, state):
    width = state.shape[1]
    scaled = state * root
    high = scaled.astype(BF16)
    rest = scaled - high.astype(F32)
    middle = rest.astype(BF16)
    low = (rest - middle.astype(F32)).astype(BF16)
    spread = dot(link, jnp.concatenate([high, middle, low], axis=1))
    return (spread[:, :width] + (spread[:, width : 2 * width] + spread[:, 2 * width :])) * root


def live_rows(count, first, rows):
    index = lax.broadcasted_iota(jnp.int32, (rows, 1), 0) + first
    return jnp.where(index < count, 1.0, 0.0).astype(F32)


def norm_stats(values):
    mean = jnp.mean(values, axis=-1, keepdims=True)
    centred = values - mean
    var = jnp.mean(centred * centred, axis=-1, keepdims=True)
    inv = lax.rsqrt(var + 1e-05)
    return centred * inv, inv


def quad_stack(block):
    head = lax.broadcasted_iota(jnp.int32, block.shape, 1) // HEAD
    return jnp.concatenate(
        [jnp.where(head == h, block, jnp.zeros_like(block)) for h in range(4)], axis=0
    )


def grad_softmax(probs, grad_probs):
    tokens, columns = probs.shape
    weighted = (probs * grad_probs).reshape(HOP_TOKENS, GROUP, columns)
    total = jnp.sum(weighted, axis=0)
    shaped = probs.reshape(HOP_TOKENS, GROUP, columns)
    return (weighted - shaped * total[None]).reshape(tokens, columns).astype(BF16)


def quad_probs(scores):
    tokens, columns = scores.shape
    scores = scores.reshape(HOP_TOKENS, GROUP, columns)
    top = jnp.max(scores, axis=0)
    power = jnp.exp((scores - top[None]) * HEAD ** (-0.5))
    row = lax.broadcasted_iota(jnp.int32, (GROUP, columns), 0)
    col = lax.broadcasted_iota(jnp.int32, (GROUP, columns), 1) % GROUP
    share = jnp.where(row == col, 1.0 / jnp.sum(power, axis=0), 0.0)
    return (power * share[None]).reshape(tokens, columns)


def queries_from(weights, block):
    tokens = block.shape[0]
    out = []
    lane = lax.broadcasted_iota(jnp.int32, (tokens, 2 * HEAD), 1)
    for first in (0, 2 * HEAD):
        both = dot_lead(weights[:, first : first + 2 * HEAD], block[:, first : first + 2 * HEAD])
        out.append(jnp.where(lane < HEAD, both[:tokens], both[tokens:]))
    return jnp.concatenate(out, axis=1)


def hop_rows(values, index):
    shaped = values.reshape(HOP_PAIRS, GROUPS, 2, GROUP, values.shape[-1])
    return shaped[index // 2, :, index % 2].reshape(NODES_PER_TILE, values.shape[-1])


def hop_join(parts):
    width = parts[0].shape[-1]
    blocks = []
    for pair in range(HOP_PAIRS):
        both = [parts[2 * pair + k].reshape(GROUPS, 1, GROUP, width) for k in range(2)]
        blocks.append(jnp.concatenate(both, axis=1))
    return jnp.concatenate(blocks, axis=0).reshape(TOKENS, width)


def interleave(streams):
    live = list(enumerate(streams))
    turn = 0
    while live:
        live = [
            (place, stream)
            for place, stream in live
            if turn < place * SKEW or next(stream, live) is not live
        ]
        turn += 1


class Place:
    def __init__(self, lines):
        self.lines = lines
        self.core = lax.axis_index("grp")
        self.owner = lax.axis_index("fsdp")
        self.line = lax.div(self.owner, PLANE)
        self.spot = lax.rem(self.owner, PLANE)

    def line_turn(self, ahead):
        return lax.rem(self.line + ahead + self.lines, self.lines)

    def spot_turn(self, ahead):
        return lax.rem(self.spot + ahead + PLANE, PLANE)

    def line_peer(self, ahead):
        return (self.core, self.line_turn(ahead) * PLANE + self.spot)

    def plane_peer(self, ahead):
        return (self.core, self.line * PLANE + self.spot_turn(ahead))

    def sibling(self):
        return (1 - self.core, self.owner)

    def peers(self):
        return (
            [self.line_peer(d) for d in range(1, self.lines)]
            + [self.plane_peer(e) for e in range(1, PLANE)]
            + [self.sibling()]
        )

    def greet(self):
        barrier = pltpu.get_barrier_semaphore()
        for peer in self.peers():
            pl.semaphore_signal(barrier, inc=1, device_id=peer, device_id_type=MESH)

    def greeted(self):
        pl.semaphore_wait(pltpu.get_barrier_semaphore(), self.lines + PLANE - 1)


def remote(source, target, send, recv, device):
    return pltpu.make_async_remote_copy(
        src_ref=source,
        dst_ref=target,
        send_sem=send,
        recv_sem=recv,
        device_id=device,
        device_id_type=MESH,
    )


class Gather:
    def __init__(self, place, slots, source, send, recv, pair, halves=True):
        self.place, self.slots, self.source = place, slots, source
        self.send, self.recv, self.pair_sems, self.halves = send, recv, pair, halves

    def slot(self, owner):
        return self.slots.at[owner, self.place.core] if self.halves else self.slots.at[owner]

    def own_copies(self):
        place = self.place
        peers = [place.line_peer(d) for d in range(1, place.lines)]
        peers += [place.plane_peer(e) for e in range(1, PLANE)]
        return [
            remote(
                self.source, self.slot(place.owner), self.send.at[i], self.recv.at[place.owner], peer
            )
            for i, peer in enumerate(peers)
        ]

    def onward(self, d):
        place = self.place
        owner = place.line_turn(-d) * PLANE + place.spot
        first = place.lines + PLANE - 2 + (d - 1) * (PLANE - 1)
        return [
            remote(
                self.slot(owner),
                self.slot(owner),
                self.send.at[first + e - 1],
                self.recv.at[owner],
                place.plane_peer(e),
            )
            for e in range(1, PLANE)
        ]

    def start_line(self):
        for copy in self.own_copies()[: self.place.lines - 1]:
            copy.start()

    def start_plane(self):
        for copy in self.own_copies()[self.place.lines - 1 :]:
            copy.start()

    def start(self):
        self.start_line()
        self.start_plane()

    def forward(self):
        for d in range(1, self.place.lines):
            copies = self.onward(d)
            copies[0].wait_recv()
            for copy in copies:
                copy.start()

    def finish(self):
        place = self.place
        for d in range(place.lines):
            for e in range(1, PLANE):
                owner = place.line_turn(d) * PLANE + place.spot_turn(-e)
                remote(
                    self.slot(owner),
                    self.slot(owner),
                    self.send.at[0],
                    self.recv.at[owner],
                    place.plane_peer(e),
                ).wait_recv()
        for copy in self.own_copies():
            copy.wait_send()
        for d in range(1, place.lines):
            for copy in self.onward(d):
                copy.wait_send()

    def pair(self):
        half = self.slots.at[:, self.place.core]
        return remote(half, half, self.pair_sems.at[0], self.pair_sems.at[1], self.place.sibling())


class Scatter:
    def __init__(self, place, terms, got, chip, plane_got, line_out, line_got, result, sems):
        self.place, self.terms, self.got, self.chip = place, terms, got, chip
        self.plane_got, self.line_out, self.line_got = plane_got, line_out, line_got
        self.result, self.sems = result, sems

    def pair(self):
        place = self.place
        return remote(
            self.terms.at[:, 1 - place.core],
            self.got,
            self.sems.at[0, 0],
            self.sems.at[1, 0],
            place.sibling(),
        )

    def plane(self):
        place = self.place
        return [
            remote(
                self.chip.at[:, place.spot_turn(e)],
                self.plane_got.at[e - 1],
                self.sems.at[0, e],
                self.sems.at[1, e],
                place.plane_peer(e),
            )
            for e in range(1, PLANE)
        ]

    def line(self):
        place = self.place
        return [
            remote(
                self.line_out.at[place.line_turn(d)],
                self.line_got.at[d - 1],
                self.sems.at[0, PLANE + d - 1],
                self.sems.at[1, PLANE + d - 1],
                place.line_peer(d),
            )
            for d in range(1, place.lines)
        ]

    def last(self):
        place = self.place
        half = self.result.at[place.core]
        k = PLANE + place.lines - 1
        return remote(half, half, self.sems.at[0, k], self.sems.at[1, k], place.sibling())

    def begin(self):
        self.pair().start()

    def to_plane(self):
        place = self.place
        self.pair().wait()

        def add(line, carry):
            for spot in range(PLANE):
                owner = line * PLANE + spot
                both = self.terms[owner, place.core].astype(F32) + self.got[owner].astype(F32)
                self.chip[line, spot] = both.astype(BF16)
            return carry

        lax.fori_loop(0, place.lines, add, 0)
        for copy in self.plane():
            copy.start()

    def to_line(self):
        place = self.place
        for copy in self.plane():
            copy.wait()

        def add(line, carry):
            total = self.chip[line, place.spot].astype(F32)
            for e in range(PLANE - 1):
                total = total + self.plane_got[e, line].astype(F32)
            self.line_out[line] = total.astype(BF16)
            return carry

        lax.fori_loop(0, place.lines, add, 0)
        for copy in self.line():
            copy.start()

    def to_sibling(self):
        place = self.place
        for copy in self.line():
            copy.wait()
        total = self.line_out[place.line].astype(F32)
        for d in range(place.lines - 1):
            total = total + self.line_got[d].astype(F32)
        self.result[place.core] = total
        self.last().start()

    def end(self):
        self.last().wait()


class TailScatter:
    def __init__(self, place, own, plane_got, line_out, line_got, mine, other, sems):
        self.place, self.own, self.plane_got, self.line_out = place, own, plane_got, line_out
        self.line_got, self.mine, self.other, self.sems = line_got, mine, other, sems

    def plane(self):
        place = self.place
        return [
            remote(
                self.own.at[place.spot_turn(e)],
                self.plane_got.at[e - 1],
                self.sems.at[0, e],
                self.sems.at[1, e],
                place.plane_peer(e),
            )
            for e in range(1, PLANE)
        ]

    def line(self):
        place = self.place
        return [
            remote(
                self.line_out.at[place.line_turn(d)],
                self.line_got.at[d - 1],
                self.sems.at[0, PLANE + d - 1],
                self.sems.at[1, PLANE + d - 1],
                place.line_peer(d),
            )
            for d in range(1, place.lines)
        ]

    def last(self):
        return remote(
            self.mine, self.other, self.sems.at[0, 0], self.sems.at[1, 0], self.place.sibling()
        )

    def begin(self):
        for copy in self.plane():
            copy.start()

    def to_line(self):
        place = self.place
        for copy in self.plane():
            copy.wait()
        total = self.own[place.spot]
        for e in range(PLANE - 1):
            total = total + self.plane_got[e]
        for line in range(place.lines):
            self.line_out[line, 0] = total[line]
            self.line_out[line, 1] = total[place.lines]
        for copy in self.line():
            copy.start()

    def to_sibling(self):
        place = self.place
        for copy in self.line():
            copy.wait()
        total = self.line_out[place.line]
        for d in range(place.lines - 1):
            total = total + self.line_got[d]
        self.mine[...] = total
        self.last().start()

    def end(self):
        self.last().wait()
        return self.mine[...] + self.other[...]


def hop_states(counts_ref, adjacency_ref, features_ref, stacked_ref):
    clusters, slots = adjacency_ref.shape[:2]
    per_cluster = slots // NODES_PER_TILE
    links = []
    states = []
    for cluster in range(clusters):
        count = counts_ref[cluster]
        links.append(link_of(adjacency_ref[cluster], count))
        states.append(
            features_ref[cluster * slots : (cluster + 1) * slots].astype(F32)
            * live_rows(count, 0, slots)
        )
    earlier = [None] * clusters
    for index in range(HOP_TOKENS):
        for cluster in range(clusters):
            if index > 0:
                states[cluster] = hop(*links[cluster], states[cluster])
            if index % 2 == 0:
                earlier[cluster] = states[cluster]
                continue
            for part in range(per_cluster):
                rows = slice(part * NODES_PER_TILE, (part + 1) * NODES_PER_TILE)
                both = [
                    state[rows].reshape(GROUPS, GROUP, state.shape[-1])
                    for state in (earlier[cluster], states[cluster])
                ]
                stacked_ref[cluster * per_cluster + part, index // 2] = jnp.concatenate(
                    both, axis=1
                ).astype(BF16)


def spread_vectors(small, owners, width):
    rows = small.shape[0]
    lane = lax.broadcasted_iota(jnp.int32, (128, width), 0)
    column = lax.broadcasted_iota(jnp.int32, (128, width), 1)
    row = lax.broadcasted_iota(jnp.int32, (rows, width), 0)
    place = lax.broadcasted_iota(jnp.int32, (rows, width), 1)
    piece = width // owners
    pieces = dot(small, jnp.where(lane == column % piece, 1.0, 0.0).astype(BF16))
    out = []
    for vector in range(4):
        mine = jnp.logical_and(row % 8 == vector, lax.div(row, 8) == lax.div(place, piece))
        out.append(jnp.sum(jnp.where(mine, pieces, 0.0), axis=0, keepdims=True))
    pieces = dot(small, jnp.where(lane == column % (2 * piece), 1.0, 0.0).astype(BF16))
    for first in (0, owners // 2):
        owner = lax.div(place, 2 * piece) + first
        mine = jnp.logical_and(row % 8 == 4, lax.div(row, 8) == owner)
        out.append(jnp.sum(jnp.where(mine, pieces, 0.0), axis=0, keepdims=True))
    return jnp.concatenate(out + [jnp.zeros((2, width), F32)], axis=0)


def hop_back(counts_ref, adjacency_ref, grad_stacked_ref, grad_features_ref, between):
    clusters, slots = adjacency_ref.shape[:2]
    per_cluster = slots // NODES_PER_TILE
    links = []
    states = []

    def hop_grad(cluster, index):
        return jnp.concatenate(
            [
                grad_stacked_ref[cluster * per_cluster + p, index // 2, :, index % 2].reshape(
                    NODES_PER_TILE, grad_stacked_ref.shape[-1]
                )
                for p in range(per_cluster)
            ],
            axis=0,
        )

    for cluster in range(clusters):
        links.append(link_of(adjacency_ref[cluster], counts_ref[cluster]))
        states.append(hop_grad(cluster, HOPS))
    for index in range(HOPS - 1, -1, -1):
        for cluster in range(clusters):
            states[cluster] = hop_grad(cluster, index) + hop(*links[cluster], states[cluster])
        if index in between:
            between[index]()
    for cluster in range(clusters):
        grad_features_ref[cluster * slots : (cluster + 1) * slots] = states[cluster] * live_rows(
            counts_ref[cluster], 0, slots
        )


def block_of(ref, tile, group, first):
    return ref[tile, :, group, :, first : first + QUAD].reshape(GROUP * HOP_TOKENS, QUAD)


def put_block(ref, tile, group, first, block):
    ref[tile, :, group, :, first : first + QUAD] = block.astype(BF16).reshape(
        HOP_PAIRS, 2 * GROUP, QUAD
    )


def tokens_of(ref, tile):
    return ref[tile].reshape(TOKENS, ref.shape[-1])


def embed_tile(tile, stacked_ref, embed, gain, shift, second_ref, normed_ref):
    hidden = dot(tokens_of(stacked_ref, tile), embed)
    second_ref[tile] = hidden
    normal, _ = norm_stats(hidden)
    normed_ref[tile] = (normal * gain + shift).astype(BF16)


def attend_tile(tile, normed_ref, attend, merge_of, triple_ref, mixed_ref, second_ref):
    width = normed_ref.shape[-1]
    triple = dot(normed_ref[tile], attend).astype(BF16)
    triple_ref[tile] = triple.reshape(triple_ref.shape[1:])
    places = [(tile, g, first) for g in range(GROUPS) for first in range(0, width, QUAD)]
    keys = [block_of(triple_ref, t, g, width + first) for t, g, first in places]
    queries = [quad_stack(block_of(triple_ref, *place)) for place in places]
    scores = [dot_last(k, q) for k, q in zip(keys, queries)]
    probs = [quad_probs(score).astype(BF16) for score in scores]
    values = [block_of(triple_ref, t, g, 2 * width + first) for t, g, first in places]
    blocks = [queries_from(p, v) for p, v in zip(probs, values)]
    for place, block in zip(places, blocks):
        put_block(mixed_ref, *place, block)
    second_ref[tile] += dot(tokens_of(mixed_ref, tile), merge_of())


def middle_step(
    first_tile,
    counts_ref,
    second_ref,
    mixed_ref,
    cotangent_ref,
    rows_ref,
    expand,
    reducer,
    output_ref,
    rows_grad_ref,
    grad_merge_ref,
    grad_expand_ref,
    grad_reduce_ref,
):
    width = second_ref.shape[-1]
    gain, shift = rows_ref[2:3], rows_ref[3:4]
    row_node, row_hop = rows_ref[4:5], rows_ref[5:6]

    def stream(part):
        tile = first_tile + part
        second = second_ref[tile]
        normal, inv = norm_stats(second)
        inner = (normal * gain + shift).astype(BF16)
        yield
        before = dot(inner, expand)
        yield
        square = before * before
        curve = jnp.tanh(GELU_A * before * (1.0 + GELU_B * square))
        after = (0.5 * before * (1.0 + curve)).astype(BF16)
        slope = 0.5 * (1.0 + curve) + (0.5 * GELU_A) * before * (1.0 - curve * curve) * (
            1.0 + (3.0 * GELU_B) * square
        )
        yield
        third = second + dot(after, reducer)
        yield
        shaped = [hop_rows(third, k) for k in range(HOP_TOKENS)]
        node = tile * NODES_PER_TILE
        keep = live_rows(counts_ref[lax.div(node, 128)], lax.rem(node, 128), NODES_PER_TILE)
        centre = shaped[0]
        base = jnp.sum(centre * row_node, axis=-1, keepdims=True)
        logits = [
            base + jnp.sum(shaped[k] * row_hop, axis=-1, keepdims=True)
            for k in range(1, HOP_TOKENS)
        ]
        top = functools.reduce(jnp.maximum, logits)
        powers = [jnp.exp(logit - top) for logit in logits]
        scale = 1.0 / functools.reduce(jnp.add, powers)
        shares = [power * scale for power in powers]
        total = centre
        for k in range(1, HOP_TOKENS):
            total = total + shares[k - 1] * shaped[k]
        output_ref[tile] = total * keep
        cotangent = cotangent_ref[tile] * keep
        grad_shares = [
            jnp.sum(cotangent * shaped[k], axis=-1, keepdims=True) for k in range(1, HOP_TOKENS)
        ]
        mean_share = functools.reduce(jnp.add, [s * g for s, g in zip(shares, grad_shares)])
        grad_logits = [s * (g - mean_share) for s, g in zip(shares, grad_shares)]
        grad_base = functools.reduce(jnp.add, grad_logits)
        parts = [cotangent + grad_base * row_node]
        read_hop = jnp.zeros((NODES_PER_TILE, width), F32)
        for k in range(1, HOP_TOKENS):
            parts.append(shares[k - 1] * cotangent + grad_logits[k - 1] * row_hop)
            read_hop = read_hop + grad_logits[k - 1] * shaped[k]
        rows_grad_ref[4:5] += jnp.sum(grad_base * centre, axis=0, keepdims=True)
        rows_grad_ref[5:6] += jnp.sum(read_hop, axis=0, keepdims=True)
        grad_third = hop_join(parts)
        grad_branch = grad_third.astype(BF16)
        yield
        grad_after = dot_last(grad_branch, reducer)
        grad_reduce_ref[...] += dot_lead(after, grad_branch)
        yield
        grad_before = (slope * grad_after).astype(BF16)
        yield
        grad_inner = dot_last(grad_before, expand)
        grad_expand_ref[...] += dot_lead(inner, grad_before)
        yield
        rows_grad_ref[2:3] += jnp.sum(grad_inner * normal, axis=0, keepdims=True)
        rows_grad_ref[3:4] += jnp.sum(grad_inner, axis=0, keepdims=True)
        grad_normal = grad_inner * gain
        grad_second = grad_third + inv * (
            grad_normal
            - jnp.mean(grad_normal, axis=-1, keepdims=True)
            - normal * jnp.mean(grad_normal * normal, axis=-1, keepdims=True)
        )
        second_ref[tile] = grad_second
        yield
        grad_merge_ref[...] += dot_lead(tokens_of(mixed_ref, tile), grad_second.astype(BF16))

    interleave([stream(part) for part in range(FEEDS)])


def pack_terms(terms_ref, grad_merge_ref, grad_expand_ref, grad_reduce_ref):
    width, spread = grad_expand_ref.shape
    wide = grad_expand_ref[...].astype(BF16).reshape(PACK, 2, width // PACK // 2, spread)
    deep = grad_reduce_ref[...].astype(BF16).reshape(PACK, 2, spread // PACK // 2, width)
    square = grad_merge_ref[...].astype(BF16).reshape(PACK, 2, width // PACK // 2, width)
    terms_ref[:, :, 0:16] = wide[..., :width]
    terms_ref[:, :, 16:32] = wide[..., width:]
    terms_ref[:, :, 32:64] = deep
    terms_ref[:, :, 64:80] = square


def attend_back_step(quad, first_tile, triple_ref, second_ref, normed_ref, merge, grad_mixed_ref, grad_attend_ref):
    width = normed_ref.shape[-1]
    for part in range(STREAMS):
        grad_mixed = dot_last(second_ref[first_tile + part].astype(BF16), merge).astype(BF16)
        grad_mixed_ref[part] = grad_mixed.reshape(grad_mixed_ref.shape[1:])
    places = [(part, group) for part in range(STREAMS) for group in range(GROUPS)]
    scale = HEAD ** (-0.5)
    starts = [kind * width + quad * QUAD for kind in range(3)]

    def read(kind):
        return [block_of(triple_ref, first_tile + p, g, starts[kind]) for p, g in places]

    keys = read(1)
    queries = [quad_stack(block) for block in read(0)]
    scores = [dot_last(k, q) for k, q in zip(keys, queries)]
    values = read(2)
    out_grads = [quad_stack(block_of(grad_mixed_ref, p, g, 0)) for p, g in places]
    grad_probs = [dot_last(v, o) for v, o in zip(values, out_grads)]
    probs = [quad_probs(score) for score in scores]
    grad_scores = [grad_softmax(p, g) for p, g in zip(probs, grad_probs)]
    grad_values = [dot(p.astype(BF16), o) for p, o in zip(probs, out_grads)]
    grad_keys = [dot(s, q) for s, q in zip(grad_scores, queries)]
    grad_queries = [queries_from(s, k) for s, k in zip(grad_scores, keys)]
    for (part, group), a, b, c in zip(places, grad_queries, grad_keys, grad_values):
        for start, block in zip(starts, (a * scale, b * scale, c)):
            put_block(triple_ref, first_tile + part, group, start, block)
    tiles = pl.ds(first_tile, STREAMS)
    grads = jnp.concatenate(
        [
            triple_ref[tiles, :, :, :, start : start + QUAD].reshape(STREAMS * TOKENS, QUAD)
            for start in starts
        ],
        axis=1,
    )
    grad_attend_ref[:, 0 : 3 * QUAD] += dot_lead(
        normed_ref[tiles].reshape(STREAMS * TOKENS, width), grads
    )


def embed_back_step(
    first_tile,
    stacked_ref,
    second_ref,
    triple_ref,
    attend,
    embed,
    gain,
    rows_keep,
    grad_embed_ref,
    grad_stacked_ref,
):
    def stream(part):
        tile = first_tile + part
        stacked = tokens_of(stacked_ref, tile)
        grad_normed = dot_last(tokens_of(triple_ref, tile), attend)
        hidden = dot(stacked, embed)
        yield
        normal, inv = norm_stats(hidden)
        rows_keep[0:1] += jnp.sum(grad_normed * normal, axis=0, keepdims=True)
        rows_keep[1:2] += jnp.sum(grad_normed, axis=0, keepdims=True)
        grad_normal = grad_normed * gain
        grad_hidden = second_ref[tile] + inv * (
            grad_normal
            - jnp.mean(grad_normal, axis=-1, keepdims=True)
            - normal * jnp.mean(grad_normal * normal, axis=-1, keepdims=True)
        )
        grad_hidden = grad_hidden.astype(BF16)
        yield
        grad_embed_ref[...] += dot_lead(stacked, grad_hidden)
        grad_stacked_ref[tile] = dot_last(grad_hidden, embed).reshape(grad_stacked_ref.shape[1:])

    interleave([stream(part) for part in range(STREAMS)])


class Silent:
    def __getattr__(self, name):
        return lambda *arguments: None


def loop(count, step):
    def body(index, carry):
        step(index)
        return carry

    lax.fori_loop(0, count, body, 0)


def layer_phases(
    counts_ref,
    adjacency_ref,
    features_ref,
    cotangent_ref,
    rows_ref,
    embed_ref,
    attend_ref,
    merge_ref,
    expand_ref,
    reduce_ref,
    output_ref,
    grad_features_ref,
    terms_ref,
    early_terms,
    late_terms,
    grad_embed_ref,
    rows_keep,
    keep,
    transfers,
):
    (
        stacked_ref,
        second_ref,
        normed_ref,
        triple_ref,
        mixed_ref,
        grad_mixed_ref,
        grad_merge_ref,
        grad_expand_ref,
        grad_reduce_ref,
        grad_stacked_ref,
    ) = keep
    tiles, _, width = second_ref.shape
    pairs = tiles // STREAMS
    hop_states(counts_ref, adjacency_ref, features_ref, stacked_ref)
    transfers.head()

    def embed_step(tile):
        embed_tile(
            tile, stacked_ref, embed_ref[...], rows_ref[0:1], rows_ref[1:2], second_ref, normed_ref
        )
        transfers.beside_embed(tile, tiles)

    loop(tiles, embed_step)
    transfers.before_attention()

    def attend_step(tile):
        def merge_of():
            transfers.before_merge(tile)
            return merge_ref[...].reshape(width, width)

        attend_tile(
            tile,
            normed_ref,
            attend_ref[...].reshape(width, 3 * width),
            merge_of,
            triple_ref,
            mixed_ref,
            second_ref,
        )
        transfers.beside_attention(tile, tiles)

    loop(tiles, attend_step)
    transfers.before_middle()
    for ref in (rows_keep, grad_merge_ref, grad_expand_ref, grad_reduce_ref, grad_embed_ref):
        ref[...] = jnp.zeros_like(ref)
    spread = grad_expand_ref.shape[1]

    def feed_step(pair):
        middle_step(
            pair * FEEDS,
            counts_ref,
            second_ref,
            mixed_ref,
            cotangent_ref,
            rows_ref,
            expand_ref[...].reshape(width, spread),
            reduce_ref[...].reshape(spread, width),
            output_ref,
            rows_keep,
            grad_merge_ref,
            grad_expand_ref,
            grad_reduce_ref,
        )

    loop(tiles // FEEDS, feed_step)
    pack_terms(terms_ref, grad_merge_ref, grad_expand_ref, grad_reduce_ref)
    transfers.after_middle()
    grad_attend_ref = grad_expand_ref
    for quad, terms in enumerate((early_terms, late_terms)):
        grad_attend_ref[...] = jnp.zeros_like(grad_attend_ref)

        def back_step(pair, quad=quad):
            attend_back_step(
                quad,
                pair * STREAMS,
                triple_ref,
                second_ref,
                normed_ref,
                merge_ref[...].reshape(width, width)[quad * QUAD : (quad + 1) * QUAD],
                grad_mixed_ref,
                grad_attend_ref,
            )
            transfers.beside_backward(quad, pair, pairs)

        loop(pairs, back_step)
        terms[...] = grad_attend_ref[:, 0 : 3 * QUAD].astype(BF16).reshape(terms.shape)
        transfers.after_backward(quad)

    def embed_back(pair):
        embed_back_step(
            pair * STREAMS,
            stacked_ref,
            second_ref,
            triple_ref,
            attend_ref[...].reshape(width, 3 * width),
            embed_ref[...],
            rows_ref[0:1],
            rows_keep,
            grad_embed_ref,
            grad_stacked_ref,
        )
        transfers.beside_embed_back(pair, pairs)

    loop(pairs, embed_back)
    transfers.after_embed_back()
    hop_back(
        counts_ref,
        adjacency_ref,
        grad_stacked_ref,
        grad_features_ref,
        {1: transfers.beside_hops},
    )
    transfers.end()


class Transfers:
    def __init__(self, place, gathers, scatters, unpack_head, pack_tail, publish):
        self.place = place
        self.lead, self.attend, self.merge, self.expand, self.reducer = gathers
        self.middle, self.early, self.late, self.tail = scatters
        self.unpack_head, self.pack_tail, self.publish = unpack_head, pack_tail, publish

    def head(self):
        self.place.greeted()
        self.lead.start()
        self.attend.start_line()
        self.lead.forward()
        self.attend.start_plane()
        self.attend.forward()
        self.lead.finish()
        self.unpack_head()

    def beside_embed(self, tile, tiles):
        @pl.when(tile == 0)
        def _():
            self.merge.start()

        @pl.when(tile == tiles - 3)
        def _():
            self.merge.forward()

        @pl.when(tile == tiles - 2)
        def _():
            self.attend.finish()
            self.attend.pair().start()
            self.expand.start()
            self.reducer.start()

    def before_attention(self):
        self.merge.finish()
        self.merge.pair().start()
        self.attend.pair().wait()

    def before_merge(self, tile):
        @pl.when(tile == 0)
        def _():
            self.merge.pair().wait()
            self.expand.forward()
            self.reducer.forward()

    def beside_attention(self, tile, tiles):
        @pl.when(tile == tiles - 2)
        def _():
            self.expand.finish()
            self.expand.pair().start()
            self.reducer.finish()
            self.reducer.pair().start()

    def before_middle(self):
        self.expand.pair().wait()
        self.reducer.pair().wait()

    def after_middle(self):
        self.middle.begin()

    def beside_backward(self, quad, pair, pairs):
        if quad == 0:

            @pl.when(pair == 0)
            def _():
                self.middle.to_plane()

        else:

            @pl.when(pair == 0)
            def _():
                self.early.to_plane()

            @pl.when(pair == pairs - 2)
            def _():
                self.middle.to_line()

    def after_backward(self, quad):
        if quad == 0:
            self.early.begin()
        else:
            self.late.begin()
            self.early.to_line()

    def beside_embed_back(self, pair, pairs):
        @pl.when(pair == 0)
        def _():
            self.late.to_plane()

        @pl.when(pair == 1)
        def _():
            self.middle.to_sibling()

    def after_embed_back(self):
        self.pack_tail()
        self.tail.begin()
        self.early.to_sibling()

    def beside_hops(self):
        self.late.to_line()
        self.tail.to_line()

    def end(self):
        self.tail.to_sibling()
        self.middle.end()
        self.early.end()
        self.late.to_sibling()
        tail = self.tail.end()
        self.late.end()
        self.publish(tail)


def layer_kernel(
    lines,
    counts_ref,
    adjacency_ref,
    features_ref,
    cotangent_ref,
    embed_shard,
    vector_a,
    vector_b,
    vector_c,
    vector_d,
    vector_e,
    attend_shard,
    merge_shard,
    expand_shard,
    reduce_shard,
    output_ref,
    grad_features_ref,
    middle_share_ref,
    attend_share_ref,
    tail_share_ref,
    *scratch,
):
    keep = scratch[0:10]
    embed_ref, rows_ref, small_keep, head_slots = scratch[10:14]
    attend_slots, merge_slots, expand_slots, reduce_slots = scratch[14:18]
    grad_embed_ref, rows_keep = scratch[18:20]
    middle_refs, early_refs, late_refs = scratch[20:27], scratch[27:34], scratch[34:41]
    tail_refs = scratch[41:47]
    send, recv, pair, scatter_sems = scratch[47:51]
    owners = head_slots.shape[0]
    width = embed_ref.shape[-1]
    half_width = width // 2
    place = Place(lines)
    core, owner = place.core, place.owner
    place.greet()

    def half_of(shard):
        rows = shard.shape[0] // 2
        return shard.at[pl.ds(pl.multiple_of(core * rows, rows), rows)]

    def gather(index, slots, source, halves=True):
        return Gather(
            place, slots, source, send.at[index], recv.at[index], pair.at[index], halves
        )

    small_keep[...] = jnp.zeros_like(small_keep)
    for index, vector in enumerate((vector_a, vector_b, vector_c, vector_d, vector_e)):
        length = vector.shape[0]
        small_keep[index : index + 1, 0:length] = vector[...].astype(F32).reshape(1, length)
    mine = embed_shard[...].astype(F32)
    packed = jnp.concatenate(
        [
            jnp.concatenate([mine[:, :half_width], small_keep[...]], axis=1),
            jnp.concatenate([mine[:, half_width:], jnp.zeros((8, 128), F32)], axis=1),
        ],
        axis=0,
    )
    head_slots[owner] = packed.astype(BF16)
    matrices = (
        (attend_slots, attend_shard),
        (merge_slots, merge_shard),
        (expand_slots, expand_shard),
        (reduce_slots, reduce_shard),
    )
    for slots, shard in matrices:
        slots[owner, core] = half_of(shard)[...]
    gathers = [gather(0, head_slots, head_slots.at[owner], False)]
    gathers += [
        gather(1 + index, slots, half_of(shard)) for index, (slots, shard) in enumerate(matrices)
    ]
    middle = Scatter(place, *middle_refs, scatter_sems.at[0])
    early = Scatter(place, *early_refs, scatter_sems.at[1])
    late = Scatter(place, *late_refs, scatter_sems.at[2])
    tail = TailScatter(place, *tail_refs, scatter_sems.at[3])

    def unpack_head():
        whole_head = head_slots[...].astype(F32)
        top = whole_head[:, 0:8].reshape(owners * 8, half_width + 128)
        bottom = whole_head[:, 8:16].reshape(owners * 8, half_width + 128)
        embed_ref[:, :half_width] = top[:, :half_width].astype(BF16)
        embed_ref[:, half_width:] = bottom[:, :half_width].astype(BF16)
        rows_ref[...] = spread_vectors(top[:, half_width:].astype(BF16), owners, width)

    def pack_tail():
        own = grad_embed_ref[...].reshape(lines, PLANE, 8, width)
        for spot in range(PLANE):
            tail.own[spot, 0:lines] = own[:, spot]
            tail.own[spot, lines] = rows_keep[...]

    def publish(tail_total):
        middle_share_ref[...] = middle.result[...]
        attend_share_ref[0] = early.result[...]
        attend_share_ref[1] = late.result[...]
        tail_share_ref[...] = tail_total

    transfers = Transfers(
        place, gathers, (middle, early, late, tail), unpack_head, pack_tail, publish
    )
    layer_phases(
        counts_ref,
        adjacency_ref,
        features_ref,
        cotangent_ref,
        rows_ref,
        embed_ref,
        attend_slots,
        merge_slots,
        expand_slots,
        reduce_slots,
        output_ref,
        grad_features_ref,
        middle.terms,
        early.terms,
        late.terms,
        grad_embed_ref,
        rows_keep,
        keep,
        transfers,
    )


def layer_alone_kernel(*refs):
    layer_phases(*refs[:17], refs[17:], Silent())


def unpack_kernel(
    middle_ref,
    attend_ref,
    tail_ref,
    features_ref,
    nodes_ref,
    output_ref,
    grad_features_ref,
    grad_embed_ref,
    grad_gain_one,
    grad_shift_one,
    grad_attend,
    grad_merge,
    grad_gain_two,
    grad_shift_two,
    grad_expand,
    grad_reduce,
    grad_readout,
):
    owner = lax.axis_index("fsdp")
    width = middle_ref.shape[-1]
    output_ref[...] = nodes_ref[...]
    grad_features_ref[...] = features_ref[...]
    for half in range(2):
        for quad in range(width // QUAD):
            for kind in range(3):
                first = kind * width + quad * QUAD
                grad_attend[half * 16 : half * 16 + 16, first : first + QUAD] = attend_ref[
                    quad, half, :, kind * QUAD : (kind + 1) * QUAD
                ]
        grad_expand[half * 16 : half * 16 + 16, 0:width] = middle_ref[half, 0:16]
        grad_expand[half * 16 : half * 16 + 16, width : 2 * width] = middle_ref[half, 16:32]
        grad_reduce[half * 32 : half * 32 + 32] = middle_ref[half, 32:64]
        grad_merge[half * 16 : half * 16 + 16] = middle_ref[half, 64:80]
    grad_embed_ref[...] = tail_ref[0]
    rows = tail_ref[1]
    length = grad_gain_one.shape[0]
    turned = pltpu.roll(rows, lax.rem(width - owner * length, width), 1)
    for index, ref in enumerate((grad_gain_one, grad_shift_one, grad_gain_two, grad_shift_two)):
        ref[...] = turned[index : index + 1, 0:length].reshape(length)
    length = grad_readout.shape[0]
    first = owner * length
    turned = pltpu.roll(rows, lax.rem(2 * width - first, width), 1)
    row = jnp.where(first < width, turned[4:5, 0:length], turned[5:6, 0:length])
    grad_readout[...] = row.reshape(length)


def sds(shape, dtype):
    return jax.ShapeDtypeStruct(shape, dtype)


SMEM_SPEC = pl.BlockSpec(memory_space=pltpu.SMEM)
VMEM_SPEC = pl.BlockSpec(memory_space=pltpu.VMEM)
ANY_SPEC = pl.BlockSpec(memory_space=pl.ANY)


def layer_keep(tiles, feat, width, spread):
    rows = (HOP_PAIRS, GROUPS, 2 * GROUP)
    return [
        pltpu.VMEM((tiles, *rows, feat), BF16),
        pltpu.VMEM((tiles, TOKENS, width), F32),
        pltpu.VMEM((tiles, TOKENS, width), BF16),
        pltpu.VMEM((tiles, *rows, 3 * width), BF16),
        pltpu.VMEM((tiles, *rows, width), BF16),
        pltpu.VMEM((STREAMS, *rows, QUAD), BF16),
        pltpu.VMEM((width, width), F32),
        pltpu.VMEM((width, spread), F32),
        pltpu.VMEM((spread, width), F32),
        pltpu.VMEM((tiles, HOP_PAIRS, GROUPS, 2, GROUP, feat), F32),
    ]


def layer_part(
    lines, counts, adjacency, features, cotangent, embed, vectors, attend, merge, expand, reducer
):
    nodes, feat = features.shape
    owners = lines * PLANE
    width, spread = expand.shape[0] * owners, expand.shape[1]
    tiles = nodes // NODES_PER_TILE
    rest = (80, width)
    wide = (width // owners // 2, 3 * QUAD)
    copies = lines + PLANE - 2 + (lines - 1) * (PLANE - 1)

    def slots(shard):
        return pltpu.VMEM((owners, 2, shard.shape[0] // 2, shard.shape[1]), BF16)

    def buffers(shape):
        return [
            pltpu.VMEM((owners, 2) + shape, BF16),
            pltpu.VMEM((owners,) + shape, BF16),
            pltpu.VMEM((lines, PLANE) + shape, BF16),
            pltpu.VMEM((PLANE - 1, lines) + shape, BF16),
            pltpu.VMEM((lines,) + shape, BF16),
            pltpu.VMEM((lines - 1,) + shape, BF16),
            pltpu.VMEM((2,) + shape, F32),
        ]

    outs = [
        cotangent.shape,
        features.shape,
        (2,) + rest,
        (width // QUAD, 2) + wide,
        (2, 8, width),
    ]
    return pl.pallas_call(
        functools.partial(layer_kernel, lines),
        in_specs=[SMEM_SPEC] + [VMEM_SPEC] * 13,
        out_specs=[VMEM_SPEC] * 5,
        out_shape=[sds(shape, F32) for shape in outs],
        scratch_shapes=layer_keep(tiles, feat, width, spread)
        + [
            pltpu.VMEM((feat, width), BF16),
            pltpu.VMEM((8, width), F32),
            pltpu.VMEM((8, 128), F32),
            pltpu.VMEM((owners, 16, width // 2 + 128), BF16),
        ]
        + [slots(shard) for shard in (attend, merge, expand, reducer)]
        + [pltpu.VMEM((feat, width), F32), pltpu.VMEM((8, width), F32)]
        + buffers(rest)
        + buffers(wide) * 2
        + [
            pltpu.VMEM((PLANE, lines + 1, 8, width), F32),
            pltpu.VMEM((PLANE - 1, lines + 1, 8, width), F32),
            pltpu.VMEM((lines, 2, 8, width), F32),
            pltpu.VMEM((lines - 1, 2, 8, width), F32),
            pltpu.VMEM((2, 8, width), F32),
            pltpu.VMEM((2, 8, width), F32),
        ]
        + [
            pltpu.SemaphoreType.DMA((5, copies)),
            pltpu.SemaphoreType.DMA((5, owners)),
            pltpu.SemaphoreType.DMA((5, 2)),
            pltpu.SemaphoreType.DMA((4, 2, PLANE + lines)),
        ],
        compiler_params=pltpu.CompilerParams(
            vmem_limit_bytes=VMEM_GRANT, collective_id=0, has_side_effects=True
        ),
        name="layer",
    )(counts, adjacency, features, cotangent, embed, *vectors, attend, merge, expand, reducer)


def layer_alone_part(
    counts, adjacency, features, cotangent, rows, embed, attend, merge, expand, reducer
):
    nodes, feat = features.shape
    width, spread = expand.shape
    tiles = nodes // NODES_PER_TILE
    wide = (PACK, 2, width // PACK // 2, 3 * QUAD)
    return pl.pallas_call(
        layer_alone_kernel,
        in_specs=[SMEM_SPEC] + [VMEM_SPEC] * 9,
        out_specs=[VMEM_SPEC] * 7,
        out_shape=[
            sds(cotangent.shape, F32),
            sds(features.shape, F32),
            sds((PACK, 2, 80, width), BF16),
            sds(wide, BF16),
            sds(wide, BF16),
            sds((feat, width), F32),
            sds((8, width), F32),
        ],
        scratch_shapes=layer_keep(tiles, feat, width, spread),
        compiler_params=pltpu.CompilerParams(vmem_limit_bytes=VMEM_GRANT),
        name="layer_alone",
    )(counts, adjacency, features, cotangent, rows, embed, attend, merge, expand, reducer)


def unpack_part(middle, attend, tail, features, nodes, shapes):
    return pl.pallas_call(
        unpack_kernel,
        out_shape=[sds(shape, F32) for shape in [nodes.shape, features.shape] + shapes],
        compiler_params=pltpu.CompilerParams(vmem_limit_bytes=VMEM_GRANT),
        name="unpack_shares",
    )(middle, attend, tail, features, nodes)


def gather(block):
    return lax.all_gather(block, "fsdp", axis=0, tiled=True)


def share(term):
    part = lax.psum_scatter(term.astype(BF16), "fsdp", scatter_dimension=0, tiled=True)
    return lax.psum(part.astype(F32), "grp")


def body(
    features,
    adjacency,
    counts,
    input_weight,
    first_gain,
    first_shift,
    attend_weight,
    merge_weight,
    second_gain,
    second_shift,
    expand_weight,
    reduce_weight,
    readout_weight,
    cotangent,
):
    vectors = (first_gain, first_shift, second_gain, second_shift, readout_weight)
    owners = lax.axis_size("fsdp")
    if owners % PLANE == 0 and input_weight.shape[0] == 8 and attend_weight.shape[0] == 32:
        lines = owners // PLANE
        tiles = cotangent.shape[0] // NODES_PER_TILE
        output, grad_features, *shares = layer_part(
            lines,
            counts,
            adjacency,
            features,
            cotangent.reshape(tiles, NODES_PER_TILE, cotangent.shape[1]),
            input_weight,
            vectors,
            attend_weight,
            merge_weight,
            expand_weight,
            reduce_weight,
        )
        shapes = [
            weight.shape
            for weight in (
                input_weight,
                first_gain,
                first_shift,
                attend_weight,
                merge_weight,
                second_gain,
                second_shift,
                expand_weight,
                reduce_weight,
                readout_weight,
            )
        ]
        return tuple(
            unpack_part(*shares, grad_features, output.reshape(cotangent.shape), shapes)
        )
    return body_apart(
        features,
        adjacency,
        counts,
        input_weight,
        vectors,
        attend_weight,
        merge_weight,
        expand_weight,
        reduce_weight,
        cotangent,
    )


def body_apart(
    features,
    adjacency,
    counts,
    input_weight,
    vectors,
    attend_weight,
    merge_weight,
    expand_weight,
    reduce_weight,
    cotangent,
):
    lengths = [v.shape[0] for v in vectors]
    places = [sum(lengths[:i]) for i in range(len(lengths) + 1)]
    packed = lax.all_gather(jnp.concatenate(vectors), "fsdp", axis=0, tiled=False)
    width = merge_weight.shape[1]
    full = [
        packed[:, places[i] : places[i + 1]].astype(F32).reshape(-1, width)
        for i in range(len(lengths))
    ]
    rows = jnp.concatenate(full + [jnp.zeros((2, width), F32)], axis=0)
    embed, attend, merge, expand, reducer = map(
        gather, (input_weight, attend_weight, merge_weight, expand_weight, reduce_weight)
    )
    tiles = cotangent.shape[0] // NODES_PER_TILE
    output, grad_features, terms, early, late, grad_embed, rows_grad = layer_alone_part(
        counts,
        adjacency,
        features,
        cotangent.reshape(tiles, NODES_PER_TILE, width),
        rows,
        embed,
        attend,
        merge,
        expand,
        reducer,
    )
    grad_attend = jnp.stack([early.reshape(width, 3, QUAD), late.reshape(width, 3, QUAD)], axis=2)
    grad_attend = grad_attend.reshape(width, 3 * width)
    spread = expand.shape[1]
    grad_expand = jnp.concatenate([terms[:, :, 0:16], terms[:, :, 16:32]], axis=-1)
    parts = lax.axis_size("fsdp")
    pieces = [rows_grad[i] for i in range(4)] + [rows_grad[4:6]]
    packed_grad = jnp.concatenate([piece.reshape(parts, -1) for piece in pieces], axis=1)
    packed_grad = lax.psum(
        lax.psum_scatter(packed_grad, "fsdp", scatter_dimension=0, tiled=True), "grp"
    ).reshape(-1)
    small = [packed_grad[places[i] : places[i + 1]] for i in range(len(lengths))]
    return (
        output.reshape(cotangent.shape),
        grad_features,
        share(grad_embed),
        small[0],
        small[1],
        share(grad_attend),
        share(terms[:, :, 64:80].reshape(width, width)),
        small[2],
        small[3],
        share(grad_expand.reshape(width, spread)),
        share(terms[:, :, 32:64].reshape(spread, width)),
        small[4],
    )


def solution(mesh):
    nodes = ("grp", "fsdp")
    rows = P("fsdp", None)
    vector = P("fsdp")
    in_specs = (
        P(nodes, None),
        P(nodes, None, None),
        P(nodes),
        rows,
        vector,
        vector,
        rows,
        rows,
        vector,
        vector,
        rows,
        rows,
        vector,
        P(nodes, None),
    )
    out_specs = (
        P(nodes, None),
        P(nodes, None),
        rows,
        vector,
        vector,
        rows,
        rows,
        vector,
        vector,
        rows,
        rows,
        vector,
    )
    return jax.shard_map(body, mesh=mesh, in_specs=in_specs, out_specs=out_specs, check_vma=False)
```

```python
import functools

import jax
import jax.numpy as jnp
from jax import lax
from jax.experimental import pallas as pl
from jax.experimental.pallas import tpu as pltpu
from jax.sharding import PartitionSpec as P

HEADS = 8
HEAD = 64
HOPS = 7
HOP_TOKENS = HOPS + 1
NODES_PER_TILE = 64
TOKENS = NODES_PER_TILE * HOP_TOKENS
GROUP = 8
STREAMS = 2
FEEDS = 1
SKEW = 1
GROUPS = NODES_PER_TILE // GROUP
HOP_PAIRS = HOP_TOKENS // 2
QUAD = 4 * HEAD
MIB = 1 << 20
VMEM_GRANT = 62 * MIB
F32 = jnp.float32
BF16 = jnp.bfloat16
GELU_A = 0.7978845608028654
GELU_B = 0.044715
PLANE = 4
PACK = 16
MESH = pl.DeviceIdType.MESH


def dot(left, right):
    return jnp.dot(left, right, preferred_element_type=F32)


def dot_lead(left, right):
    return lax.dot_general(left, right, (((0,), (0,)), ((), ())), preferred_element_type=F32)


def dot_last(left, right):
    return lax.dot_general(left, right, (((1,), (1,)), ((), ())), preferred_element_type=F32)


def link_of(adjacency, count):
    slots = adjacency.shape[0]
    rows = lax.broadcasted_iota(jnp.int32, (slots, slots), 0)
    cols = lax.broadcasted_iota(jnp.int32, (slots, slots), 1)
    live = jnp.logical_and(rows < count, cols < count)
    link = jnp.where(live, adjacency, 0) + jnp.where(rows == cols, 1, 0)
    link = link.astype(F32)
    root = lax.rsqrt(jnp.sum(link, axis=-1, keepdims=True))
    return link.astype(BF16), root


def hop(link, root, state):
    width = state.shape[1]
    scaled = state * root
    high = scaled.astype(BF16)
    rest = scaled - high.astype(F32)
    middle = rest.astype(BF16)
    low = (rest - middle.astype(F32)).astype(BF16)
    spread = dot(link, jnp.concatenate([high, middle, low], axis=1))
    return (spread[:, :width] + (spread[:, width : 2 * width] + spread[:, 2 * width :])) * root


def live_rows(count, first, rows):
    index = lax.broadcasted_iota(jnp.int32, (rows, 1), 0) + first
    return jnp.where(index < count, 1.0, 0.0).astype(F32)


def norm_stats(values):
    mean = jnp.mean(values, axis=-1, keepdims=True)
    centred = values - mean
    var = jnp.mean(centred * centred, axis=-1, keepdims=True)
    inv = lax.rsqrt(var + 1e-05)
    return centred * inv, inv


def quad_stack(block):
    head = lax.broadcasted_iota(jnp.int32, block.shape, 1) // HEAD
    return jnp.concatenate(
        [jnp.where(head == h, block, jnp.zeros_like(block)) for h in range(4)], axis=0
    )


def grad_softmax(probs, grad_probs):
    tokens, columns = probs.shape
    weighted = (probs * grad_probs).reshape(HOP_TOKENS, GROUP, columns)
    total = jnp.sum(weighted, axis=0)
    shaped = probs.reshape(HOP_TOKENS, GROUP, columns)
    return (weighted - shaped * total[None]).reshape(tokens, columns).astype(BF16)


def quad_probs(scores):
    tokens, columns = scores.shape
    scores = scores.reshape(HOP_TOKENS, GROUP, columns)
    top = jnp.max(scores, axis=0)
    power = jnp.exp((scores - top[None]) * HEAD ** (-0.5))
    row = lax.broadcasted_iota(jnp.int32, (GROUP, columns), 0)
    col = lax.broadcasted_iota(jnp.int32, (GROUP, columns), 1) % GROUP
    share = jnp.where(row == col, 1.0 / jnp.sum(power, axis=0), 0.0)
    return (power * share[None]).reshape(tokens, columns)


def queries_from(weights, block):
    tokens = block.shape[0]
    out = []
    lane = lax.broadcasted_iota(jnp.int32, (tokens, 2 * HEAD), 1)
    for first in (0, 2 * HEAD):
        both = dot_lead(weights[:, first : first + 2 * HEAD], block[:, first : first + 2 * HEAD])
        out.append(jnp.where(lane < HEAD, both[:tokens], both[tokens:]))
    return jnp.concatenate(out, axis=1)


def hop_rows(values, index):
    shaped = values.reshape(HOP_PAIRS, GROUPS, 2, GROUP, values.shape[-1])
    return shaped[index // 2, :, index % 2].reshape(NODES_PER_TILE, values.shape[-1])


def hop_join(parts):
    width = parts[0].shape[-1]
    blocks = []
    for pair in range(HOP_PAIRS):
        both = [parts[2 * pair + k].reshape(GROUPS, 1, GROUP, width) for k in range(2)]
        blocks.append(jnp.concatenate(both, axis=1))
    return jnp.concatenate(blocks, axis=0).reshape(TOKENS, width)


def interleave(streams):
    live = list(enumerate(streams))
    turn = 0
    while live:
        live = [
            (place, stream)
            for place, stream in live
            if turn < place * SKEW or next(stream, live) is not live
        ]
        turn += 1


class Place:
    def __init__(self, lines):
        self.lines = lines
        self.core = lax.axis_index("grp")
        self.owner = lax.axis_index("fsdp")
        self.line = lax.div(self.owner, PLANE)
        self.spot = lax.rem(self.owner, PLANE)

    def line_turn(self, ahead):
        return lax.rem(self.line + ahead + self.lines, self.lines)

    def spot_turn(self, ahead):
        return lax.rem(self.spot + ahead + PLANE, PLANE)

    def line_peer(self, ahead):
        return (self.core, self.line_turn(ahead) * PLANE + self.spot)

    def plane_peer(self, ahead):
        return (self.core, self.line * PLANE + self.spot_turn(ahead))

    def sibling(self):
        return (1 - self.core, self.owner)

    def peers(self):
        return (
            [self.line_peer(d) for d in range(1, self.lines)]
            + [self.plane_peer(e) for e in range(1, PLANE)]
            + [self.sibling()]
        )

    def greet(self):
        barrier = pltpu.get_barrier_semaphore()
        for peer in self.peers():
            pl.semaphore_signal(barrier, inc=1, device_id=peer, device_id_type=MESH)

    def greeted(self):
        pl.semaphore_wait(pltpu.get_barrier_semaphore(), self.lines + PLANE - 1)


def remote(source, target, send, recv, device):
    return pltpu.make_async_remote_copy(
        src_ref=source,
        dst_ref=target,
        send_sem=send,
        recv_sem=recv,
        device_id=device,
        device_id_type=MESH,
    )


class Gather:
    def __init__(self, place, slots, send, recv, pair, halves):
        self.place, self.slots = place, slots
        self.send, self.recv, self.pair_sems, self.halves = send, recv, pair, halves

    def slot(self, owner):
        return self.slots.at[owner, self.place.core] if self.halves else self.slots.at[owner]

    def own_copies(self):
        place = self.place
        peers = [place.line_peer(d) for d in range(1, place.lines)]
        peers += [place.plane_peer(e) for e in range(1, PLANE)]
        own = self.slot(place.owner)
        return [
            remote(own, own, self.send.at[i], self.recv.at[place.owner], peer)
            for i, peer in enumerate(peers)
        ]

    def onward(self, d):
        place = self.place
        owner = place.line_turn(-d) * PLANE + place.spot
        first = place.lines + PLANE - 2 + (d - 1) * (PLANE - 1)
        return [
            remote(
                self.slot(owner),
                self.slot(owner),
                self.send.at[first + e - 1],
                self.recv.at[owner],
                place.plane_peer(e),
            )
            for e in range(1, PLANE)
        ]

    def start_line(self):
        for copy in self.own_copies()[: self.place.lines - 1]:
            copy.start()

    def start_plane(self):
        for copy in self.own_copies()[self.place.lines - 1 :]:
            copy.start()

    def start(self):
        self.start_line()
        self.start_plane()

    def forward(self):
        for d in range(1, self.place.lines):
            copies = self.onward(d)
            copies[0].wait_recv()
            for copy in copies:
                copy.start()

    def finish(self):
        place = self.place
        for d in range(place.lines):
            for e in range(1, PLANE):
                owner = place.line_turn(d) * PLANE + place.spot_turn(-e)
                remote(
                    self.slot(owner),
                    self.slot(owner),
                    self.send.at[0],
                    self.recv.at[owner],
                    place.plane_peer(e),
                ).wait_recv()
        for copy in self.own_copies():
            copy.wait_send()
        for d in range(1, place.lines):
            for copy in self.onward(d):
                copy.wait_send()

    def pair(self):
        half = self.slots.at[:, self.place.core]
        return remote(half, half, self.pair_sems.at[0], self.pair_sems.at[1], self.place.sibling())


class Scatter:
    def __init__(self, place, terms, got, chip, plane_got, line_out, line_got, result, sems):
        self.place, self.terms, self.got, self.chip = place, terms, got, chip
        self.plane_got, self.line_out, self.line_got = plane_got, line_out, line_got
        self.result, self.sems = result, sems

    def pair(self):
        place = self.place
        return remote(
            self.terms.at[:, 1 - place.core],
            self.got,
            self.sems.at[0, 0],
            self.sems.at[1, 0],
            place.sibling(),
        )

    def plane(self):
        place = self.place
        return [
            remote(
                self.chip.at[:, place.spot_turn(e)],
                self.plane_got.at[e - 1],
                self.sems.at[0, e],
                self.sems.at[1, e],
                place.plane_peer(e),
            )
            for e in range(1, PLANE)
        ]

    def line(self):
        place = self.place
        return [
            remote(
                self.line_out.at[place.line_turn(d)],
                self.line_got.at[d - 1],
                self.sems.at[0, PLANE + d - 1],
                self.sems.at[1, PLANE + d - 1],
                place.line_peer(d),
            )
            for d in range(1, place.lines)
        ]

    def last(self):
        place = self.place
        half = self.result.at[place.core]
        k = PLANE + place.lines - 1
        return remote(half, half, self.sems.at[0, k], self.sems.at[1, k], place.sibling())

    def begin(self):
        self.pair().start()

    def to_plane(self):
        place = self.place
        self.pair().wait()

        def add(line, carry):
            for spot in range(PLANE):
                owner = line * PLANE + spot
                self.chip[line, spot] = self.terms[owner, place.core] + self.got[owner]
            return carry

        lax.fori_loop(0, place.lines, add, 0)
        for copy in self.plane():
            copy.start()

    def to_line(self):
        place = self.place
        for copy in self.plane():
            copy.wait()

        def add(line, carry):
            total = self.chip[line, place.spot].astype(F32)
            for e in range(PLANE - 1):
                total = total + self.plane_got[e, line].astype(F32)
            self.line_out[line] = total.astype(BF16)
            return carry

        lax.fori_loop(0, place.lines, add, 0)
        for copy in self.line():
            copy.start()

    def to_sibling(self):
        place = self.place
        for copy in self.line():
            copy.wait()
        total = self.line_out[place.line].astype(F32)
        for d in range(place.lines - 1):
            total = total + self.line_got[d].astype(F32)
        self.result[place.core] = total
        self.last().start()

    def end(self):
        self.last().wait()


class TailScatter:
    def __init__(self, place, own, plane_got, line_out, line_got, mine, other, sems):
        self.place, self.own, self.plane_got, self.line_out = place, own, plane_got, line_out
        self.line_got, self.mine, self.other, self.sems = line_got, mine, other, sems

    def plane(self):
        place = self.place
        return [
            remote(
                self.own.at[place.spot_turn(e)],
                self.plane_got.at[e - 1],
                self.sems.at[0, e],
                self.sems.at[1, e],
                place.plane_peer(e),
            )
            for e in range(1, PLANE)
        ]

    def line(self):
        place = self.place
        return [
            remote(
                self.line_out.at[place.line_turn(d)],
                self.line_got.at[d - 1],
                self.sems.at[0, PLANE + d - 1],
                self.sems.at[1, PLANE + d - 1],
                place.line_peer(d),
            )
            for d in range(1, place.lines)
        ]

    def last(self):
        return remote(
            self.mine, self.other, self.sems.at[0, 0], self.sems.at[1, 0], self.place.sibling()
        )

    def begin(self):
        for copy in self.plane():
            copy.start()

    def to_line(self):
        place = self.place
        for copy in self.plane():
            copy.wait()
        total = self.own[place.spot]
        for e in range(PLANE - 1):
            total = total + self.plane_got[e]
        for line in range(place.lines):
            self.line_out[line, 0] = total[line]
            self.line_out[line, 1] = total[place.lines]
        for copy in self.line():
            copy.start()

    def to_sibling(self):
        place = self.place
        for copy in self.line():
            copy.wait()
        total = self.line_out[place.line]
        for d in range(place.lines - 1):
            total = total + self.line_got[d]
        self.mine[...] = total
        self.last().start()

    def end(self):
        self.last().wait()
        return self.mine[...] + self.other[...]


def hop_states(counts_ref, adjacency_ref, features_ref, stacked_ref):
    clusters, slots = adjacency_ref.shape[:2]
    per_cluster = slots // NODES_PER_TILE
    links = []
    states = []
    for cluster in range(clusters):
        count = counts_ref[cluster]
        links.append(link_of(adjacency_ref[cluster], count))
        states.append(
            features_ref[cluster * slots : (cluster + 1) * slots].astype(F32)
            * live_rows(count, 0, slots)
        )
    earlier = [None] * clusters
    for index in range(HOP_TOKENS):
        for cluster in range(clusters):
            if index > 0:
                states[cluster] = hop(*links[cluster], states[cluster])
            if index % 2 == 0:
                earlier[cluster] = states[cluster]
                continue
            for part in range(per_cluster):
                rows = slice(part * NODES_PER_TILE, (part + 1) * NODES_PER_TILE)
                both = [
                    state[rows].reshape(GROUPS, GROUP, state.shape[-1])
                    for state in (earlier[cluster], states[cluster])
                ]
                stacked_ref[cluster * per_cluster + part, index // 2] = jnp.concatenate(
                    both, axis=1
                ).astype(BF16)


def spread_vectors(small, owners, width):
    rows = small.shape[0]
    lane = lax.broadcasted_iota(jnp.int32, (128, width), 0)
    column = lax.broadcasted_iota(jnp.int32, (128, width), 1)
    row = lax.broadcasted_iota(jnp.int32, (rows, width), 0)
    place = lax.broadcasted_iota(jnp.int32, (rows, width), 1)
    piece = width // owners
    pieces = dot(small, jnp.where(lane == column % piece, 1.0, 0.0).astype(BF16))
    out = []
    for vector in range(4):
        mine = jnp.logical_and(row % 8 == vector, lax.div(row, 8) == lax.div(place, piece))
        out.append(jnp.sum(jnp.where(mine, pieces, 0.0), axis=0, keepdims=True))
    pieces = dot(small, jnp.where(lane == column % (2 * piece), 1.0, 0.0).astype(BF16))
    for first in (0, owners // 2):
        owner = lax.div(place, 2 * piece) + first
        mine = jnp.logical_and(row % 8 == 4, lax.div(row, 8) == owner)
        out.append(jnp.sum(jnp.where(mine, pieces, 0.0), axis=0, keepdims=True))
    return jnp.concatenate(out + [jnp.zeros((2, width), F32)], axis=0)


def hop_back(counts_ref, adjacency_ref, grad_stacked_ref, grad_features_ref, between):
    clusters, slots = adjacency_ref.shape[:2]
    per_cluster = slots // NODES_PER_TILE
    links = []
    states = []

    def hop_grad(cluster, index):
        return jnp.concatenate(
            [
                grad_stacked_ref[cluster * per_cluster + p, index // 2, :, index % 2].reshape(
                    NODES_PER_TILE, grad_stacked_ref.shape[-1]
                )
                for p in range(per_cluster)
            ],
            axis=0,
        )

    for cluster in range(clusters):
        links.append(link_of(adjacency_ref[cluster], counts_ref[cluster]))
        states.append(hop_grad(cluster, HOPS))
    for index in range(HOPS - 1, -1, -1):
        for cluster in range(clusters):
            states[cluster] = hop_grad(cluster, index) + hop(*links[cluster], states[cluster])
        if index in between:
            between[index]()
    for cluster in range(clusters):
        grad_features_ref[cluster * slots : (cluster + 1) * slots] = states[cluster] * live_rows(
            counts_ref[cluster], 0, slots
        )


def block_of(ref, tile, group, first):
    return ref[tile, :, group, :, first : first + QUAD].reshape(GROUP * HOP_TOKENS, QUAD)


def put_block(ref, tile, group, first, block):
    ref[tile, :, group, :, first : first + QUAD] = block.astype(BF16).reshape(
        HOP_PAIRS, 2 * GROUP, QUAD
    )


def tokens_of(ref, tile):
    return ref[tile].reshape(TOKENS, ref.shape[-1])


def embed_tile(tile, stacked_ref, embed, gain, shift, second_ref, normed_ref):
    hidden = dot(tokens_of(stacked_ref, tile), embed)
    second_ref[tile] = hidden
    normal, _ = norm_stats(hidden)
    normed_ref[tile] = (normal * gain + shift).astype(BF16)


def project_step(first_tile, kind, normed_ref, weight, triple_ref):
    width = normed_ref.shape[-1]
    tiles = pl.ds(first_tile, STREAMS)
    normed = normed_ref[tiles].reshape(STREAMS * TOKENS, width)
    triple_ref[tiles, :, :, :, kind * width : (kind + 1) * width] = (
        dot(normed, weight).astype(BF16).reshape(STREAMS, *triple_ref.shape[1:-1], width)
    )


def attend_tile(tile, normed_ref, value_weight, triple_ref, mixed_ref):
    width = normed_ref.shape[-1]
    triple_ref[tile, :, :, :, 2 * width :] = (
        dot(normed_ref[tile], value_weight).astype(BF16).reshape(*triple_ref.shape[1:-1], width)
    )
    places = [(tile, g, first) for g in range(GROUPS) for first in range(0, width, QUAD)]
    keys = [block_of(triple_ref, t, g, width + first) for t, g, first in places]
    queries = [quad_stack(block_of(triple_ref, *place)) for place in places]
    scores = [dot_last(k, q) for k, q in zip(keys, queries)]
    probs = [quad_probs(score).astype(BF16) for score in scores]
    values = [block_of(triple_ref, t, g, 2 * width + first) for t, g, first in places]
    blocks = [queries_from(p, v) for p, v in zip(probs, values)]
    for place, block in zip(places, blocks):
        put_block(mixed_ref, *place, block)


def middle_step(
    first_tile,
    counts_ref,
    second_ref,
    mixed_ref,
    cotangent_ref,
    rows_ref,
    expand,
    reducer,
    output_ref,
    rows_grad_ref,
    grad_merge_ref,
    grad_expand_ref,
    grad_reduce_ref,
):
    width = second_ref.shape[-1]
    gain, shift = rows_ref[2:3], rows_ref[3:4]
    row_node, row_hop = rows_ref[4:5], rows_ref[5:6]

    def stream(part):
        tile = first_tile + part
        second = second_ref[tile]
        normal, inv = norm_stats(second)
        inner = (normal * gain + shift).astype(BF16)
        yield
        before = dot(inner, expand)
        yield
        square = before * before
        gate = 1.0 / (1.0 + jnp.exp(before * (square * (-2.0 * GELU_A * GELU_B) - 2.0 * GELU_A)))
        gated = before * gate
        after = gated.astype(BF16)
        slope = gate + (gated - gated * gate) * (
            square * (6.0 * GELU_A * GELU_B) + 2.0 * GELU_A
        )
        yield
        third = second + dot(after, reducer)
        yield
        shaped = [hop_rows(third, k) for k in range(HOP_TOKENS)]
        node = tile * NODES_PER_TILE
        keep = live_rows(counts_ref[lax.div(node, 128)], lax.rem(node, 128), NODES_PER_TILE)
        centre = shaped[0]
        base = jnp.sum(centre * row_node, axis=-1, keepdims=True)
        logits = [
            base + jnp.sum(shaped[k] * row_hop, axis=-1, keepdims=True)
            for k in range(1, HOP_TOKENS)
        ]
        top = functools.reduce(jnp.maximum, logits)
        powers = [jnp.exp(logit - top) for logit in logits]
        scale = 1.0 / functools.reduce(jnp.add, powers)
        shares = [power * scale for power in powers]
        total = centre
        for k in range(1, HOP_TOKENS):
            total = total + shares[k - 1] * shaped[k]
        output_ref[tile] = total * keep
        cotangent = cotangent_ref[tile] * keep
        grad_shares = [
            jnp.sum(cotangent * shaped[k], axis=-1, keepdims=True) for k in range(1, HOP_TOKENS)
        ]
        mean_share = functools.reduce(jnp.add, [s * g for s, g in zip(shares, grad_shares)])
        grad_logits = [s * (g - mean_share) for s, g in zip(shares, grad_shares)]
        grad_base = functools.reduce(jnp.add, grad_logits)
        parts = [cotangent + grad_base * row_node]
        read_hop = jnp.zeros((NODES_PER_TILE, width), F32)
        for k in range(1, HOP_TOKENS):
            parts.append(shares[k - 1] * cotangent + grad_logits[k - 1] * row_hop)
            read_hop = read_hop + grad_logits[k - 1] * shaped[k]
        rows_grad_ref[4:5] += jnp.sum(grad_base * centre, axis=0, keepdims=True)
        rows_grad_ref[5:6] += jnp.sum(read_hop, axis=0, keepdims=True)
        grad_third = hop_join(parts)
        grad_branch = grad_third.astype(BF16)
        yield
        grad_after = dot_last(grad_branch, reducer)
        grad_reduce_ref[...] += dot_lead(after, grad_branch)
        yield
        grad_before = (slope * grad_after).astype(BF16)
        yield
        grad_inner = dot_last(grad_before, expand)
        grad_expand_ref[...] += dot_lead(inner, grad_before)
        yield
        rows_grad_ref[2:3] += jnp.sum(grad_inner * normal, axis=0, keepdims=True)
        rows_grad_ref[3:4] += jnp.sum(grad_inner, axis=0, keepdims=True)
        grad_normal = grad_inner * gain
        grad_second = grad_third + inv * (
            grad_normal
            - jnp.mean(grad_normal, axis=-1, keepdims=True)
            - normal * jnp.mean(grad_normal * normal, axis=-1, keepdims=True)
        )
        second_ref[tile] = grad_second
        yield
        grad_merge_ref[...] += dot_lead(tokens_of(mixed_ref, tile), grad_second.astype(BF16))

    interleave([stream(part) for part in range(FEEDS)])


def pack_terms(terms_ref, grad_merge_ref, grad_expand_ref, grad_reduce_ref):
    width, spread = grad_expand_ref.shape
    wide = grad_expand_ref[...].astype(BF16).reshape(PACK, 2, width // PACK // 2, spread)
    deep = grad_reduce_ref[...].astype(BF16).reshape(PACK, 2, spread // PACK // 2, width)
    square = grad_merge_ref[...].astype(BF16).reshape(PACK, 2, width // PACK // 2, width)
    terms_ref[:, :, 0:16] = wide[..., :width]
    terms_ref[:, :, 16:32] = wide[..., width:]
    terms_ref[:, :, 32:64] = deep
    terms_ref[:, :, 64:80] = square


def attend_back_step(quad, first_tile, triple_ref, second_ref, normed_ref, merge, grad_mixed_ref, grad_attend_ref):
    width = normed_ref.shape[-1]
    for part in range(STREAMS):
        grad_mixed = dot_last(second_ref[first_tile + part].astype(BF16), merge).astype(BF16)
        grad_mixed_ref[part] = grad_mixed.reshape(grad_mixed_ref.shape[1:])
    places = [(part, group) for part in range(STREAMS) for group in range(GROUPS)]
    scale = HEAD ** (-0.5)
    starts = [kind * width + quad * QUAD for kind in range(3)]

    def read(kind):
        return [block_of(triple_ref, first_tile + p, g, starts[kind]) for p, g in places]

    keys = read(1)
    queries = [quad_stack(block) for block in read(0)]
    scores = [dot_last(k, q) for k, q in zip(keys, queries)]
    values = read(2)
    out_grads = [quad_stack(block_of(grad_mixed_ref, p, g, 0)) for p, g in places]
    grad_probs = [dot_last(v, o) for v, o in zip(values, out_grads)]
    probs = [quad_probs(score) for score in scores]
    grad_scores = [grad_softmax(p, g) for p, g in zip(probs, grad_probs)]
    grad_values = [dot(p.astype(BF16), o) for p, o in zip(probs, out_grads)]
    grad_keys = [dot(s, q) for s, q in zip(grad_scores, queries)]
    grad_queries = [queries_from(s, k) for s, k in zip(grad_scores, keys)]
    for (part, group), a, b, c in zip(places, grad_queries, grad_keys, grad_values):
        for start, block in zip(starts, (a * scale, b * scale, c)):
            put_block(triple_ref, first_tile + part, group, start, block)
    tiles = pl.ds(first_tile, STREAMS)
    grads = jnp.concatenate(
        [
            triple_ref[tiles, :, :, :, start : start + QUAD].reshape(STREAMS * TOKENS, QUAD)
            for start in starts
        ],
        axis=1,
    )
    grad_attend_ref[:, 0 : 3 * QUAD] += dot_lead(
        normed_ref[tiles].reshape(STREAMS * TOKENS, width), grads
    )


def embed_back_step(
    first_tile,
    stacked_ref,
    second_ref,
    triple_ref,
    attend,
    embed,
    gain,
    rows_keep,
    grad_embed_ref,
    normed_ref,
):
    def stream(part):
        tile = first_tile + part
        stacked = tokens_of(stacked_ref, tile)
        grad_normed = dot_last(tokens_of(triple_ref, tile), attend)
        hidden = dot(stacked, embed)
        yield
        normal, inv = norm_stats(hidden)
        rows_keep[0:1] += jnp.sum(grad_normed * normal, axis=0, keepdims=True)
        rows_keep[1:2] += jnp.sum(grad_normed, axis=0, keepdims=True)
        grad_normal = grad_normed * gain
        grad_hidden = second_ref[tile] + inv * (
            grad_normal
            - jnp.mean(grad_normal, axis=-1, keepdims=True)
            - normal * jnp.mean(grad_normal * normal, axis=-1, keepdims=True)
        )
        grad_hidden = grad_hidden.astype(BF16)
        yield
        grad_embed_ref[...] += dot_lead(stacked, grad_hidden)
        normed_ref[tile] = grad_hidden

    interleave([stream(part) for part in range(STREAMS)])


class Silent:
    def __getattr__(self, name):
        return lambda *arguments: None


def loop(count, step):
    def body(index, carry):
        step(index)
        return carry

    lax.fori_loop(0, count, body, 0)


def layer_phases(
    counts_ref,
    adjacency_ref,
    features_ref,
    cotangent_ref,
    rows_ref,
    embed_ref,
    query_ref,
    key_ref,
    value_ref,
    merge_ref,
    expand_ref,
    reduce_ref,
    output_ref,
    grad_features_ref,
    terms_ref,
    early_terms,
    late_terms,
    grad_embed_ref,
    rows_keep,
    keep,
    transfers,
):
    (
        stacked_ref,
        second_ref,
        normed_ref,
        triple_ref,
        mixed_ref,
        grad_mixed_ref,
        grad_merge_ref,
        grad_expand_ref,
        grad_reduce_ref,
        grad_stacked_ref,
    ) = keep
    tiles, _, width = second_ref.shape
    pairs = tiles // STREAMS
    hop_states(counts_ref, adjacency_ref, features_ref, stacked_ref)
    transfers.head()

    def embed_step(tile):
        embed_tile(
            tile, stacked_ref, embed_ref[...], rows_ref[0:1], rows_ref[1:2], second_ref, normed_ref
        )
        transfers.beside_embed(tile, tiles)

    loop(tiles, embed_step)
    for kind, weight_ref in enumerate((query_ref, key_ref)):
        transfers.before_projection(kind)

        def project(pair, kind=kind, weight_ref=weight_ref):
            weight = weight_ref[...].reshape(width, width)
            project_step(pair * STREAMS, kind, normed_ref, weight, triple_ref)
            transfers.beside_projection(kind, pair)

        loop(pairs, project)
    transfers.before_projection(2)

    def attend_step(tile):
        attend_tile(tile, normed_ref, value_ref[...].reshape(width, width), triple_ref, mixed_ref)
        transfers.beside_attention(tile, tiles)

    loop(tiles, attend_step)
    transfers.before_merge()

    def merge_step(pair):
        mixed = mixed_ref[pl.ds(pair * STREAMS, STREAMS)].reshape(STREAMS * TOKENS, width)
        second_ref[pl.ds(pair * STREAMS, STREAMS)] += dot(
            mixed, merge_ref[...].reshape(width, width)
        ).reshape(STREAMS, TOKENS, width)

    loop(pairs, merge_step)
    transfers.before_middle()
    for ref in (rows_keep, grad_merge_ref, grad_expand_ref, grad_reduce_ref, grad_embed_ref):
        ref[...] = jnp.zeros_like(ref)
    spread = grad_expand_ref.shape[1]

    def feed_step(pair):
        middle_step(
            pair * FEEDS,
            counts_ref,
            second_ref,
            mixed_ref,
            cotangent_ref,
            rows_ref,
            expand_ref[...].reshape(width, spread),
            reduce_ref[...].reshape(spread, width),
            output_ref,
            rows_keep,
            grad_merge_ref,
            grad_expand_ref,
            grad_reduce_ref,
        )

    loop(tiles // FEEDS, feed_step)
    pack_terms(terms_ref, grad_merge_ref, grad_expand_ref, grad_reduce_ref)
    transfers.after_middle()
    grad_attend_ref = grad_expand_ref
    for quad, terms in enumerate((early_terms, late_terms)):
        grad_attend_ref[...] = jnp.zeros_like(grad_attend_ref)

        def back_step(pair, quad=quad):
            attend_back_step(
                quad,
                pair * STREAMS,
                triple_ref,
                second_ref,
                normed_ref,
                merge_ref[...].reshape(width, width)[quad * QUAD : (quad + 1) * QUAD],
                grad_mixed_ref,
                grad_attend_ref,
            )
            transfers.beside_backward(quad, pair, pairs)

        loop(pairs, back_step)
        terms[...] = grad_attend_ref[:, 0 : 3 * QUAD].astype(BF16).reshape(terms.shape)
        transfers.after_backward(quad)

    def embed_back(pair):
        embed_back_step(
            pair * STREAMS,
            stacked_ref,
            second_ref,
            triple_ref,
            jnp.concatenate(
                [ref[...].reshape(width, width) for ref in (query_ref, key_ref, value_ref)], axis=1
            ),
            embed_ref[...],
            rows_ref[0:1],
            rows_keep,
            grad_embed_ref,
            normed_ref,
        )
        transfers.beside_embed_back(pair, pairs)

    loop(pairs, embed_back)
    transfers.after_embed_back()

    def stacked_back(pair):
        grad_hidden = normed_ref[pl.ds(pair * STREAMS, STREAMS)].reshape(STREAMS * TOKENS, width)
        grad_stacked_ref[pl.ds(pair * STREAMS, STREAMS)] = dot_last(
            grad_hidden, embed_ref[...]
        ).reshape(STREAMS, *grad_stacked_ref.shape[1:])

    loop(pairs, stacked_back)
    hop_back(
        counts_ref,
        adjacency_ref,
        grad_stacked_ref,
        grad_features_ref,
        {1: transfers.beside_hops},
    )
    transfers.end()


class Transfers:
    def __init__(self, place, gathers, scatters, unpack_head, pack_tail, publish):
        self.place = place
        self.lead, *self.attend = gathers[:4]
        self.merge, self.expand, self.reducer = gathers[4:]
        self.middle, self.early, self.late, self.tail = scatters
        self.unpack_head, self.pack_tail, self.publish = unpack_head, pack_tail, publish

    def head(self):
        queries, keys, values = self.attend
        self.place.greeted()
        self.lead.start()
        for part in self.attend:
            part.start_line()
        self.lead.forward()
        queries.start_plane()
        queries.forward()
        keys.start_plane()
        self.lead.finish()
        keys.forward()
        self.unpack_head()
        values.start_plane()
        values.forward()
        self.merge.start()
        self.expand.start()

    def beside_embed(self, tile, tiles):
        @pl.when(tile == 2)
        def _():
            self.attend[0].finish()
            self.attend[0].pair().start()

        @pl.when(tile == tiles - 1)
        def _():
            self.merge.forward()

    def before_projection(self, kind):
        self.attend[kind].pair().wait()

    def beside_projection(self, kind, pair):
        @pl.when(pair == 0)
        def _():
            self.attend[kind + 1].finish()
            self.attend[kind + 1].pair().start()
            if kind == 0:
                self.reducer.start()

        @pl.when(pair == 1)
        def _():
            (self.expand, self.reducer)[kind].forward()

    def beside_attention(self, tile, tiles):
        @pl.when(tile == tiles // 2)
        def _():
            self.merge.finish()
            self.merge.pair().start()

        @pl.when(tile == tiles - 2)
        def _():
            self.expand.finish()
            self.expand.pair().start()

    def before_merge(self):
        self.merge.pair().wait()
        self.reducer.finish()
        self.reducer.pair().start()

    def before_middle(self):
        self.expand.pair().wait()
        self.reducer.pair().wait()

    def after_middle(self):
        self.middle.begin()

    def beside_backward(self, quad, pair, pairs):
        if quad == 0:

            @pl.when(pair == 0)
            def _():
                self.middle.to_plane()

        else:

            @pl.when(pair == 0)
            def _():
                self.early.to_plane()

            @pl.when(pair == pairs - 2)
            def _():
                self.middle.to_line()

    def after_backward(self, quad):
        if quad == 0:
            self.early.begin()
        else:
            self.late.begin()
            self.early.to_line()

    def beside_embed_back(self, pair, pairs):
        @pl.when(pair == 0)
        def _():
            self.late.to_plane()

        @pl.when(pair == 1)
        def _():
            self.middle.to_sibling()

    def after_embed_back(self):
        self.pack_tail()
        self.tail.begin()
        self.early.to_sibling()

    def beside_hops(self):
        self.late.to_line()
        self.tail.to_line()

    def end(self):
        self.tail.to_sibling()
        self.middle.end()
        self.early.end()
        self.late.to_sibling()
        tail = self.tail.end()
        self.late.end()
        self.publish(tail)


def layer_kernel(
    lines,
    counts_ref,
    adjacency_ref,
    features_ref,
    cotangent_ref,
    embed_shard,
    vector_a,
    vector_b,
    vector_c,
    vector_d,
    vector_e,
    attend_shard,
    merge_shard,
    expand_shard,
    reduce_shard,
    output_ref,
    grad_features_ref,
    middle_share_ref,
    attend_share_ref,
    tail_share_ref,
    *scratch,
):
    keep = scratch[0:10]
    embed_ref, rows_ref, small_keep, head_slots = scratch[10:14]
    attend_slots = scratch[14:17]
    merge_slots, expand_slots, reduce_slots = scratch[17:20]
    grad_embed_ref, rows_keep = scratch[20:22]
    middle_refs, early_refs, late_refs = scratch[22:29], scratch[29:36], scratch[36:43]
    tail_refs = scratch[43:49]
    send, recv, pair, scatter_sems = scratch[49:53]
    owners = head_slots.shape[0]
    width = embed_ref.shape[-1]
    half_width = width // 2
    place = Place(lines)
    core, owner = place.core, place.owner
    place.greet()

    small_keep[...] = jnp.zeros_like(small_keep)
    for index, vector in enumerate((vector_a, vector_b, vector_c, vector_d, vector_e)):
        length = vector.shape[0]
        small_keep[index : index + 1, 0:length] = vector[...].astype(F32).reshape(1, length)
    mine = embed_shard[...].astype(F32)
    packed = jnp.concatenate(
        [
            jnp.concatenate([mine[:, :half_width], small_keep[...]], axis=1),
            jnp.concatenate([mine[:, half_width:], jnp.zeros((8, 128), F32)], axis=1),
        ],
        axis=0,
    )
    head_slots[owner] = packed.astype(BF16)

    def half_of(shard):
        rows = shard.shape[0] // 2
        return shard[pl.ds(pl.multiple_of(core * rows, rows), rows)]

    whole_attend = half_of(attend_shard)
    for kind, slots in enumerate(attend_slots):
        slots[owner, core] = whole_attend[:, kind * width : (kind + 1) * width]
    matrices = (merge_slots, expand_slots, reduce_slots)
    for slots, shard in zip(matrices, (merge_shard, expand_shard, reduce_shard)):
        slots[owner, core] = half_of(shard)
    gathers = [
        Gather(place, slots, send.at[index], recv.at[index], pair.at[index], index > 0)
        for index, slots in enumerate((head_slots, *attend_slots, *matrices))
    ]
    middle = Scatter(place, *middle_refs, scatter_sems.at[0])
    early = Scatter(place, *early_refs, scatter_sems.at[1])
    late = Scatter(place, *late_refs, scatter_sems.at[2])
    tail = TailScatter(place, *tail_refs, scatter_sems.at[3])

    def unpack_head():
        whole_head = head_slots[...].astype(F32)
        top = whole_head[:, 0:8].reshape(owners * 8, half_width + 128)
        bottom = whole_head[:, 8:16].reshape(owners * 8, half_width + 128)
        embed_ref[:, :half_width] = top[:, :half_width].astype(BF16)
        embed_ref[:, half_width:] = bottom[:, :half_width].astype(BF16)
        rows_ref[...] = spread_vectors(top[:, half_width:].astype(BF16), owners, width)

    def pack_tail():
        own = grad_embed_ref[...].reshape(lines, PLANE, 8, width)
        for spot in range(PLANE):
            tail.own[spot, 0:lines] = own[:, spot]
            tail.own[spot, lines] = rows_keep[...]

    def publish(tail_total):
        middle_share_ref[...] = middle.result[...]
        attend_share_ref[0] = early.result[...]
        attend_share_ref[1] = late.result[...]
        tail_share_ref[...] = tail_total

    transfers = Transfers(
        place, gathers, (middle, early, late, tail), unpack_head, pack_tail, publish
    )
    layer_phases(
        counts_ref,
        adjacency_ref,
        features_ref,
        cotangent_ref,
        rows_ref,
        embed_ref,
        *attend_slots,
        merge_slots,
        expand_slots,
        reduce_slots,
        output_ref,
        grad_features_ref,
        middle.terms,
        early.terms,
        late.terms,
        grad_embed_ref,
        rows_keep,
        keep,
        transfers,
    )


def layer_alone_kernel(*refs):
    layer_phases(*refs[:19], refs[19:], Silent())


def unpack_kernel(
    middle_ref,
    attend_ref,
    tail_ref,
    features_ref,
    nodes_ref,
    output_ref,
    grad_features_ref,
    grad_embed_ref,
    grad_gain_one,
    grad_shift_one,
    grad_attend,
    grad_merge,
    grad_gain_two,
    grad_shift_two,
    grad_expand,
    grad_reduce,
    grad_readout,
):
    owner = lax.axis_index("fsdp")
    width = middle_ref.shape[-1]
    output_ref[...] = nodes_ref[...]
    grad_features_ref[...] = features_ref[...]
    for half in range(2):
        for quad in range(width // QUAD):
            for kind in range(3):
                first = kind * width + quad * QUAD
                grad_attend[half * 16 : half * 16 + 16, first : first + QUAD] = attend_ref[
                    quad, half, :, kind * QUAD : (kind + 1) * QUAD
                ]
        grad_expand[half * 16 : half * 16 + 16, 0:width] = middle_ref[half, 0:16]
        grad_expand[half * 16 : half * 16 + 16, width : 2 * width] = middle_ref[half, 16:32]
        grad_reduce[half * 32 : half * 32 + 32] = middle_ref[half, 32:64]
        grad_merge[half * 16 : half * 16 + 16] = middle_ref[half, 64:80]
    grad_embed_ref[...] = tail_ref[0]
    rows = tail_ref[1]
    length = grad_gain_one.shape[0]
    turned = pltpu.roll(rows, lax.rem(width - owner * length, width), 1)
    for index, ref in enumerate((grad_gain_one, grad_shift_one, grad_gain_two, grad_shift_two)):
        ref[...] = turned[index : index + 1, 0:length].reshape(length)
    length = grad_readout.shape[0]
    first = owner * length
    turned = pltpu.roll(rows, lax.rem(2 * width - first, width), 1)
    row = jnp.where(first < width, turned[4:5, 0:length], turned[5:6, 0:length])
    grad_readout[...] = row.reshape(length)


def sds(shape, dtype):
    return jax.ShapeDtypeStruct(shape, dtype)


SMEM_SPEC = pl.BlockSpec(memory_space=pltpu.SMEM)
VMEM_SPEC = pl.BlockSpec(memory_space=pltpu.VMEM)
ANY_SPEC = pl.BlockSpec(memory_space=pl.ANY)


def layer_keep(tiles, feat, width, spread):
    rows = (HOP_PAIRS, GROUPS, 2 * GROUP)
    return [
        pltpu.VMEM((tiles, *rows, feat), BF16),
        pltpu.VMEM((tiles, TOKENS, width), F32),
        pltpu.VMEM((tiles, TOKENS, width), BF16),
        pltpu.VMEM((tiles, *rows, 3 * width), BF16),
        pltpu.VMEM((tiles, *rows, width), BF16),
        pltpu.VMEM((STREAMS, *rows, QUAD), BF16),
        pltpu.VMEM((width, width), F32),
        pltpu.VMEM((width, spread), F32),
        pltpu.VMEM((spread, width), F32),
        pltpu.VMEM((tiles, HOP_PAIRS, GROUPS, 2, GROUP, feat), F32),
    ]


def layer_part(
    lines, counts, adjacency, features, cotangent, embed, vectors, attend, merge, expand, reducer
):
    nodes, feat = features.shape
    owners = lines * PLANE
    width, spread = expand.shape[0] * owners, expand.shape[1]
    tiles = nodes // NODES_PER_TILE
    rest = (80, width)
    wide = (width // owners // 2, 3 * QUAD)
    copies = lines + PLANE - 2 + (lines - 1) * (PLANE - 1)

    def slots(rows, columns):
        return pltpu.VMEM((owners, 2, rows // 2, columns), BF16)

    def buffers(shape):
        return [
            pltpu.VMEM((owners, 2) + shape, BF16),
            pltpu.VMEM((owners,) + shape, BF16),
            pltpu.VMEM((lines, PLANE) + shape, BF16),
            pltpu.VMEM((PLANE - 1, lines) + shape, BF16),
            pltpu.VMEM((lines,) + shape, BF16),
            pltpu.VMEM((lines - 1,) + shape, BF16),
            pltpu.VMEM((2,) + shape, F32),
        ]

    outs = [
        cotangent.shape,
        features.shape,
        (2,) + rest,
        (width // QUAD, 2) + wide,
        (2, 8, width),
    ]
    return pl.pallas_call(
        functools.partial(layer_kernel, lines),
        in_specs=[SMEM_SPEC] + [VMEM_SPEC] * 13,
        out_specs=[VMEM_SPEC] * 5,
        out_shape=[sds(shape, F32) for shape in outs],
        scratch_shapes=layer_keep(tiles, feat, width, spread)
        + [
            pltpu.VMEM((feat, width), BF16),
            pltpu.VMEM((8, width), F32),
            pltpu.VMEM((8, 128), F32),
            pltpu.VMEM((owners, 16, width // 2 + 128), BF16),
        ]
        + [slots(attend.shape[0], width)] * 3
        + [slots(*shard.shape) for shard in (merge, expand, reducer)]
        + [pltpu.VMEM((feat, width), F32), pltpu.VMEM((8, width), F32)]
        + buffers(rest)
        + buffers(wide) * 2
        + [
            pltpu.VMEM((PLANE, lines + 1, 8, width), F32),
            pltpu.VMEM((PLANE - 1, lines + 1, 8, width), F32),
            pltpu.VMEM((lines, 2, 8, width), F32),
            pltpu.VMEM((lines - 1, 2, 8, width), F32),
            pltpu.VMEM((2, 8, width), F32),
            pltpu.VMEM((2, 8, width), F32),
        ]
        + [
            pltpu.SemaphoreType.DMA((7, copies)),
            pltpu.SemaphoreType.DMA((7, owners)),
            pltpu.SemaphoreType.DMA((7, 2)),
            pltpu.SemaphoreType.DMA((4, 2, PLANE + lines)),
        ],
        compiler_params=pltpu.CompilerParams(
            vmem_limit_bytes=VMEM_GRANT, collective_id=0, has_side_effects=True
        ),
        name="layer",
    )(counts, adjacency, features, cotangent, embed, *vectors, attend, merge, expand, reducer)


def layer_alone_part(
    counts, adjacency, features, cotangent, rows, embed, attend, merge, expand, reducer
):
    nodes, feat = features.shape
    width, spread = expand.shape
    tiles = nodes // NODES_PER_TILE
    wide = (PACK, 2, width // PACK // 2, 3 * QUAD)
    return pl.pallas_call(
        layer_alone_kernel,
        in_specs=[SMEM_SPEC] + [VMEM_SPEC] * 11,
        out_specs=[VMEM_SPEC] * 7,
        out_shape=[
            sds(cotangent.shape, F32),
            sds(features.shape, F32),
            sds((PACK, 2, 80, width), BF16),
            sds(wide, BF16),
            sds(wide, BF16),
            sds((feat, width), F32),
            sds((8, width), F32),
        ],
        scratch_shapes=layer_keep(tiles, feat, width, spread),
        compiler_params=pltpu.CompilerParams(vmem_limit_bytes=VMEM_GRANT),
        name="layer_alone",
    )(
        counts,
        adjacency,
        features,
        cotangent,
        rows,
        embed,
        attend[:, :width],
        attend[:, width : 2 * width],
        attend[:, 2 * width :],
        merge,
        expand,
        reducer,
    )


def unpack_part(middle, attend, tail, features, nodes, shapes):
    return pl.pallas_call(
        unpack_kernel,
        out_shape=[sds(shape, F32) for shape in [nodes.shape, features.shape] + shapes],
        compiler_params=pltpu.CompilerParams(vmem_limit_bytes=VMEM_GRANT),
        name="unpack_shares",
    )(middle, attend, tail, features, nodes)


def gather(block):
    return lax.all_gather(block, "fsdp", axis=0, tiled=True)


def share(term):
    part = lax.psum_scatter(term.astype(BF16), "fsdp", scatter_dimension=0, tiled=True)
    return lax.psum(part.astype(F32), "grp")


def body(
    features,
    adjacency,
    counts,
    input_weight,
    first_gain,
    first_shift,
    attend_weight,
    merge_weight,
    second_gain,
    second_shift,
    expand_weight,
    reduce_weight,
    readout_weight,
    cotangent,
):
    vectors = (first_gain, first_shift, second_gain, second_shift, readout_weight)
    owners = lax.axis_size("fsdp")
    if owners % PLANE == 0 and input_weight.shape[0] == 8 and attend_weight.shape[0] == 32:
        lines = owners // PLANE
        tiles = cotangent.shape[0] // NODES_PER_TILE
        output, grad_features, *shares = layer_part(
            lines,
            counts,
            adjacency,
            features,
            cotangent.reshape(tiles, NODES_PER_TILE, cotangent.shape[1]),
            input_weight,
            vectors,
            attend_weight,
            merge_weight,
            expand_weight,
            reduce_weight,
        )
        shapes = [
            weight.shape
            for weight in (
                input_weight,
                first_gain,
                first_shift,
                attend_weight,
                merge_weight,
                second_gain,
                second_shift,
                expand_weight,
                reduce_weight,
                readout_weight,
            )
        ]
        return tuple(
            unpack_part(*shares, grad_features, output.reshape(cotangent.shape), shapes)
        )
    return body_apart(
        features,
        adjacency,
        counts,
        input_weight,
        vectors,
        attend_weight,
        merge_weight,
        expand_weight,
        reduce_weight,
        cotangent,
    )


def body_apart(
    features,
    adjacency,
    counts,
    input_weight,
    vectors,
    attend_weight,
    merge_weight,
    expand_weight,
    reduce_weight,
    cotangent,
):
    lengths = [v.shape[0] for v in vectors]
    places = [sum(lengths[:i]) for i in range(len(lengths) + 1)]
    packed = lax.all_gather(jnp.concatenate(vectors), "fsdp", axis=0, tiled=False)
    width = merge_weight.shape[1]
    full = [
        packed[:, places[i] : places[i + 1]].astype(F32).reshape(-1, width)
        for i in range(len(lengths))
    ]
    rows = jnp.concatenate(full + [jnp.zeros((2, width), F32)], axis=0)
    embed, attend, merge, expand, reducer = map(
        gather, (input_weight, attend_weight, merge_weight, expand_weight, reduce_weight)
    )
    tiles = cotangent.shape[0] // NODES_PER_TILE
    output, grad_features, terms, early, late, grad_embed, rows_grad = layer_alone_part(
        counts,
        adjacency,
        features,
        cotangent.reshape(tiles, NODES_PER_TILE, width),
        rows,
        embed,
        attend,
        merge,
        expand,
        reducer,
    )
    grad_attend = jnp.stack([early.reshape(width, 3, QUAD), late.reshape(width, 3, QUAD)], axis=2)
    grad_attend = grad_attend.reshape(width, 3 * width)
    spread = expand.shape[1]
    grad_expand = jnp.concatenate([terms[:, :, 0:16], terms[:, :, 16:32]], axis=-1)
    parts = lax.axis_size("fsdp")
    pieces = [rows_grad[i] for i in range(4)] + [rows_grad[4:6]]
    packed_grad = jnp.concatenate([piece.reshape(parts, -1) for piece in pieces], axis=1)
    packed_grad = lax.psum(
        lax.psum_scatter(packed_grad, "fsdp", scatter_dimension=0, tiled=True), "grp"
    ).reshape(-1)
    small = [packed_grad[places[i] : places[i + 1]] for i in range(len(lengths))]
    return (
        output.reshape(cotangent.shape),
        grad_features,
        share(grad_embed),
        small[0],
        small[1],
        share(grad_attend),
        share(terms[:, :, 64:80].reshape(width, width)),
        small[2],
        small[3],
        share(grad_expand.reshape(width, spread)),
        share(terms[:, :, 32:64].reshape(spread, width)),
        small[4],
    )


def solution(mesh):
    nodes = ("grp", "fsdp")
    rows = P("fsdp", None)
    vector = P("fsdp")
    in_specs = (
        P(nodes, None),
        P(nodes, None, None),
        P(nodes),
        rows,
        vector,
        vector,
        rows,
        rows,
        vector,
        vector,
        rows,
        rows,
        vector,
        P(nodes, None),
    )
    out_specs = (
        P(nodes, None),
        P(nodes, None),
        rows,
        vector,
        vector,
        rows,
        rows,
        vector,
        vector,
        rows,
        rows,
        vector,
    )
    return jax.shard_map(body, mesh=mesh, in_specs=in_specs, out_specs=out_specs, check_vma=False)
```

```python
import functools

import jax
import jax.numpy as jnp
from jax import lax
from jax.experimental import pallas as pl
from jax.experimental.pallas import tpu as pltpu
from jax.sharding import PartitionSpec as P

HEADS = 8
HEAD = 64
HOPS = 7
HOP_TOKENS = HOPS + 1
NODES_PER_TILE = 64
TOKENS = NODES_PER_TILE * HOP_TOKENS
GROUP = 8
STREAMS = 2
FEEDS = 1
SKEW = 1
GROUPS = NODES_PER_TILE // GROUP
HOP_PAIRS = HOP_TOKENS // 2
QUAD = 4 * HEAD
MIB = 1 << 20
VMEM_GRANT = 62 * MIB
F32 = jnp.float32
BF16 = jnp.bfloat16
GELU_A = 0.7978845608028654
GELU_B = 0.044715
LOG2_E = 1.4426950408889634
PLANE = 4
PACK = 16
MESH = pl.DeviceIdType.MESH


def dot(left, right):
    return jnp.dot(left, right, preferred_element_type=F32)


def dot_lead(left, right):
    return lax.dot_general(left, right, (((0,), (0,)), ((), ())), preferred_element_type=F32)


def dot_last(left, right):
    return lax.dot_general(left, right, (((1,), (1,)), ((), ())), preferred_element_type=F32)


def link_of(adjacency, count):
    slots = adjacency.shape[0]
    rows = lax.broadcasted_iota(jnp.int32, (slots, slots), 0)
    cols = lax.broadcasted_iota(jnp.int32, (slots, slots), 1)
    live = jnp.logical_and(rows < count, cols < count)
    link = jnp.where(live, adjacency, 0) + jnp.where(rows == cols, 1, 0)
    link = link.astype(F32)
    root = lax.rsqrt(jnp.sum(link, axis=-1, keepdims=True))
    return link.astype(BF16), root


def hop(link, root, state):
    width = state.shape[1]
    scaled = state * root
    high = scaled.astype(BF16)
    rest = scaled - high.astype(F32)
    middle = rest.astype(BF16)
    low = (rest - middle.astype(F32)).astype(BF16)
    spread = dot(link, jnp.concatenate([high, middle, low], axis=1))
    return (spread[:, :width] + (spread[:, width : 2 * width] + spread[:, 2 * width :])) * root


def live_rows(count, first, rows):
    index = lax.broadcasted_iota(jnp.int32, (rows, 1), 0) + first
    return jnp.where(index < count, 1.0, 0.0).astype(F32)


def norm_stats(values):
    mean = jnp.mean(values, axis=-1, keepdims=True)
    centred = values - mean
    var = jnp.mean(centred * centred, axis=-1, keepdims=True)
    inv = lax.rsqrt(var + 1e-05)
    return centred * inv, inv


def quad_stack(block):
    head = lax.broadcasted_iota(jnp.int32, block.shape, 1) // HEAD
    return jnp.concatenate(
        [jnp.where(head == h, block, jnp.zeros_like(block)) for h in range(4)], axis=0
    )


def grad_softmax(probs, grad_probs):
    tokens, columns = probs.shape
    weighted = (probs * grad_probs).reshape(HOP_TOKENS, GROUP, columns)
    total = jnp.sum(weighted, axis=0)
    shaped = probs.reshape(HOP_TOKENS, GROUP, columns)
    return (weighted - shaped * total[None]).reshape(tokens, columns).astype(BF16)


def quad_probs(scores):
    tokens, columns = scores.shape
    scores = scores.reshape(HOP_TOKENS, GROUP, columns)
    top = jnp.max(scores, axis=0)
    power = jnp.exp2((scores - top[None]) * (HEAD ** (-0.5) * LOG2_E))
    row = lax.broadcasted_iota(jnp.int32, (GROUP, columns), 0)
    col = lax.broadcasted_iota(jnp.int32, (GROUP, columns), 1) % GROUP
    share = jnp.where(row == col, 1.0 / jnp.sum(power, axis=0), 0.0)
    return (power * share[None]).reshape(tokens, columns)


def queries_from(weights, block):
    tokens = block.shape[0]
    out = []
    lane = lax.broadcasted_iota(jnp.int32, (tokens, 2 * HEAD), 1)
    for first in (0, 2 * HEAD):
        both = dot_lead(weights[:, first : first + 2 * HEAD], block[:, first : first + 2 * HEAD])
        out.append(jnp.where(lane < HEAD, both[:tokens], both[tokens:]))
    return jnp.concatenate(out, axis=1)


def hop_rows(values, index):
    shaped = values.reshape(HOP_PAIRS, GROUPS, 2, GROUP, values.shape[-1])
    return shaped[index // 2, :, index % 2].reshape(NODES_PER_TILE, values.shape[-1])


def hop_join(parts):
    width = parts[0].shape[-1]
    blocks = []
    for pair in range(HOP_PAIRS):
        both = [parts[2 * pair + k].reshape(GROUPS, 1, GROUP, width) for k in range(2)]
        blocks.append(jnp.concatenate(both, axis=1))
    return jnp.concatenate(blocks, axis=0).reshape(TOKENS, width)


def interleave(streams):
    live = list(enumerate(streams))
    turn = 0
    while live:
        live = [
            (place, stream)
            for place, stream in live
            if turn < place * SKEW or next(stream, live) is not live
        ]
        turn += 1


class Place:
    def __init__(self, lines):
        self.lines = lines
        self.core = lax.axis_index("grp")
        self.owner = lax.axis_index("fsdp")
        self.line = lax.div(self.owner, PLANE)
        self.spot = lax.rem(self.owner, PLANE)

    def line_turn(self, ahead):
        return lax.rem(self.line + ahead + self.lines, self.lines)

    def spot_turn(self, ahead):
        return lax.rem(self.spot + ahead + PLANE, PLANE)

    def line_peer(self, ahead):
        return (self.core, self.line_turn(ahead) * PLANE + self.spot)

    def plane_peer(self, ahead):
        return (self.core, self.line * PLANE + self.spot_turn(ahead))

    def side_peer(self):
        return (self.core, self.owner + 1 - 2 * lax.rem(self.spot, 2))

    def side_spot(self):
        return self.spot + 1 - 2 * lax.rem(self.spot, 2)

    def sibling(self):
        return (1 - self.core, self.owner)

    def peers(self):
        return (
            [self.line_peer(d) for d in range(1, self.lines)]
            + [self.plane_peer(e) for e in range(1, PLANE)]
            + [self.sibling()]
        )

    def greet(self):
        barrier = pltpu.get_barrier_semaphore()
        for peer in self.peers():
            pl.semaphore_signal(barrier, inc=1, device_id=peer, device_id_type=MESH)

    def greeted(self):
        pl.semaphore_wait(pltpu.get_barrier_semaphore(), self.lines + PLANE - 1)


def remote(source, target, send, recv, device):
    return pltpu.make_async_remote_copy(
        src_ref=source,
        dst_ref=target,
        send_sem=send,
        recv_sem=recv,
        device_id=device,
        device_id_type=MESH,
    )


class Gather:
    def __init__(self, place, slots, send, recv, halves):
        self.place, self.slots, self.send, self.recv = place, slots, send, recv
        self.halves = halves

    def slot(self, line, spot):
        if self.halves:
            return self.slots.at[line, spot, self.place.core]
        return self.slots.at[line, spot]

    def line_copies(self):
        place = self.place
        own = self.slot(place.line, place.spot)
        return [
            remote(own, own, self.send.at[d], self.recv.at[d], place.line_peer(d))
            for d in range(1, place.lines)
        ]

    def plane_copies(self):
        place = self.place
        line = self.slot(slice(None), place.spot)
        first = place.lines - 1
        return [
            remote(line, line, self.send.at[first + e], self.recv.at[first + e], place.plane_peer(e))
            for e in range(1, PLANE)
        ]

    def start(self):
        for copy in self.line_copies():
            copy.start()

    def forward(self):
        for copy in self.line_copies():
            copy.wait()
        for copy in self.plane_copies():
            copy.start()

    def finish(self):
        for copy in self.plane_copies():
            copy.wait()

    def pair(self):
        half = self.slots.at[:, :, self.place.core]
        return remote(half, half, self.send.at[0], self.recv.at[0], self.place.sibling())


class CrossGather(Gather):
    def step_copies(self):
        place = self.place
        line = self.slot(slice(None), place.spot)
        first = place.lines
        return [
            remote(line, line, self.send.at[first + k], self.recv.at[first + k], peer)
            for k, peer in enumerate((place.side_peer(), place.plane_peer(2)))
        ]

    def cross_copies(self):
        place = self.place
        first = place.lines + 2
        half = self.slots.shape[-1] // 2
        copies = []
        for k, (spot, peer) in enumerate(
            ((place.side_spot(), place.plane_peer(2)), (place.spot_turn(2), place.side_peer()))
        ):
            part = self.slots.at[:, spot, place.core, :, k * half : (k + 1) * half]
            copies.append(
                remote(part, part, self.send.at[first + k], self.recv.at[first + k], peer)
            )
        return copies

    def forward(self):
        for copy in self.line_copies():
            copy.wait()
        for copy in self.step_copies():
            copy.start()

    def cross(self):
        for copy in self.step_copies():
            copy.wait()
        for copy in self.cross_copies():
            copy.start()

    def finish(self):
        for copy in self.cross_copies():
            copy.wait()


class Scatter:
    def __init__(self, place, terms, got, chip, plane_got, line_out, line_got, result, sems):
        self.place, self.terms, self.got, self.chip = place, terms, got, chip
        self.plane_got, self.line_out, self.line_got = plane_got, line_out, line_got
        self.result, self.sems = result, sems

    def pair(self):
        place = self.place
        return remote(
            self.terms.at[:, 1 - place.core],
            self.got,
            self.sems.at[0, 0],
            self.sems.at[1, 0],
            place.sibling(),
        )

    def plane(self):
        place = self.place
        return [
            remote(
                self.chip.at[:, place.spot_turn(e)],
                self.plane_got.at[e - 1],
                self.sems.at[0, e],
                self.sems.at[1, e],
                place.plane_peer(e),
            )
            for e in range(1, PLANE)
        ]

    def line(self):
        place = self.place
        return [
            remote(
                self.line_out.at[place.line_turn(d)],
                self.line_got.at[d - 1],
                self.sems.at[0, PLANE + d - 1],
                self.sems.at[1, PLANE + d - 1],
                place.line_peer(d),
            )
            for d in range(1, place.lines)
        ]

    def last(self):
        place = self.place
        half = self.result.at[place.core]
        k = PLANE + place.lines - 1
        return remote(half, half, self.sems.at[0, k], self.sems.at[1, k], place.sibling())

    def begin(self):
        self.pair().start()

    def to_plane(self):
        place = self.place
        self.pair().wait()

        def add(line, carry):
            for spot in range(PLANE):
                owner = line * PLANE + spot
                self.chip[line, spot] = self.terms[owner, place.core] + self.got[owner]
            return carry

        lax.fori_loop(0, place.lines, add, 0)
        for copy in self.plane():
            copy.start()

    def to_line(self):
        place = self.place
        for copy in self.plane():
            copy.wait()

        def add(line, carry):
            total = self.chip[line, place.spot].astype(F32)
            for e in range(PLANE - 1):
                total = total + self.plane_got[e, line].astype(F32)
            self.line_out[line] = total.astype(BF16)
            return carry

        lax.fori_loop(0, place.lines, add, 0)
        for copy in self.line():
            copy.start()

    def to_sibling(self):
        place = self.place
        for copy in self.line():
            copy.wait()
        total = self.line_out[place.line].astype(F32)
        for d in range(place.lines - 1):
            total = total + self.line_got[d].astype(F32)
        self.result[place.core] = total
        self.last().start()

    def end(self):
        self.last().wait()


class TailScatter:
    def __init__(self, place, own, plane_got, line_out, line_got, mine, other, sems):
        self.place, self.own, self.plane_got, self.line_out = place, own, plane_got, line_out
        self.line_got, self.mine, self.other, self.sems = line_got, mine, other, sems

    def plane(self):
        place = self.place
        return [
            remote(
                self.own.at[place.spot_turn(e)],
                self.plane_got.at[e - 1],
                self.sems.at[0, e],
                self.sems.at[1, e],
                place.plane_peer(e),
            )
            for e in range(1, PLANE)
        ]

    def line(self):
        place = self.place
        return [
            remote(
                self.line_out.at[place.line_turn(d)],
                self.line_got.at[d - 1],
                self.sems.at[0, PLANE + d - 1],
                self.sems.at[1, PLANE + d - 1],
                place.line_peer(d),
            )
            for d in range(1, place.lines)
        ]

    def last(self):
        return remote(
            self.mine, self.other, self.sems.at[0, 0], self.sems.at[1, 0], self.place.sibling()
        )

    def begin(self):
        for copy in self.plane():
            copy.start()

    def to_line(self):
        place = self.place
        for copy in self.plane():
            copy.wait()
        total = self.own[place.spot]
        for e in range(PLANE - 1):
            total = total + self.plane_got[e]
        for line in range(place.lines):
            self.line_out[line, 0] = total[line]
            self.line_out[line, 1] = total[place.lines]
        for copy in self.line():
            copy.start()

    def to_sibling(self):
        place = self.place
        for copy in self.line():
            copy.wait()
        total = self.line_out[place.line]
        for d in range(place.lines - 1):
            total = total + self.line_got[d]
        self.mine[...] = total
        self.last().start()

    def end(self):
        self.last().wait()
        return self.mine[...] + self.other[...]


def hop_states(counts_ref, adjacency_ref, features_ref, stacked_ref):
    clusters, slots = adjacency_ref.shape[:2]
    per_cluster = slots // NODES_PER_TILE
    links = []
    states = []
    for cluster in range(clusters):
        count = counts_ref[cluster]
        links.append(link_of(adjacency_ref[cluster], count))
        states.append(
            features_ref[cluster * slots : (cluster + 1) * slots].astype(F32)
            * live_rows(count, 0, slots)
        )
    earlier = [None] * clusters
    for index in range(HOP_TOKENS):
        for cluster in range(clusters):
            if index > 0:
                states[cluster] = hop(*links[cluster], states[cluster])
            if index % 2 == 0:
                earlier[cluster] = states[cluster]
                continue
            for part in range(per_cluster):
                rows = slice(part * NODES_PER_TILE, (part + 1) * NODES_PER_TILE)
                both = [
                    state[rows].reshape(GROUPS, GROUP, state.shape[-1])
                    for state in (earlier[cluster], states[cluster])
                ]
                stacked_ref[cluster * per_cluster + part, index // 2] = jnp.concatenate(
                    both, axis=1
                ).astype(BF16)


def spread_vectors(small, owners, width):
    rows = small.shape[0]
    lane = lax.broadcasted_iota(jnp.int32, (128, width), 0)
    column = lax.broadcasted_iota(jnp.int32, (128, width), 1)
    row = lax.broadcasted_iota(jnp.int32, (rows, width), 0)
    place = lax.broadcasted_iota(jnp.int32, (rows, width), 1)
    piece = width // owners
    pieces = dot(small, jnp.where(lane == column % piece, 1.0, 0.0).astype(BF16))
    out = []
    for vector in range(4):
        mine = jnp.logical_and(row % 8 == vector, lax.div(row, 8) == lax.div(place, piece))
        out.append(jnp.sum(jnp.where(mine, pieces, 0.0), axis=0, keepdims=True))
    pieces = dot(small, jnp.where(lane == column % (2 * piece), 1.0, 0.0).astype(BF16))
    for first in (0, owners // 2):
        owner = lax.div(place, 2 * piece) + first
        mine = jnp.logical_and(row % 8 == 4, lax.div(row, 8) == owner)
        out.append(jnp.sum(jnp.where(mine, pieces, 0.0), axis=0, keepdims=True))
    return jnp.concatenate(out + [jnp.zeros((2, width), F32)], axis=0)


def hop_back(counts_ref, adjacency_ref, grad_stacked_ref, grad_features_ref, between):
    clusters, slots = adjacency_ref.shape[:2]
    per_cluster = slots // NODES_PER_TILE
    links = []
    states = []

    def hop_grad(cluster, index):
        return jnp.concatenate(
            [
                grad_stacked_ref[cluster * per_cluster + p, index // 2, :, index % 2].reshape(
                    NODES_PER_TILE, grad_stacked_ref.shape[-1]
                )
                for p in range(per_cluster)
            ],
            axis=0,
        )

    for cluster in range(clusters):
        links.append(link_of(adjacency_ref[cluster], counts_ref[cluster]))
        states.append(hop_grad(cluster, HOPS))
    for index in range(HOPS - 1, -1, -1):
        for cluster in range(clusters):
            states[cluster] = hop_grad(cluster, index) + hop(*links[cluster], states[cluster])
        if index in between:
            between[index]()
    for cluster in range(clusters):
        grad_features_ref[cluster * slots : (cluster + 1) * slots] = states[cluster] * live_rows(
            counts_ref[cluster], 0, slots
        )


def block_of(ref, tile, group, first):
    return ref[tile, :, group, :, first : first + QUAD].reshape(GROUP * HOP_TOKENS, QUAD)


def put_block(ref, tile, group, first, block):
    ref[tile, :, group, :, first : first + QUAD] = block.astype(BF16).reshape(
        HOP_PAIRS, 2 * GROUP, QUAD
    )


def tokens_of(ref, tile):
    return ref[tile].reshape(TOKENS, ref.shape[-1])


def embed_tile(tile, stacked_ref, embed, gain, shift, second_ref, normed_ref):
    hidden = dot(tokens_of(stacked_ref, tile), embed)
    second_ref[tile] = hidden
    normal, _ = norm_stats(hidden)
    normed_ref[tile] = (normal * gain + shift).astype(BF16)


def project_step(first_tile, kind, normed_ref, weight, triple_ref):
    width = normed_ref.shape[-1]
    tiles = pl.ds(first_tile, STREAMS)
    normed = normed_ref[tiles].reshape(STREAMS * TOKENS, width)
    triple_ref[tiles, :, :, :, kind * width : (kind + 1) * width] = (
        dot(normed, weight).astype(BF16).reshape(STREAMS, *triple_ref.shape[1:-1], width)
    )


def attend_tile(tile, normed_ref, value_weight, triple_ref, mixed_ref):
    width = normed_ref.shape[-1]
    triple_ref[tile, :, :, :, 2 * width :] = (
        dot(normed_ref[tile], value_weight).astype(BF16).reshape(*triple_ref.shape[1:-1], width)
    )
    places = [(tile, g, first) for g in range(GROUPS) for first in range(0, width, QUAD)]
    keys = [block_of(triple_ref, t, g, width + first) for t, g, first in places]
    queries = [quad_stack(block_of(triple_ref, *place)) for place in places]
    scores = [dot_last(k, q) for k, q in zip(keys, queries)]
    probs = [quad_probs(score).astype(BF16) for score in scores]
    values = [block_of(triple_ref, t, g, 2 * width + first) for t, g, first in places]
    blocks = [queries_from(p, v) for p, v in zip(probs, values)]
    for place, block in zip(places, blocks):
        put_block(mixed_ref, *place, block)


def middle_step(
    first_tile,
    counts_ref,
    second_ref,
    mixed_ref,
    cotangent_ref,
    rows_ref,
    expand,
    reducer,
    output_ref,
    rows_grad_ref,
    grad_merge_ref,
    grad_expand_ref,
    grad_reduce_ref,
):
    width = second_ref.shape[-1]
    gain, shift = rows_ref[2:3], rows_ref[3:4]
    row_node, row_hop = rows_ref[4:5], rows_ref[5:6]

    def stream(part):
        tile = first_tile + part
        second = second_ref[tile]
        normal, inv = norm_stats(second)
        inner = (normal * gain + shift).astype(BF16)
        yield
        before = dot(inner, expand)
        yield
        square = before * before
        gate = 0.5 + 0.5 * jnp.tanh(before * (square * (GELU_A * GELU_B) + GELU_A))
        gated = before * gate
        after = gated.astype(BF16)
        slope = gate + (gated - gated * gate) * (
            square * (6.0 * GELU_A * GELU_B) + 2.0 * GELU_A
        )
        yield
        third = second + dot(after, reducer)
        yield
        shaped = [hop_rows(third, k) for k in range(HOP_TOKENS)]
        node = tile * NODES_PER_TILE
        keep = live_rows(counts_ref[lax.div(node, 128)], lax.rem(node, 128), NODES_PER_TILE)
        centre = shaped[0]
        base = jnp.sum(centre * row_node, axis=-1, keepdims=True)
        logits = [
            base + jnp.sum(shaped[k] * row_hop, axis=-1, keepdims=True)
            for k in range(1, HOP_TOKENS)
        ]
        top = functools.reduce(jnp.maximum, logits)
        powers = [jnp.exp(logit - top) for logit in logits]
        scale = 1.0 / functools.reduce(jnp.add, powers)
        shares = [power * scale for power in powers]
        total = centre
        for k in range(1, HOP_TOKENS):
            total = total + shares[k - 1] * shaped[k]
        output_ref[tile] = total * keep
        cotangent = cotangent_ref[tile] * keep
        grad_shares = [
            jnp.sum(cotangent * shaped[k], axis=-1, keepdims=True) for k in range(1, HOP_TOKENS)
        ]
        mean_share = functools.reduce(jnp.add, [s * g for s, g in zip(shares, grad_shares)])
        grad_logits = [s * (g - mean_share) for s, g in zip(shares, grad_shares)]
        grad_base = functools.reduce(jnp.add, grad_logits)
        parts = [cotangent + grad_base * row_node]
        read_hop = jnp.zeros((NODES_PER_TILE, width), F32)
        for k in range(1, HOP_TOKENS):
            parts.append(shares[k - 1] * cotangent + grad_logits[k - 1] * row_hop)
            read_hop = read_hop + grad_logits[k - 1] * shaped[k]
        rows_grad_ref[4:5] += jnp.sum(grad_base * centre, axis=0, keepdims=True)
        rows_grad_ref[5:6] += jnp.sum(read_hop, axis=0, keepdims=True)
        grad_third = hop_join(parts)
        grad_branch = grad_third.astype(BF16)
        yield
        grad_after = dot_last(grad_branch, reducer)
        grad_reduce_ref[...] += dot_lead(after, grad_branch)
        yield
        grad_before = (slope * grad_after).astype(BF16)
        yield
        grad_inner = dot_last(grad_before, expand)
        grad_expand_ref[...] += dot_lead(inner, grad_before)
        yield
        rows_grad_ref[2:3] += jnp.sum(grad_inner * normal, axis=0, keepdims=True)
        rows_grad_ref[3:4] += jnp.sum(grad_inner, axis=0, keepdims=True)
        grad_normal = grad_inner * gain
        grad_second = grad_third + inv * (
            grad_normal
            - jnp.mean(grad_normal, axis=-1, keepdims=True)
            - normal * jnp.mean(grad_normal * normal, axis=-1, keepdims=True)
        )
        second_ref[tile] = grad_second
        yield
        grad_merge_ref[...] += dot_lead(tokens_of(mixed_ref, tile), grad_second.astype(BF16))

    interleave([stream(part) for part in range(FEEDS)])


def pack_terms(terms_ref, grad_merge_ref, grad_expand_ref, grad_reduce_ref):
    width, spread = grad_expand_ref.shape
    wide = grad_expand_ref[...].astype(BF16).reshape(PACK, 2, width // PACK // 2, spread)
    deep = grad_reduce_ref[...].astype(BF16).reshape(PACK, 2, spread // PACK // 2, width)
    square = grad_merge_ref[...].astype(BF16).reshape(PACK, 2, width // PACK // 2, width)
    terms_ref[:, :, 0:16] = wide[..., :width]
    terms_ref[:, :, 16:32] = wide[..., width:]
    terms_ref[:, :, 32:64] = deep
    terms_ref[:, :, 64:80] = square


def attend_back_step(quad, first_tile, triple_ref, second_ref, normed_ref, merge, grad_mixed_ref, grad_attend_ref):
    width = normed_ref.shape[-1]
    for part in range(STREAMS):
        grad_mixed = dot_last(second_ref[first_tile + part].astype(BF16), merge).astype(BF16)
        grad_mixed_ref[part] = grad_mixed.reshape(grad_mixed_ref.shape[1:])
    places = [(part, group) for part in range(STREAMS) for group in range(GROUPS)]
    scale = HEAD ** (-0.5)
    starts = [kind * width + quad * QUAD for kind in range(3)]

    def read(kind):
        return [block_of(triple_ref, first_tile + p, g, starts[kind]) for p, g in places]

    keys = read(1)
    queries = [quad_stack(block) for block in read(0)]
    scores = [dot_last(k, q) for k, q in zip(keys, queries)]
    values = read(2)
    out_grads = [quad_stack(block_of(grad_mixed_ref, p, g, 0)) for p, g in places]
    grad_probs = [dot_last(v, o) for v, o in zip(values, out_grads)]
    probs = [quad_probs(score) for score in scores]
    grad_scores = [grad_softmax(p, g) for p, g in zip(probs, grad_probs)]
    grad_values = [dot(p.astype(BF16), o) for p, o in zip(probs, out_grads)]
    grad_keys = [dot(s, q) for s, q in zip(grad_scores, queries)]
    grad_queries = [queries_from(s, k) for s, k in zip(grad_scores, keys)]
    for (part, group), a, b, c in zip(places, grad_queries, grad_keys, grad_values):
        for start, block in zip(starts, (a * scale, b * scale, c)):
            put_block(triple_ref, first_tile + part, group, start, block)
    tiles = pl.ds(first_tile, STREAMS)
    grads = jnp.concatenate(
        [
            triple_ref[tiles, :, :, :, start : start + QUAD].reshape(STREAMS * TOKENS, QUAD)
            for start in starts
        ],
        axis=1,
    )
    grad_attend_ref[:, 0 : 3 * QUAD] += dot_lead(
        normed_ref[tiles].reshape(STREAMS * TOKENS, width), grads
    )


def embed_back_step(
    first_tile,
    stacked_ref,
    second_ref,
    triple_ref,
    attend,
    embed,
    gain,
    rows_keep,
    grad_embed_ref,
    normed_ref,
):
    def stream(part):
        tile = first_tile + part
        stacked = tokens_of(stacked_ref, tile)
        grad_normed = dot_last(tokens_of(triple_ref, tile), attend)
        hidden = dot(stacked, embed)
        yield
        normal, inv = norm_stats(hidden)
        rows_keep[0:1] += jnp.sum(grad_normed * normal, axis=0, keepdims=True)
        rows_keep[1:2] += jnp.sum(grad_normed, axis=0, keepdims=True)
        grad_normal = grad_normed * gain
        grad_hidden = second_ref[tile] + inv * (
            grad_normal
            - jnp.mean(grad_normal, axis=-1, keepdims=True)
            - normal * jnp.mean(grad_normal * normal, axis=-1, keepdims=True)
        )
        grad_hidden = grad_hidden.astype(BF16)
        yield
        grad_embed_ref[...] += dot_lead(stacked, grad_hidden)
        normed_ref[tile] = grad_hidden

    interleave([stream(part) for part in range(STREAMS)])


class Silent:
    def __getattr__(self, name):
        return lambda *arguments: None


def loop(count, step):
    def body(index, carry):
        step(index)
        return carry

    lax.fori_loop(0, count, body, 0)


def layer_phases(
    counts_ref,
    adjacency_ref,
    features_ref,
    cotangent_ref,
    rows_ref,
    embed_ref,
    query_ref,
    key_ref,
    value_ref,
    merge_ref,
    expand_ref,
    reduce_ref,
    output_ref,
    grad_features_ref,
    terms_ref,
    early_terms,
    late_terms,
    grad_embed_ref,
    rows_keep,
    keep,
    transfers,
):
    (
        stacked_ref,
        second_ref,
        normed_ref,
        triple_ref,
        mixed_ref,
        grad_mixed_ref,
        grad_merge_ref,
        grad_expand_ref,
        grad_reduce_ref,
        grad_stacked_ref,
    ) = keep
    tiles, _, width = second_ref.shape
    pairs = tiles // STREAMS
    sums = (grad_merge_ref, grad_expand_ref, grad_reduce_ref)

    def clear():
        for ref in (rows_keep, grad_embed_ref, *sums):
            ref[...] = jnp.zeros_like(ref)

    transfers.lead()
    hop_states(counts_ref, adjacency_ref, features_ref, stacked_ref)
    if not transfers.head(clear):
        clear()

    def embed_step(tile):
        embed_tile(
            tile, stacked_ref, embed_ref[...], rows_ref[0:1], rows_ref[1:2], second_ref, normed_ref
        )
        transfers.beside_embed(tile, tiles)

    loop(tiles, embed_step)
    for kind, weight_ref in enumerate((query_ref, key_ref)):
        transfers.before_projection(kind)

        def project(pair, kind=kind, weight_ref=weight_ref):
            weight = weight_ref[...].reshape(width, width)
            project_step(pair * STREAMS, kind, normed_ref, weight, triple_ref)
            transfers.beside_projection(kind, pair)

        loop(pairs, project)
    transfers.before_projection(2)

    def attend_step(tile):
        attend_tile(tile, normed_ref, value_ref[...].reshape(width, width), triple_ref, mixed_ref)
        transfers.beside_attention(tile, tiles)

    loop(tiles, attend_step)
    transfers.before_merge()

    def merge_step(pair):
        mixed = mixed_ref[pl.ds(pair * STREAMS, STREAMS)].reshape(STREAMS * TOKENS, width)
        second_ref[pl.ds(pair * STREAMS, STREAMS)] += dot(
            mixed, merge_ref[...].reshape(width, width)
        ).reshape(STREAMS, TOKENS, width)

    loop(pairs, merge_step)
    transfers.before_middle()
    spread = grad_expand_ref.shape[1]

    def feed_step(pair):
        middle_step(
            pair * FEEDS,
            counts_ref,
            second_ref,
            mixed_ref,
            cotangent_ref,
            rows_ref,
            expand_ref[...].reshape(width, spread),
            reduce_ref[...].reshape(spread, width),
            output_ref,
            rows_keep,
            grad_merge_ref,
            grad_expand_ref,
            grad_reduce_ref,
        )

    loop(tiles // FEEDS, feed_step)
    pack_terms(terms_ref, grad_merge_ref, grad_expand_ref, grad_reduce_ref)
    transfers.after_middle()
    grad_attend_ref = grad_expand_ref
    for quad, terms in enumerate((early_terms, late_terms)):
        grad_attend_ref[...] = jnp.zeros_like(grad_attend_ref)

        def back_step(pair, quad=quad):
            attend_back_step(
                quad,
                pair * STREAMS,
                triple_ref,
                second_ref,
                normed_ref,
                merge_ref[...].reshape(width, width)[quad * QUAD : (quad + 1) * QUAD],
                grad_mixed_ref,
                grad_attend_ref,
            )
            transfers.beside_backward(quad, pair, pairs)

        loop(pairs, back_step)
        terms[...] = grad_attend_ref[:, 0 : 3 * QUAD].astype(BF16).reshape(terms.shape)
        transfers.after_backward(quad)

    def embed_back(pair):
        embed_back_step(
            pair * STREAMS,
            stacked_ref,
            second_ref,
            triple_ref,
            jnp.concatenate(
                [ref[...].reshape(width, width) for ref in (query_ref, key_ref, value_ref)], axis=1
            ),
            embed_ref[...],
            rows_ref[0:1],
            rows_keep,
            grad_embed_ref,
            normed_ref,
        )
        transfers.beside_embed_back(pair, pairs)

    loop(pairs, embed_back)
    transfers.after_embed_back()

    def stacked_back(pair):
        grad_hidden = normed_ref[pl.ds(pair * STREAMS, STREAMS)].reshape(STREAMS * TOKENS, width)
        grad_stacked_ref[pl.ds(pair * STREAMS, STREAMS)] = dot_last(
            grad_hidden, embed_ref[...]
        ).reshape(STREAMS, *grad_stacked_ref.shape[1:])

    loop(pairs, stacked_back)
    hop_back(
        counts_ref,
        adjacency_ref,
        grad_stacked_ref,
        grad_features_ref,
        {1: transfers.beside_hops},
    )
    transfers.end()


class Transfers:
    def __init__(self, place, gathers, scatters, copies, fill, unpack_head, pack_tail, publish):
        self.place = place
        self.first, *self.attend = gathers[:4]
        self.merge, self.expand, self.reducer = gathers[4:]
        self.middle, self.early, self.late, self.tail = scatters
        self.inputs, self.cotangent, self.output = copies[:2], copies[2], copies[3]
        self.fill = fill
        self.unpack_head, self.pack_tail, self.publish = unpack_head, pack_tail, publish

    def lead(self):
        for copy in (*self.inputs, self.cotangent):
            copy.start()
        self.place.greeted()
        self.first.start()
        self.fill()
        for part in self.attend[:2]:
            part.start()
        for copy in self.inputs:
            copy.wait()

    def head(self, clear):
        queries, keys, values = self.attend
        self.first.forward()
        values.start()
        self.merge.start()
        queries.forward()
        clear()
        self.first.finish()
        keys.forward()
        self.unpack_head()
        values.forward()
        self.expand.start()
        return True

    def beside_embed(self, tile, tiles):
        @pl.when(tile == 2)
        def _():
            self.attend[0].finish()
            self.attend[0].pair().start()

        @pl.when(tile == tiles - 2)
        def _():
            self.attend[1].cross()

        @pl.when(tile == tiles - 1)
        def _():
            self.merge.forward()

    def before_projection(self, kind):
        self.attend[kind].pair().wait()

    def beside_projection(self, kind, pair):
        @pl.when(pair == 0)
        def _():
            if kind == 0:
                self.attend[2].cross()
                self.reducer.start()
            self.attend[kind + 1].finish()
            self.attend[kind + 1].pair().start()

        @pl.when(pair == 1)
        def _():
            if kind == 0:
                self.expand.forward()
            else:
                self.merge.cross()
                self.reducer.forward()

    def beside_attention(self, tile, tiles):
        @pl.when(tile == 1)
        def _():
            self.expand.cross()
            self.merge.finish()
            self.merge.pair().start()

        @pl.when(tile == tiles - 3)
        def _():
            self.reducer.cross()

        @pl.when(tile == tiles - 2)
        def _():
            self.expand.finish()
            self.expand.pair().start()

    def before_merge(self):
        self.merge.pair().wait()
        self.reducer.finish()
        self.reducer.pair().start()

    def before_middle(self):
        self.expand.pair().wait()
        self.reducer.pair().wait()
        self.cotangent.wait()

    def after_middle(self):
        self.middle.begin()
        self.output.start()

    def beside_backward(self, quad, pair, pairs):
        if quad == 0:

            @pl.when(pair == 0)
            def _():
                self.middle.to_plane()

        else:

            @pl.when(pair == 0)
            def _():
                self.early.to_plane()

            @pl.when(pair == pairs - 2)
            def _():
                self.middle.to_line()

    def after_backward(self, quad):
        if quad == 0:
            self.early.begin()
        else:
            self.late.begin()
            self.early.to_line()

    def beside_embed_back(self, pair, pairs):
        @pl.when(pair == 0)
        def _():
            self.late.to_plane()

        @pl.when(pair == 1)
        def _():
            self.middle.to_sibling()

    def after_embed_back(self):
        self.pack_tail()
        self.tail.begin()
        self.early.to_sibling()

    def beside_hops(self):
        self.late.to_line()
        self.tail.to_line()

    def end(self):
        self.tail.to_sibling()
        self.middle.end()
        self.early.end()
        self.late.to_sibling()
        tail = self.tail.end()
        self.late.end()
        self.output.wait()
        self.publish(tail)


def layer_kernel(
    lines,
    counts_ref,
    adjacency_in,
    features_in,
    cotangent_in,
    embed_shard,
    vector_a,
    vector_b,
    vector_c,
    vector_d,
    vector_e,
    attend_shard,
    merge_shard,
    expand_shard,
    reduce_shard,
    output_out,
    grad_features_ref,
    middle_share_ref,
    attend_share_ref,
    tail_share_ref,
    adjacency_ref,
    features_ref,
    cotangent_ref,
    output_ref,
    local,
    *scratch,
):
    keep = scratch[0:10]
    embed_ref, rows_ref, small_keep, head_slots = scratch[10:14]
    attend_slots = scratch[14:17]
    merge_slots, expand_slots, reduce_slots = scratch[17:20]
    grad_embed_ref, rows_keep = scratch[20:22]
    middle_refs, early_refs, late_refs = scratch[22:29], scratch[29:36], scratch[36:43]
    tail_refs = scratch[43:49]
    send, recv, scatter_sems = scratch[49:52]
    owners = lines * PLANE
    width = embed_ref.shape[-1]
    half_width = width // 2
    place = Place(lines)
    core, line, spot = place.core, place.line, place.spot
    place.greet()

    small_keep[...] = jnp.zeros_like(small_keep)
    for index, vector in enumerate((vector_a, vector_b, vector_c, vector_d, vector_e)):
        length = vector.shape[0]
        small_keep[index : index + 1, 0:length] = vector[...].astype(F32).reshape(1, length)
    mine = embed_shard[...].astype(F32)
    packed = jnp.concatenate(
        [
            jnp.concatenate([mine[:, :half_width], small_keep[...]], axis=1),
            jnp.concatenate([mine[:, half_width:], jnp.zeros((8, 128), F32)], axis=1),
        ],
        axis=0,
    )
    head_slots[line, spot] = packed.astype(BF16)

    def half_of(shard):
        rows = shard.shape[0] // 2
        return shard[pl.ds(pl.multiple_of(core * rows, rows), rows)]

    matrices = (merge_slots, expand_slots, reduce_slots)

    def fill():
        whole_attend = half_of(attend_shard)
        for kind, slots in enumerate(attend_slots):
            slots[line, spot, core] = whole_attend[:, kind * width : (kind + 1) * width]
        for slots, shard in zip(matrices, (merge_shard, expand_shard, reduce_shard)):
            slots[line, spot, core] = half_of(shard)

    copies = [
        pltpu.make_async_copy(source, target, local.at[index])
        for index, (source, target) in enumerate(
            (
                (adjacency_in, adjacency_ref),
                (features_in, features_ref),
                (cotangent_in, cotangent_ref),
                (output_ref, output_out),
            )
        )
    ]
    gathers = [
        (CrossGather if index > 1 else Gather)(
            place, slots, send.at[index], recv.at[index], index > 0
        )
        for index, slots in enumerate((head_slots, *attend_slots, *matrices))
    ]
    middle = Scatter(place, *middle_refs, scatter_sems.at[0])
    early = Scatter(place, *early_refs, scatter_sems.at[1])
    late = Scatter(place, *late_refs, scatter_sems.at[2])
    tail = TailScatter(place, *tail_refs, scatter_sems.at[3])

    def unpack_head():
        whole_head = head_slots[...].astype(F32).reshape(owners, 16, half_width + 128)
        top = whole_head[:, 0:8].reshape(owners * 8, half_width + 128)
        bottom = whole_head[:, 8:16].reshape(owners * 8, half_width + 128)
        embed_ref[:, :half_width] = top[:, :half_width].astype(BF16)
        embed_ref[:, half_width:] = bottom[:, :half_width].astype(BF16)
        rows_ref[...] = spread_vectors(top[:, half_width:].astype(BF16), owners, width)

    def pack_tail():
        own = grad_embed_ref[...].reshape(lines, PLANE, 8, width)
        for spot in range(PLANE):
            tail.own[spot, 0:lines] = own[:, spot]
            tail.own[spot, lines] = rows_keep[...]

    def publish(tail_total):
        middle_share_ref[...] = middle.result[...]
        attend_share_ref[0] = early.result[...]
        attend_share_ref[1] = late.result[...]
        tail_share_ref[...] = tail_total

    scatters = (middle, early, late, tail)
    transfers = Transfers(
        place, gathers, scatters, copies, fill, unpack_head, pack_tail, publish
    )
    layer_phases(
        counts_ref,
        adjacency_ref,
        features_ref,
        cotangent_ref,
        rows_ref,
        embed_ref,
        *attend_slots,
        merge_slots,
        expand_slots,
        reduce_slots,
        output_ref,
        grad_features_ref,
        middle.terms,
        early.terms,
        late.terms,
        grad_embed_ref,
        rows_keep,
        keep,
        transfers,
    )


def layer_alone_kernel(*refs):
    layer_phases(*refs[:19], refs[19:], Silent())


def unpack_kernel(
    middle_ref,
    attend_ref,
    tail_ref,
    features_ref,
    nodes_ref,
    output_ref,
    grad_features_ref,
    grad_embed_ref,
    grad_gain_one,
    grad_shift_one,
    grad_attend,
    grad_merge,
    grad_gain_two,
    grad_shift_two,
    grad_expand,
    grad_reduce,
    grad_readout,
):
    owner = lax.axis_index("fsdp")
    width = middle_ref.shape[-1]
    output_ref[...] = nodes_ref[...]
    grad_features_ref[...] = features_ref[...]
    for half in range(2):
        for quad in range(width // QUAD):
            for kind in range(3):
                first = kind * width + quad * QUAD
                grad_attend[half * 16 : half * 16 + 16, first : first + QUAD] = attend_ref[
                    quad, half, :, kind * QUAD : (kind + 1) * QUAD
                ]
        grad_expand[half * 16 : half * 16 + 16, 0:width] = middle_ref[half, 0:16]
        grad_expand[half * 16 : half * 16 + 16, width : 2 * width] = middle_ref[half, 16:32]
        grad_reduce[half * 32 : half * 32 + 32] = middle_ref[half, 32:64]
        grad_merge[half * 16 : half * 16 + 16] = middle_ref[half, 64:80]
    grad_embed_ref[...] = tail_ref[0]
    rows = tail_ref[1]
    length = grad_gain_one.shape[0]
    turned = pltpu.roll(rows, lax.rem(width - owner * length, width), 1)
    for index, ref in enumerate((grad_gain_one, grad_shift_one, grad_gain_two, grad_shift_two)):
        ref[...] = turned[index : index + 1, 0:length].reshape(length)
    length = grad_readout.shape[0]
    first = owner * length
    turned = pltpu.roll(rows, lax.rem(2 * width - first, width), 1)
    row = jnp.where(first < width, turned[4:5, 0:length], turned[5:6, 0:length])
    grad_readout[...] = row.reshape(length)


def sds(shape, dtype):
    return jax.ShapeDtypeStruct(shape, dtype)


SMEM_SPEC = pl.BlockSpec(memory_space=pltpu.SMEM)
VMEM_SPEC = pl.BlockSpec(memory_space=pltpu.VMEM)
ANY_SPEC = pl.BlockSpec(memory_space=pl.ANY)


def layer_keep(tiles, feat, width, spread):
    rows = (HOP_PAIRS, GROUPS, 2 * GROUP)
    return [
        pltpu.VMEM((tiles, *rows, feat), BF16),
        pltpu.VMEM((tiles, TOKENS, width), F32),
        pltpu.VMEM((tiles, TOKENS, width), BF16),
        pltpu.VMEM((tiles, *rows, 3 * width), BF16),
        pltpu.VMEM((tiles, *rows, width), BF16),
        pltpu.VMEM((STREAMS, *rows, QUAD), BF16),
        pltpu.VMEM((width, width), F32),
        pltpu.VMEM((width, spread), F32),
        pltpu.VMEM((spread, width), F32),
        pltpu.VMEM((tiles, HOP_PAIRS, GROUPS, 2, GROUP, feat), F32),
    ]


def layer_part(
    lines, counts, adjacency, features, cotangent, embed, vectors, attend, merge, expand, reducer
):
    nodes, feat = features.shape
    owners = lines * PLANE
    width, spread = expand.shape[0] * owners, expand.shape[1]
    tiles = nodes // NODES_PER_TILE
    rest = (80, width)
    wide = (width // owners // 2, 3 * QUAD)

    def slots(rows, columns):
        return pltpu.VMEM((lines, PLANE, 2, rows // 2, columns), BF16)

    def buffers(shape):
        return [
            pltpu.VMEM((owners, 2) + shape, BF16),
            pltpu.VMEM((owners,) + shape, BF16),
            pltpu.VMEM((lines, PLANE) + shape, BF16),
            pltpu.VMEM((PLANE - 1, lines) + shape, BF16),
            pltpu.VMEM((lines,) + shape, BF16),
            pltpu.VMEM((lines - 1,) + shape, BF16),
            pltpu.VMEM((2,) + shape, F32),
        ]

    outs = [
        cotangent.shape,
        features.shape,
        (2,) + rest,
        (width // QUAD, 2) + wide,
        (2, 8, width),
    ]
    return pl.pallas_call(
        functools.partial(layer_kernel, lines),
        in_specs=[SMEM_SPEC] + [ANY_SPEC] * 3 + [VMEM_SPEC] * 10,
        out_specs=[ANY_SPEC] + [VMEM_SPEC] * 4,
        out_shape=[sds(shape, F32) for shape in outs],
        scratch_shapes=[
            pltpu.VMEM(adjacency.shape, jnp.int32),
            pltpu.VMEM(features.shape, BF16),
            pltpu.VMEM(cotangent.shape, F32),
            pltpu.VMEM(cotangent.shape, F32),
            pltpu.SemaphoreType.DMA((4,)),
        ]
        + layer_keep(tiles, feat, width, spread)
        + [
            pltpu.VMEM((feat, width), BF16),
            pltpu.VMEM((8, width), F32),
            pltpu.VMEM((8, 128), F32),
            pltpu.VMEM((lines, PLANE, 16, width // 2 + 128), BF16),
        ]
        + [slots(attend.shape[0], width)] * 3
        + [slots(*shard.shape) for shard in (merge, expand, reducer)]
        + [pltpu.VMEM((feat, width), F32), pltpu.VMEM((8, width), F32)]
        + buffers(rest)
        + buffers(wide) * 2
        + [
            pltpu.VMEM((PLANE, lines + 1, 8, width), F32),
            pltpu.VMEM((PLANE - 1, lines + 1, 8, width), F32),
            pltpu.VMEM((lines, 2, 8, width), F32),
            pltpu.VMEM((lines - 1, 2, 8, width), F32),
            pltpu.VMEM((2, 8, width), F32),
            pltpu.VMEM((2, 8, width), F32),
        ]
        + [
            pltpu.SemaphoreType.DMA((7, lines + PLANE)),
            pltpu.SemaphoreType.DMA((7, lines + PLANE)),
            pltpu.SemaphoreType.DMA((4, 2, PLANE + lines)),
        ],
        compiler_params=pltpu.CompilerParams(
            vmem_limit_bytes=VMEM_GRANT, collective_id=0, has_side_effects=True
        ),
        name="layer",
    )(counts, adjacency, features, cotangent, embed, *vectors, attend, merge, expand, reducer)


def layer_alone_part(
    counts, adjacency, features, cotangent, rows, embed, attend, merge, expand, reducer
):
    nodes, feat = features.shape
    width, spread = expand.shape
    tiles = nodes // NODES_PER_TILE
    wide = (PACK, 2, width // PACK // 2, 3 * QUAD)
    return pl.pallas_call(
        layer_alone_kernel,
        in_specs=[SMEM_SPEC] + [VMEM_SPEC] * 11,
        out_specs=[VMEM_SPEC] * 7,
        out_shape=[
            sds(cotangent.shape, F32),
            sds(features.shape, F32),
            sds((PACK, 2, 80, width), BF16),
            sds(wide, BF16),
            sds(wide, BF16),
            sds((feat, width), F32),
            sds((8, width), F32),
        ],
        scratch_shapes=layer_keep(tiles, feat, width, spread),
        compiler_params=pltpu.CompilerParams(vmem_limit_bytes=VMEM_GRANT),
        name="layer_alone",
    )(
        counts,
        adjacency,
        features,
        cotangent,
        rows,
        embed,
        attend[:, :width],
        attend[:, width : 2 * width],
        attend[:, 2 * width :],
        merge,
        expand,
        reducer,
    )


def unpack_part(middle, attend, tail, features, nodes, shapes):
    return pl.pallas_call(
        unpack_kernel,
        out_shape=[sds(shape, F32) for shape in [nodes.shape, features.shape] + shapes],
        compiler_params=pltpu.CompilerParams(vmem_limit_bytes=VMEM_GRANT),
        name="unpack_shares",
    )(middle, attend, tail, features, nodes)


def gather(block):
    return lax.all_gather(block, "fsdp", axis=0, tiled=True)


def share(term):
    part = lax.psum_scatter(term.astype(BF16), "fsdp", scatter_dimension=0, tiled=True)
    return lax.psum(part.astype(F32), "grp")


def body(
    features,
    adjacency,
    counts,
    input_weight,
    first_gain,
    first_shift,
    attend_weight,
    merge_weight,
    second_gain,
    second_shift,
    expand_weight,
    reduce_weight,
    readout_weight,
    cotangent,
):
    vectors = (first_gain, first_shift, second_gain, second_shift, readout_weight)
    owners = lax.axis_size("fsdp")
    if owners % PLANE == 0 and input_weight.shape[0] == 8 and attend_weight.shape[0] == 32:
        lines = owners // PLANE
        tiles = cotangent.shape[0] // NODES_PER_TILE
        output, grad_features, *shares = layer_part(
            lines,
            counts,
            adjacency,
            features,
            cotangent.reshape(tiles, NODES_PER_TILE, cotangent.shape[1]),
            input_weight,
            vectors,
            attend_weight,
            merge_weight,
            expand_weight,
            reduce_weight,
        )
        shapes = [
            weight.shape
            for weight in (
                input_weight,
                first_gain,
                first_shift,
                attend_weight,
                merge_weight,
                second_gain,
                second_shift,
                expand_weight,
                reduce_weight,
                readout_weight,
            )
        ]
        return tuple(
            unpack_part(*shares, grad_features, output.reshape(cotangent.shape), shapes)
        )
    return body_apart(
        features,
        adjacency,
        counts,
        input_weight,
        vectors,
        attend_weight,
        merge_weight,
        expand_weight,
        reduce_weight,
        cotangent,
    )


def body_apart(
    features,
    adjacency,
    counts,
    input_weight,
    vectors,
    attend_weight,
    merge_weight,
    expand_weight,
    reduce_weight,
    cotangent,
):
    lengths = [v.shape[0] for v in vectors]
    places = [sum(lengths[:i]) for i in range(len(lengths) + 1)]
    packed = lax.all_gather(jnp.concatenate(vectors), "fsdp", axis=0, tiled=False)
    width = merge_weight.shape[1]
    full = [
        packed[:, places[i] : places[i + 1]].astype(F32).reshape(-1, width)
        for i in range(len(lengths))
    ]
    rows = jnp.concatenate(full + [jnp.zeros((2, width), F32)], axis=0)
    embed, attend, merge, expand, reducer = map(
        gather, (input_weight, attend_weight, merge_weight, expand_weight, reduce_weight)
    )
    tiles = cotangent.shape[0] // NODES_PER_TILE
    output, grad_features, terms, early, late, grad_embed, rows_grad = layer_alone_part(
        counts,
        adjacency,
        features,
        cotangent.reshape(tiles, NODES_PER_TILE, width),
        rows,
        embed,
        attend,
        merge,
        expand,
        reducer,
    )
    grad_attend = jnp.stack([early.reshape(width, 3, QUAD), late.reshape(width, 3, QUAD)], axis=2)
    grad_attend = grad_attend.reshape(width, 3 * width)
    spread = expand.shape[1]
    grad_expand = jnp.concatenate([terms[:, :, 0:16], terms[:, :, 16:32]], axis=-1)
    parts = lax.axis_size("fsdp")
    pieces = [rows_grad[i] for i in range(4)] + [rows_grad[4:6]]
    packed_grad = jnp.concatenate([piece.reshape(parts, -1) for piece in pieces], axis=1)
    packed_grad = lax.psum(
        lax.psum_scatter(packed_grad, "fsdp", scatter_dimension=0, tiled=True), "grp"
    ).reshape(-1)
    small = [packed_grad[places[i] : places[i + 1]] for i in range(len(lengths))]
    return (
        output.reshape(cotangent.shape),
        grad_features,
        share(grad_embed),
        small[0],
        small[1],
        share(grad_attend),
        share(terms[:, :, 64:80].reshape(width, width)),
        small[2],
        small[3],
        share(grad_expand.reshape(width, spread)),
        share(terms[:, :, 32:64].reshape(spread, width)),
        small[4],
    )


def solution(mesh):
    nodes = ("grp", "fsdp")
    rows = P("fsdp", None)
    vector = P("fsdp")
    in_specs = (
        P(nodes, None),
        P(nodes, None, None),
        P(nodes),
        rows,
        vector,
        vector,
        rows,
        rows,
        vector,
        vector,
        rows,
        rows,
        vector,
        P(nodes, None),
    )
    out_specs = (
        P(nodes, None),
        P(nodes, None),
        rows,
        vector,
        vector,
        rows,
        rows,
        vector,
        vector,
        rows,
        rows,
        vector,
    )
    return jax.shard_map(body, mesh=mesh, in_specs=in_specs, out_specs=out_specs, check_vma=False)
```

```python
import functools

import jax
import jax.numpy as jnp
from jax import lax
from jax.experimental import pallas as pl
from jax.experimental.pallas import tpu as pltpu
from jax.sharding import PartitionSpec as P

HEADS = 8
HEAD = 64
HOPS = 7
HOP_TOKENS = HOPS + 1
NODES_PER_TILE = 64
TOKENS = NODES_PER_TILE * HOP_TOKENS
GROUP = 8
STREAMS = 2
FEEDS = 1
SKEW = 1
GROUPS = NODES_PER_TILE // GROUP
HOP_PAIRS = HOP_TOKENS // 2
QUAD = 4 * HEAD
MIB = 1 << 20
VMEM_GRANT = 62 * MIB
F32 = jnp.float32
BF16 = jnp.bfloat16
GELU_A = 0.7978845608028654
GELU_B = 0.044715
LOG2_E = 1.4426950408889634
PLANE = 4
PACK = 16
MESH = pl.DeviceIdType.MESH


def dot(left, right):
    return jnp.dot(left, right, preferred_element_type=F32)


def dot_lead(left, right):
    return lax.dot_general(left, right, (((0,), (0,)), ((), ())), preferred_element_type=F32)


def dot_last(left, right):
    return lax.dot_general(left, right, (((1,), (1,)), ((), ())), preferred_element_type=F32)


def link_of(adjacency, count):
    slots = adjacency.shape[0]
    rows = lax.broadcasted_iota(jnp.int32, (slots, slots), 0)
    cols = lax.broadcasted_iota(jnp.int32, (slots, slots), 1)
    live = jnp.logical_and(rows < count, cols < count)
    link = jnp.where(live, adjacency, 0) + jnp.where(rows == cols, 1, 0)
    link = link.astype(F32)
    root = lax.rsqrt(jnp.sum(link, axis=-1, keepdims=True))
    return link.astype(BF16), root


def hop(link, root, state):
    width = state.shape[1]
    scaled = state * root
    high = scaled.astype(BF16)
    rest = scaled - high.astype(F32)
    middle = rest.astype(BF16)
    low = (rest - middle.astype(F32)).astype(BF16)
    spread = dot(link, jnp.concatenate([high, middle, low], axis=1))
    return (spread[:, :width] + (spread[:, width : 2 * width] + spread[:, 2 * width :])) * root


def live_rows(count, first, rows):
    index = lax.broadcasted_iota(jnp.int32, (rows, 1), 0) + first
    return jnp.where(index < count, 1.0, 0.0).astype(F32)


def norm_stats(values):
    mean = jnp.mean(values, axis=-1, keepdims=True)
    centred = values - mean
    var = jnp.mean(centred * centred, axis=-1, keepdims=True)
    inv = lax.rsqrt(var + 1e-05)
    return centred * inv, inv


def quad_stack(block):
    head = lax.broadcasted_iota(jnp.int32, block.shape, 1) // HEAD
    return jnp.concatenate(
        [jnp.where(head == h, block, jnp.zeros_like(block)) for h in range(4)], axis=0
    )


def grad_softmax(probs, grad_probs):
    tokens, columns = probs.shape
    weighted = (probs * grad_probs).reshape(HOP_TOKENS, GROUP, columns)
    total = jnp.sum(weighted, axis=0)
    shaped = probs.reshape(HOP_TOKENS, GROUP, columns)
    return (weighted - shaped * total[None]).reshape(tokens, columns).astype(BF16)


def quad_probs(scores, scale):
    tokens, columns = scores.shape
    scores = scores.reshape(HOP_TOKENS, GROUP, columns)
    top = jnp.max(scores, axis=0)
    power = jnp.exp2((scores - top[None]) * (scale * LOG2_E))
    row = lax.broadcasted_iota(jnp.int32, (GROUP, columns), 0)
    col = lax.broadcasted_iota(jnp.int32, (GROUP, columns), 1) % GROUP
    share = jnp.where(row == col, 1.0 / jnp.sum(power, axis=0), 0.0)
    return (power * share[None]).reshape(tokens, columns)


def queries_from(weights, block):
    tokens = block.shape[0]
    out = []
    lane = lax.broadcasted_iota(jnp.int32, (tokens, 2 * HEAD), 1)
    for first in (0, 2 * HEAD):
        both = dot_lead(weights[:, first : first + 2 * HEAD], block[:, first : first + 2 * HEAD])
        out.append(jnp.where(lane < HEAD, both[:tokens], both[tokens:]))
    return jnp.concatenate(out, axis=1)


def hop_rows(values, index):
    shaped = values.reshape(HOP_PAIRS, GROUPS, 2, GROUP, values.shape[-1])
    return shaped[index // 2, :, index % 2].reshape(NODES_PER_TILE, values.shape[-1])


def hop_join(parts):
    width = parts[0].shape[-1]
    blocks = []
    for pair in range(HOP_PAIRS):
        both = [parts[2 * pair + k].reshape(GROUPS, 1, GROUP, width) for k in range(2)]
        blocks.append(jnp.concatenate(both, axis=1))
    return jnp.concatenate(blocks, axis=0).reshape(TOKENS, width)


def interleave(streams):
    live = list(enumerate(streams))
    turn = 0
    while live:
        live = [
            (place, stream)
            for place, stream in live
            if turn < place * SKEW or next(stream, live) is not live
        ]
        turn += 1


class Place:
    def __init__(self, lines):
        self.lines = lines
        self.core = lax.axis_index("grp")
        self.owner = lax.axis_index("fsdp")
        self.line = lax.div(self.owner, PLANE)
        self.spot = lax.rem(self.owner, PLANE)

    def line_turn(self, ahead):
        return lax.rem(self.line + ahead + self.lines, self.lines)

    def spot_turn(self, ahead):
        return lax.rem(self.spot + ahead + PLANE, PLANE)

    def line_peer(self, ahead):
        return (self.core, self.line_turn(ahead) * PLANE + self.spot)

    def plane_peer(self, ahead):
        return (self.core, self.line * PLANE + self.spot_turn(ahead))

    def side_peer(self):
        return (self.core, self.owner + 1 - 2 * lax.rem(self.spot, 2))

    def side_spot(self):
        return self.spot + 1 - 2 * lax.rem(self.spot, 2)

    def sibling(self):
        return (1 - self.core, self.owner)

    def peers(self):
        return (
            [self.line_peer(d) for d in range(1, self.lines)]
            + [self.plane_peer(e) for e in range(1, PLANE)]
            + [self.sibling()]
        )

    def greet(self):
        barrier = pltpu.get_barrier_semaphore()
        for peer in self.peers():
            pl.semaphore_signal(barrier, inc=1, device_id=peer, device_id_type=MESH)

    def greeted(self):
        pl.semaphore_wait(pltpu.get_barrier_semaphore(), self.lines + PLANE - 1)


def remote(source, target, send, recv, device):
    return pltpu.make_async_remote_copy(
        src_ref=source,
        dst_ref=target,
        send_sem=send,
        recv_sem=recv,
        device_id=device,
        device_id_type=MESH,
    )


class Gather:
    def __init__(self, place, slots, send, recv, halves):
        self.place, self.slots, self.send, self.recv = place, slots, send, recv
        self.halves = halves

    def slot(self, line, spot):
        if self.halves:
            return self.slots.at[line, spot, self.place.core]
        return self.slots.at[line, spot]

    def line_copies(self):
        place = self.place
        own = self.slot(place.line, place.spot)
        return [
            remote(own, own, self.send.at[d], self.recv.at[d], place.line_peer(d))
            for d in range(1, place.lines)
        ]

    def plane_copies(self):
        place = self.place
        line = self.slot(slice(None), place.spot)
        first = place.lines - 1
        return [
            remote(line, line, self.send.at[first + e], self.recv.at[first + e], place.plane_peer(e))
            for e in range(1, PLANE)
        ]

    def start(self):
        for copy in self.line_copies():
            copy.start()

    def forward(self):
        for copy in self.line_copies():
            copy.wait()
        for copy in self.plane_copies():
            copy.start()

    def finish(self):
        for copy in self.plane_copies():
            copy.wait()

    def pair(self):
        half = self.slots.at[:, :, self.place.core]
        return remote(half, half, self.send.at[0], self.recv.at[0], self.place.sibling())


class CrossGather(Gather):
    def step_copies(self):
        place = self.place
        line = self.slot(slice(None), place.spot)
        first = place.lines
        return [
            remote(line, line, self.send.at[first + k], self.recv.at[first + k], peer)
            for k, peer in enumerate((place.side_peer(), place.plane_peer(2)))
        ]

    def cross_copies(self):
        place = self.place
        first = place.lines + 2
        half = self.slots.shape[-1] // 2
        copies = []
        for k, (spot, peer) in enumerate(
            ((place.side_spot(), place.plane_peer(2)), (place.spot_turn(2), place.side_peer()))
        ):
            part = self.slots.at[:, spot, place.core, :, k * half : (k + 1) * half]
            copies.append(
                remote(part, part, self.send.at[first + k], self.recv.at[first + k], peer)
            )
        return copies

    def forward(self):
        for copy in self.line_copies():
            copy.wait()
        for copy in self.step_copies():
            copy.start()

    def cross(self):
        for copy in self.step_copies():
            copy.wait()
        for copy in self.cross_copies():
            copy.start()

    def finish(self):
        for copy in self.cross_copies():
            copy.wait()


class Scatter:
    def __init__(self, place, terms, got, chip, plane_got, line_out, line_got, result, sems):
        self.place, self.terms, self.got, self.chip = place, terms, got, chip
        self.plane_got, self.line_out, self.line_got = plane_got, line_out, line_got
        self.result, self.sems = result, sems

    def pair(self):
        place = self.place
        return remote(
            self.terms.at[:, 1 - place.core],
            self.got,
            self.sems.at[0, 0],
            self.sems.at[1, 0],
            place.sibling(),
        )

    def plane(self):
        place = self.place
        return [
            remote(
                self.chip.at[:, place.spot_turn(e)],
                self.plane_got.at[e - 1],
                self.sems.at[0, e],
                self.sems.at[1, e],
                place.plane_peer(e),
            )
            for e in range(1, PLANE)
        ]

    def line(self):
        place = self.place
        return [
            remote(
                self.line_out.at[place.line_turn(d)],
                self.line_got.at[d - 1],
                self.sems.at[0, PLANE + d - 1],
                self.sems.at[1, PLANE + d - 1],
                place.line_peer(d),
            )
            for d in range(1, place.lines)
        ]

    def last(self):
        place = self.place
        half = self.result.at[place.core]
        k = PLANE + place.lines - 1
        return remote(half, half, self.sems.at[0, k], self.sems.at[1, k], place.sibling())

    def begin(self):
        self.pair().start()

    def to_plane(self):
        place = self.place
        self.pair().wait()

        def add(line, carry):
            for spot in range(PLANE):
                owner = line * PLANE + spot
                self.chip[line, spot] = self.terms[owner, place.core] + self.got[owner]
            return carry

        lax.fori_loop(0, place.lines, add, 0)
        for copy in self.plane():
            copy.start()

    def to_line(self):
        place = self.place
        for copy in self.plane():
            copy.wait()

        def add(line, carry):
            total = self.chip[line, place.spot].astype(F32)
            for e in range(PLANE - 1):
                total = total + self.plane_got[e, line].astype(F32)
            self.line_out[line] = total.astype(BF16)
            return carry

        lax.fori_loop(0, place.lines, add, 0)
        for copy in self.line():
            copy.start()

    def to_sibling(self):
        place = self.place
        for copy in self.line():
            copy.wait()
        total = self.line_out[place.line].astype(F32)
        for d in range(place.lines - 1):
            total = total + self.line_got[d].astype(F32)
        self.result[place.core] = total
        self.last().start()

    def end(self):
        self.last().wait()


class TailScatter:
    def __init__(self, place, own, plane_got, line_out, line_got, mine, other, sems):
        self.place, self.own, self.plane_got, self.line_out = place, own, plane_got, line_out
        self.line_got, self.mine, self.other, self.sems = line_got, mine, other, sems

    def plane(self):
        place = self.place
        return [
            remote(
                self.own.at[place.spot_turn(e)],
                self.plane_got.at[e - 1],
                self.sems.at[0, e],
                self.sems.at[1, e],
                place.plane_peer(e),
            )
            for e in range(1, PLANE)
        ]

    def line(self):
        place = self.place
        return [
            remote(
                self.line_out.at[place.line_turn(d)],
                self.line_got.at[d - 1],
                self.sems.at[0, PLANE + d - 1],
                self.sems.at[1, PLANE + d - 1],
                place.line_peer(d),
            )
            for d in range(1, place.lines)
        ]

    def last(self):
        return remote(
            self.mine, self.other, self.sems.at[0, 0], self.sems.at[1, 0], self.place.sibling()
        )

    def begin(self):
        for copy in self.plane():
            copy.start()

    def to_line(self):
        place = self.place
        for copy in self.plane():
            copy.wait()
        total = self.own[place.spot].astype(F32)
        for e in range(PLANE - 1):
            total = total + self.plane_got[e].astype(F32)
        total = total.astype(BF16)
        for line in range(place.lines):
            self.line_out[line, 0] = total[line]
            self.line_out[line, 1] = total[place.lines]
        for copy in self.line():
            copy.start()

    def to_sibling(self):
        place = self.place
        for copy in self.line():
            copy.wait()
        total = self.line_out[place.line].astype(F32)
        for d in range(place.lines - 1):
            total = total + self.line_got[d].astype(F32)
        self.mine[...] = total
        self.last().start()

    def end(self):
        self.last().wait()
        return self.mine[...] + self.other[...]


def hop_states(counts_ref, adjacency_ref, features_ref, stacked_ref):
    clusters, slots = adjacency_ref.shape[:2]
    per_cluster = slots // NODES_PER_TILE
    links = []
    states = []
    for cluster in range(clusters):
        count = counts_ref[cluster]
        links.append(link_of(adjacency_ref[cluster], count))
        states.append(
            features_ref[cluster * slots : (cluster + 1) * slots].astype(F32)
            * live_rows(count, 0, slots)
        )
    earlier = [None] * clusters
    for index in range(HOP_TOKENS):
        for cluster in range(clusters):
            if index > 0:
                states[cluster] = hop(*links[cluster], states[cluster])
            if index % 2 == 0:
                earlier[cluster] = states[cluster]
                continue
            for part in range(per_cluster):
                rows = slice(part * NODES_PER_TILE, (part + 1) * NODES_PER_TILE)
                both = [
                    state[rows].reshape(GROUPS, GROUP, state.shape[-1])
                    for state in (earlier[cluster], states[cluster])
                ]
                stacked_ref[cluster * per_cluster + part, index // 2] = jnp.concatenate(
                    both, axis=1
                ).astype(BF16)


def spread_vectors(small, owners, width):
    rows = small.shape[0]
    lane = lax.broadcasted_iota(jnp.int32, (128, width), 0)
    column = lax.broadcasted_iota(jnp.int32, (128, width), 1)
    row = lax.broadcasted_iota(jnp.int32, (rows, width), 0)
    place = lax.broadcasted_iota(jnp.int32, (rows, width), 1)
    piece = width // owners
    pieces = dot(small, jnp.where(lane == column % piece, 1.0, 0.0).astype(BF16))
    out = []
    for vector in range(4):
        mine = jnp.logical_and(row % 8 == vector, lax.div(row, 8) == lax.div(place, piece))
        out.append(jnp.sum(jnp.where(mine, pieces, 0.0), axis=0, keepdims=True))
    pieces = dot(small, jnp.where(lane == column % (2 * piece), 1.0, 0.0).astype(BF16))
    for first in (0, owners // 2):
        owner = lax.div(place, 2 * piece) + first
        mine = jnp.logical_and(row % 8 == 4, lax.div(row, 8) == owner)
        out.append(jnp.sum(jnp.where(mine, pieces, 0.0), axis=0, keepdims=True))
    return jnp.concatenate(out + [jnp.zeros((2, width), F32)], axis=0)


def hop_back(counts_ref, adjacency_ref, grad_stacked_ref, grad_features_ref, between):
    clusters, slots = adjacency_ref.shape[:2]
    feat = grad_features_ref.shape[1]
    rows = TOKENS // HOP_PAIRS
    per_cluster = slots // NODES_PER_TILE
    links = []
    states = []

    def hop_grad(cluster, index):
        return jnp.concatenate(
            [
                grad_stacked_ref[
                    cluster * per_cluster + p, index // 2 * rows : (index // 2 + 1) * rows, 0:feat
                ]
                .reshape(GROUPS, 2, GROUP, feat)[:, index % 2]
                .reshape(NODES_PER_TILE, feat)
                for p in range(per_cluster)
            ],
            axis=0,
        )

    for cluster in range(clusters):
        links.append(link_of(adjacency_ref[cluster], counts_ref[cluster]))
        states.append(hop_grad(cluster, HOPS))
    for index in range(HOPS - 1, -1, -1):
        for cluster in range(clusters):
            states[cluster] = hop_grad(cluster, index) + hop(*links[cluster], states[cluster])
        if index in between:
            between[index]()
    for cluster in range(clusters):
        grad_features_ref[cluster * slots : (cluster + 1) * slots] = states[cluster] * live_rows(
            counts_ref[cluster], 0, slots
        )


def block_of(ref, tile, group, first):
    return ref[tile, :, group, :, first : first + QUAD].reshape(GROUP * HOP_TOKENS, QUAD)


def put_block(ref, tile, group, first, block):
    ref[tile, :, group, :, first : first + QUAD] = block.astype(BF16).reshape(
        HOP_PAIRS, 2 * GROUP, QUAD
    )


def tokens_of(ref, tile):
    return ref[tile].reshape(TOKENS, ref.shape[-1])


def embed_tile(tile, stacked_ref, embed, gain, shift, second_ref, normed_ref):
    hidden = dot(tokens_of(stacked_ref, tile), embed)
    second_ref[tile] = hidden
    normal, _ = norm_stats(hidden)
    normed_ref[tile] = (normal * gain + shift).astype(BF16)


def project_step(first_tile, kind, normed_ref, weight, triple_ref):
    width = normed_ref.shape[-1]
    tiles = pl.ds(first_tile, STREAMS)
    normed = normed_ref[tiles].reshape(STREAMS * TOKENS, width)
    triple_ref[tiles, :, :, :, kind * width : (kind + 1) * width] = (
        dot(normed, weight).astype(BF16).reshape(STREAMS, *triple_ref.shape[1:-1], width)
    )


def attend_tile(tile, normed_ref, value_weight, triple_ref, mixed_ref, probs_ref):
    width = normed_ref.shape[-1]
    triple_ref[tile, :, :, :, 2 * width :] = (
        dot(normed_ref[tile], value_weight).astype(BF16).reshape(*triple_ref.shape[1:-1], width)
    )
    places = [(tile, g, first) for g in range(GROUPS) for first in range(0, width, QUAD)]
    keys = [block_of(triple_ref, t, g, width + first) for t, g, first in places]
    queries = [quad_stack(block_of(triple_ref, *place)) for place in places]
    scores = [dot_last(k, q) for k, q in zip(keys, queries)]
    probs = [quad_probs(score, HEAD ** (-0.5)).astype(BF16) for score in scores]
    values = [block_of(triple_ref, t, g, 2 * width + first) for t, g, first in places]
    blocks = [queries_from(p, v) for p, v in zip(probs, values)]
    for place, block, prob in zip(places, blocks, probs):
        put_block(mixed_ref, *place, block)
        probs_ref[place[2] // QUAD, tile, place[1]] = prob


def middle_step(
    first_tile,
    counts_ref,
    second_ref,
    mixed_ref,
    cotangent_ref,
    rows_ref,
    expand,
    reducer,
    output_ref,
    rows_grad_ref,
    grad_merge_ref,
    grad_expand_ref,
    grad_reduce_ref,
):
    width = second_ref.shape[-1]
    gain, shift = rows_ref[2:3], rows_ref[3:4]
    row_node, row_hop = rows_ref[4:5], rows_ref[5:6]

    def stream(part):
        tile = first_tile + part
        second = second_ref[tile]
        normal, inv = norm_stats(second)
        inner = (normal * gain + shift).astype(BF16)
        yield
        before = dot(inner, expand)
        yield
        square = before * before
        gate = 0.5 + 0.5 * jnp.tanh(before * (square * (GELU_A * GELU_B) + GELU_A))
        gated = before * gate
        after = gated.astype(BF16)
        slope = gate + (gated - gated * gate) * (
            square * (6.0 * GELU_A * GELU_B) + 2.0 * GELU_A
        )
        yield
        third = second + dot(after, reducer)
        yield
        shaped = [hop_rows(third, k) for k in range(HOP_TOKENS)]
        node = tile * NODES_PER_TILE
        keep = live_rows(counts_ref[lax.div(node, 128)], lax.rem(node, 128), NODES_PER_TILE)
        centre = shaped[0]
        base = jnp.sum(centre * row_node, axis=-1, keepdims=True)
        logits = [
            base + jnp.sum(shaped[k] * row_hop, axis=-1, keepdims=True)
            for k in range(1, HOP_TOKENS)
        ]
        top = functools.reduce(jnp.maximum, logits)
        powers = [jnp.exp(logit - top) for logit in logits]
        scale = 1.0 / functools.reduce(jnp.add, powers)
        shares = [power * scale for power in powers]
        total = centre
        for k in range(1, HOP_TOKENS):
            total = total + shares[k - 1] * shaped[k]
        output_ref[tile] = total * keep
        cotangent = cotangent_ref[tile] * keep
        grad_shares = [
            jnp.sum(cotangent * shaped[k], axis=-1, keepdims=True) for k in range(1, HOP_TOKENS)
        ]
        mean_share = functools.reduce(jnp.add, [s * g for s, g in zip(shares, grad_shares)])
        grad_logits = [s * (g - mean_share) for s, g in zip(shares, grad_shares)]
        grad_base = functools.reduce(jnp.add, grad_logits)
        parts = [cotangent + grad_base * row_node]
        read_hop = jnp.zeros((NODES_PER_TILE, width), F32)
        for k in range(1, HOP_TOKENS):
            parts.append(shares[k - 1] * cotangent + grad_logits[k - 1] * row_hop)
            read_hop = read_hop + grad_logits[k - 1] * shaped[k]
        rows_grad_ref[4:5] += jnp.sum(grad_base * centre, axis=0, keepdims=True)
        rows_grad_ref[5:6] += jnp.sum(read_hop, axis=0, keepdims=True)
        grad_third = hop_join(parts)
        grad_branch = grad_third.astype(BF16)
        yield
        grad_after = dot_last(grad_branch, reducer)
        grad_reduce_ref[...] += dot_lead(after, grad_branch)
        yield
        grad_before = (slope * grad_after).astype(BF16)
        yield
        grad_inner = dot_last(grad_before, expand)
        grad_expand_ref[...] += dot_lead(inner, grad_before)
        yield
        rows_grad_ref[2:3] += jnp.sum(grad_inner * normal, axis=0, keepdims=True)
        rows_grad_ref[3:4] += jnp.sum(grad_inner, axis=0, keepdims=True)
        grad_normal = grad_inner * gain
        grad_second = grad_third + inv * (
            grad_normal
            - jnp.mean(grad_normal, axis=-1, keepdims=True)
            - normal * jnp.mean(grad_normal * normal, axis=-1, keepdims=True)
        )
        second_ref[tile] = grad_second
        yield
        grad_merge_ref[...] += dot_lead(tokens_of(mixed_ref, tile), grad_second.astype(BF16))

    interleave([stream(part) for part in range(FEEDS)])


def pack_terms(terms_ref, grad_merge_ref, grad_expand_ref, grad_reduce_ref):
    width, spread = grad_expand_ref.shape
    wide = grad_expand_ref[...].astype(BF16).reshape(PACK, 2, width // PACK // 2, spread)
    deep = grad_reduce_ref[...].astype(BF16).reshape(PACK, 2, spread // PACK // 2, width)
    square = grad_merge_ref[...].astype(BF16).reshape(PACK, 2, width // PACK // 2, width)
    terms_ref[:, :, 0:16] = wide[..., :width]
    terms_ref[:, :, 16:32] = wide[..., width:]
    terms_ref[:, :, 32:64] = deep
    terms_ref[:, :, 64:80] = square


def attend_back_step(
    quad,
    first_tile,
    triple_ref,
    probs_ref,
    second_ref,
    normed_ref,
    merge,
    grad_mixed_ref,
    grad_attend_ref,
):
    width = normed_ref.shape[-1]
    for part in range(STREAMS):
        grad_mixed = dot_last(second_ref[first_tile + part].astype(BF16), merge).astype(BF16)
        grad_mixed_ref[part, :, :, :, 0:QUAD] = grad_mixed.reshape(
            *grad_mixed_ref.shape[1:-1], QUAD
        )
    places = [(part, group) for part in range(STREAMS) for group in range(GROUPS)]
    scale = jnp.asarray(HEAD ** (-0.5), BF16)
    starts = [kind * width + quad * QUAD for kind in range(3)]

    def read(kind):
        return [block_of(triple_ref, first_tile + p, g, starts[kind]) for p, g in places]

    keys = read(1)
    queries = [quad_stack(block * scale) for block in read(0)]
    probs = [probs_ref[quad, first_tile + part, group] for part, group in places]
    values = read(2)
    out_grads = [quad_stack(block_of(grad_mixed_ref, p, g, 0)) for p, g in places]
    grad_probs = [dot_last(v, o) for v, o in zip(values, out_grads)]
    grad_scores = [grad_softmax(p.astype(F32), g) for p, g in zip(probs, grad_probs)]
    grad_values = [dot(p, o) for p, o in zip(probs, out_grads)]
    grad_keys = [dot(s, q) for s, q in zip(grad_scores, queries)]
    grad_queries = [queries_from(s, k * scale) for s, k in zip(grad_scores, keys)]
    for (part, group), a, b, c in zip(places, grad_queries, grad_keys, grad_values):
        for start, block in zip(starts, (a, b, c)):
            put_block(triple_ref, first_tile + part, group, start, block)
    tiles = pl.ds(first_tile, STREAMS)
    grads = jnp.concatenate(
        [
            triple_ref[tiles, :, :, :, start : start + QUAD].reshape(STREAMS * TOKENS, QUAD)
            for start in starts
        ],
        axis=1,
    )
    grad_attend_ref[:, 0 : 3 * QUAD] += dot_lead(
        normed_ref[tiles].reshape(STREAMS * TOKENS, width), grads
    )


def embed_back_step(
    first_tile,
    stacked_ref,
    second_ref,
    triple_ref,
    attend,
    embed,
    gain,
    rows_keep,
    grad_embed_ref,
    normed_ref,
):
    def stream(part):
        tile = first_tile + part
        stacked = tokens_of(stacked_ref, tile)
        grad_normed = dot_last(tokens_of(triple_ref, tile), attend)
        hidden = dot(stacked, embed)
        yield
        normal, inv = norm_stats(hidden)
        rows_keep[0:1] += jnp.sum(grad_normed * normal, axis=0, keepdims=True)
        rows_keep[1:2] += jnp.sum(grad_normed, axis=0, keepdims=True)
        grad_normal = grad_normed * gain
        grad_hidden = second_ref[tile] + inv * (
            grad_normal
            - jnp.mean(grad_normal, axis=-1, keepdims=True)
            - normal * jnp.mean(grad_normal * normal, axis=-1, keepdims=True)
        )
        grad_hidden = grad_hidden.astype(BF16)
        yield
        grad_embed_ref[...] += dot_lead(stacked, grad_hidden)
        normed_ref[tile] = grad_hidden

    interleave([stream(part) for part in range(STREAMS)])


class Silent:
    def __getattr__(self, name):
        return lambda *arguments: None


def loop(count, step):
    def body(index, carry):
        step(index)
        return carry

    lax.fori_loop(0, count, body, 0)


def layer_phases(
    counts_ref,
    adjacency_ref,
    features_ref,
    cotangent_ref,
    rows_ref,
    embed_ref,
    query_ref,
    key_ref,
    value_ref,
    merge_ref,
    expand_ref,
    reduce_ref,
    output_ref,
    grad_features_ref,
    terms_ref,
    early_terms,
    late_terms,
    grad_embed_ref,
    rows_keep,
    keep,
    transfers,
):
    (
        stacked_ref,
        second_ref,
        normed_ref,
        triple_ref,
        mixed_ref,
        grad_merge_ref,
        grad_expand_ref,
        grad_reduce_ref,
        probs_ref,
    ) = keep
    tiles, _, width = second_ref.shape
    pairs = tiles // STREAMS
    sums = (grad_merge_ref, grad_expand_ref, grad_reduce_ref)

    def clear():
        for ref in (rows_keep, grad_embed_ref, *sums):
            ref[...] = jnp.zeros_like(ref)

    transfers.lead()
    hop_states(counts_ref, adjacency_ref, features_ref, stacked_ref)
    if not transfers.head(clear):
        clear()

    def embed_step(tile):
        embed_tile(
            tile, stacked_ref, embed_ref[...], rows_ref[0:1], rows_ref[1:2], second_ref, normed_ref
        )
        transfers.beside_embed(tile, tiles)

    loop(tiles, embed_step)
    for kind, weight_ref in enumerate((query_ref, key_ref)):
        transfers.before_projection(kind)

        def project(pair, kind=kind, weight_ref=weight_ref):
            weight = weight_ref[...].reshape(width, width)
            project_step(pair * STREAMS, kind, normed_ref, weight, triple_ref)
            transfers.beside_projection(kind, pair)

        loop(pairs, project)
    transfers.before_projection(2)

    def attend_step(tile):
        attend_tile(
            tile,
            normed_ref,
            value_ref[...].reshape(width, width),
            triple_ref,
            mixed_ref,
            probs_ref,
        )
        transfers.beside_attention(tile, tiles)

    loop(tiles, attend_step)
    transfers.before_merge()

    def merge_step(pair):
        mixed = mixed_ref[pl.ds(pair * STREAMS, STREAMS)].reshape(STREAMS * TOKENS, width)
        second_ref[pl.ds(pair * STREAMS, STREAMS)] += dot(
            mixed, merge_ref[...].reshape(width, width)
        ).reshape(STREAMS, TOKENS, width)

    loop(pairs, merge_step)
    transfers.before_middle()
    spread = grad_expand_ref.shape[1]

    def feed_step(pair):
        middle_step(
            pair * FEEDS,
            counts_ref,
            second_ref,
            mixed_ref,
            cotangent_ref,
            rows_ref,
            expand_ref[...].reshape(width, spread),
            reduce_ref[...].reshape(spread, width),
            output_ref,
            rows_keep,
            grad_merge_ref,
            grad_expand_ref,
            grad_reduce_ref,
        )

    loop(tiles // FEEDS, feed_step)
    pack_terms(terms_ref, grad_merge_ref, grad_expand_ref, grad_reduce_ref)
    transfers.after_middle()
    grad_attend_ref = grad_expand_ref
    for quad, terms in enumerate((early_terms, late_terms)):
        grad_attend_ref[...] = jnp.zeros_like(grad_attend_ref)

        def back_step(pair, quad=quad):
            attend_back_step(
                quad,
                pair * STREAMS,
                triple_ref,
                probs_ref,
                second_ref,
                normed_ref,
                merge_ref[...].reshape(width, width)[quad * QUAD : (quad + 1) * QUAD],
                mixed_ref,
                grad_attend_ref,
            )
            transfers.beside_backward(quad, pair, pairs)

        loop(pairs, back_step)
        terms[...] = grad_attend_ref[:, 0 : 3 * QUAD].astype(BF16).reshape(terms.shape)
        transfers.after_backward(quad)

    def embed_back(pair):
        embed_back_step(
            pair * STREAMS,
            stacked_ref,
            second_ref,
            triple_ref,
            jnp.concatenate(
                [ref[...].reshape(width, width) for ref in (query_ref, key_ref, value_ref)], axis=1
            ),
            embed_ref[...],
            rows_ref[0:1],
            rows_keep,
            grad_embed_ref,
            normed_ref,
        )
        transfers.beside_embed_back(pair, pairs)

    loop(pairs, embed_back)
    transfers.after_embed_back()

    def stacked_back(pair):
        grad_hidden = normed_ref[pl.ds(pair * STREAMS, STREAMS)].reshape(STREAMS * TOKENS, width)
        second_ref[pl.ds(pair * STREAMS, STREAMS), :, 0 : embed_ref.shape[0]] = dot_last(
            grad_hidden, embed_ref[...]
        ).reshape(STREAMS, TOKENS, embed_ref.shape[0])

    loop(pairs, stacked_back)
    hop_back(
        counts_ref,
        adjacency_ref,
        second_ref,
        grad_features_ref,
        {1: transfers.beside_hops},
    )
    transfers.end()


class Transfers:
    def __init__(self, place, gathers, scatters, copies, fill, unpack_head, pack_tail, publish):
        self.place = place
        self.first, *self.attend = gathers[:4]
        self.merge, self.expand, self.reducer = gathers[4:]
        self.middle, self.early, self.late, self.tail = scatters
        self.inputs, self.cotangent, self.output = copies[:2], copies[2], copies[3]
        self.fill = fill
        self.unpack_head, self.pack_tail, self.publish = unpack_head, pack_tail, publish

    def lead(self):
        for copy in (*self.inputs, self.cotangent):
            copy.start()
        self.place.greeted()
        self.first.start()
        self.fill()
        for part in self.attend[:2]:
            part.start()
        for copy in self.inputs:
            copy.wait()

    def head(self, clear):
        queries, keys, values = self.attend
        self.first.forward()
        values.start()
        self.merge.start()
        queries.forward()
        clear()
        self.first.finish()
        keys.forward()
        self.unpack_head()
        values.forward()
        self.expand.start()
        return True

    def beside_embed(self, tile, tiles):
        @pl.when(tile == 2)
        def _():
            self.attend[0].finish()
            self.attend[0].pair().start()

        @pl.when(tile == tiles - 2)
        def _():
            self.attend[1].cross()

        @pl.when(tile == tiles - 1)
        def _():
            self.merge.forward()

    def before_projection(self, kind):
        self.attend[kind].pair().wait()

    def beside_projection(self, kind, pair):
        @pl.when(pair == 0)
        def _():
            if kind == 0:
                self.attend[2].cross()
                self.reducer.start()
            self.attend[kind + 1].finish()
            self.attend[kind + 1].pair().start()

        @pl.when(pair == 1)
        def _():
            if kind == 0:
                self.expand.forward()
            else:
                self.merge.cross()
                self.reducer.forward()

    def beside_attention(self, tile, tiles):
        @pl.when(tile == 1)
        def _():
            self.expand.cross()
            self.merge.finish()
            self.merge.pair().start()

        @pl.when(tile == tiles - 3)
        def _():
            self.reducer.cross()

        @pl.when(tile == tiles - 2)
        def _():
            self.expand.finish()
            self.expand.pair().start()

    def before_merge(self):
        self.merge.pair().wait()
        self.reducer.finish()
        self.reducer.pair().start()

    def before_middle(self):
        self.expand.pair().wait()
        self.reducer.pair().wait()
        self.cotangent.wait()

    def after_middle(self):
        self.middle.begin()
        self.output.start()

    def beside_backward(self, quad, pair, pairs):
        if quad == 0:

            @pl.when(pair == 0)
            def _():
                self.middle.to_plane()

        else:

            @pl.when(pair == 0)
            def _():
                self.early.to_plane()

            @pl.when(pair == pairs - 2)
            def _():
                self.middle.to_line()

    def after_backward(self, quad):
        if quad == 0:
            self.early.begin()
        else:
            self.late.begin()
            self.early.to_line()

    def beside_embed_back(self, pair, pairs):
        @pl.when(pair == 0)
        def _():
            self.late.to_plane()

        @pl.when(pair == 1)
        def _():
            self.middle.to_sibling()

    def after_embed_back(self):
        self.pack_tail()
        self.tail.begin()
        self.early.to_sibling()

    def beside_hops(self):
        self.late.to_line()
        self.tail.to_line()

    def end(self):
        self.tail.to_sibling()
        self.middle.end()
        self.early.end()
        self.late.to_sibling()
        tail = self.tail.end()
        self.late.end()
        self.output.wait()
        self.publish(tail)


def fold(block):
    half = block.shape[-1] // 2
    return jnp.concatenate([block[..., :half], block[..., half:]], axis=-2)


def layer_kernel(
    lines,
    counts_ref,
    adjacency_in,
    features_in,
    cotangent_in,
    embed_shard,
    vector_a,
    vector_b,
    vector_c,
    vector_d,
    vector_e,
    attend_shard,
    merge_shard,
    expand_shard,
    reduce_shard,
    output_out,
    grad_features_ref,
    middle_share_ref,
    attend_share_ref,
    tail_share_ref,
    adjacency_ref,
    features_ref,
    cotangent_ref,
    output_ref,
    local,
    *scratch,
):
    keep = scratch[0:9]
    scratch = scratch[9:]
    embed_ref, rows_ref, small_keep, head_slots = scratch[0:4]
    attend_slots = scratch[4:7]
    merge_slots, expand_slots, reduce_slots = scratch[7:10]
    grad_embed_ref, rows_keep = scratch[10:12]
    middle_refs, early_refs, late_refs = scratch[12:19], scratch[19:26], scratch[26:33]
    tail_refs = scratch[33:39]
    send, recv, scatter_sems = scratch[39:42]
    owners = lines * PLANE
    width = embed_ref.shape[-1]
    half_width = width // 2
    place = Place(lines)
    core, line, spot = place.core, place.line, place.spot
    place.greet()

    small_keep[...] = jnp.zeros_like(small_keep)
    for index, vector in enumerate((vector_a, vector_b, vector_c, vector_d, vector_e)):
        length = vector.shape[0]
        small_keep[index : index + 1, 0:length] = vector[...].astype(F32).reshape(1, length)
    mine = embed_shard[...].astype(F32)
    packed = jnp.concatenate(
        [
            jnp.concatenate([mine[:, :half_width], small_keep[...]], axis=1),
            jnp.concatenate([mine[:, half_width:], jnp.zeros((8, 128), F32)], axis=1),
        ],
        axis=0,
    )
    head_slots[line, spot] = packed.astype(BF16)

    def half_of(shard):
        rows = shard.shape[0] // 2
        return shard[pl.ds(pl.multiple_of(core * rows, rows), rows)]

    matrices = (merge_slots, expand_slots, reduce_slots)

    def fill():
        whole_attend = half_of(attend_shard)
        for kind, slots in enumerate(attend_slots):
            slots[line, spot, core] = whole_attend[:, kind * width : (kind + 1) * width]
        for slots, shard in zip(matrices, (merge_shard, expand_shard, reduce_shard)):
            slots[line, spot, core] = half_of(shard)

    copies = [
        pltpu.make_async_copy(source, target, local.at[index])
        for index, (source, target) in enumerate(
            (
                (adjacency_in, adjacency_ref),
                (features_in, features_ref),
                (cotangent_in, cotangent_ref),
                (output_ref, output_out),
            )
        )
    ]
    gathers = [
        (CrossGather if index > 1 else Gather)(
            place, slots, send.at[index], recv.at[index], index > 0
        )
        for index, slots in enumerate((head_slots, *attend_slots, *matrices))
    ]
    middle = Scatter(place, *middle_refs, scatter_sems.at[0])
    early = Scatter(place, *early_refs, scatter_sems.at[1])
    late = Scatter(place, *late_refs, scatter_sems.at[2])
    tail = TailScatter(place, *tail_refs, scatter_sems.at[3])

    def unpack_head():
        whole_head = head_slots[...].astype(F32).reshape(owners, 16, half_width + 128)
        top = whole_head[:, 0:8].reshape(owners * 8, half_width + 128)
        bottom = whole_head[:, 8:16].reshape(owners * 8, half_width + 128)
        embed_ref[:, :half_width] = top[:, :half_width].astype(BF16)
        embed_ref[:, half_width:] = bottom[:, :half_width].astype(BF16)
        rows_ref[...] = spread_vectors(top[:, half_width:].astype(BF16), owners, width)

    def pack_tail():
        own = fold(grad_embed_ref[...].reshape(owners, 8, width)).astype(BF16)
        own = own.reshape(lines, PLANE, 16, half_width)
        rows = fold(rows_keep[...].reshape(1, 8, width))[0].astype(BF16)
        for peer_spot in range(PLANE):
            tail.own[peer_spot, 0:lines] = own[:, peer_spot]
            tail.own[peer_spot, lines] = rows

    def publish(tail_total):
        middle_share_ref[...] = middle.result[...]
        attend_share_ref[0] = early.result[...]
        attend_share_ref[1] = late.result[...]
        tail_share_ref[...] = tail_total

    scatters = (middle, early, late, tail)
    transfers = Transfers(
        place, gathers, scatters, copies, fill, unpack_head, pack_tail, publish
    )
    layer_phases(
        counts_ref,
        adjacency_ref,
        features_ref,
        cotangent_ref,
        rows_ref,
        embed_ref,
        *attend_slots,
        merge_slots,
        expand_slots,
        reduce_slots,
        output_ref,
        grad_features_ref,
        middle.terms,
        early.terms,
        late.terms,
        grad_embed_ref,
        rows_keep,
        keep,
        transfers,
    )


def layer_alone_kernel(*refs):
    layer_phases(*refs[:19], refs[19:], Silent())


def unpack_kernel(
    middle_ref,
    attend_ref,
    tail_ref,
    features_ref,
    nodes_ref,
    output_ref,
    grad_features_ref,
    grad_embed_ref,
    grad_gain_one,
    grad_shift_one,
    grad_attend,
    grad_merge,
    grad_gain_two,
    grad_shift_two,
    grad_expand,
    grad_reduce,
    grad_readout,
):
    owner = lax.axis_index("fsdp")
    width = middle_ref.shape[-1]
    output_ref[...] = nodes_ref[...]
    grad_features_ref[...] = features_ref[...]
    for half in range(2):
        for quad in range(width // QUAD):
            for kind in range(3):
                first = kind * width + quad * QUAD
                grad_attend[half * 16 : half * 16 + 16, first : first + QUAD] = attend_ref[
                    quad, half, :, kind * QUAD : (kind + 1) * QUAD
                ]
        grad_expand[half * 16 : half * 16 + 16, 0:width] = middle_ref[half, 0:16]
        grad_expand[half * 16 : half * 16 + 16, width : 2 * width] = middle_ref[half, 16:32]
        grad_reduce[half * 32 : half * 32 + 32] = middle_ref[half, 32:64]
        grad_merge[half * 16 : half * 16 + 16] = middle_ref[half, 64:80]
    grad_embed_ref[...] = jnp.concatenate([tail_ref[0, 0:8], tail_ref[0, 8:16]], axis=1)
    rows = jnp.concatenate([tail_ref[1, 0:8], tail_ref[1, 8:16]], axis=1)
    length = grad_gain_one.shape[0]
    turned = pltpu.roll(rows, lax.rem(width - owner * length, width), 1)
    for index, ref in enumerate((grad_gain_one, grad_shift_one, grad_gain_two, grad_shift_two)):
        ref[...] = turned[index : index + 1, 0:length].reshape(length)
    length = grad_readout.shape[0]
    first = owner * length
    turned = pltpu.roll(rows, lax.rem(2 * width - first, width), 1)
    row = jnp.where(first < width, turned[4:5, 0:length], turned[5:6, 0:length])
    grad_readout[...] = row.reshape(length)


def sds(shape, dtype):
    return jax.ShapeDtypeStruct(shape, dtype)


SMEM_SPEC = pl.BlockSpec(memory_space=pltpu.SMEM)
VMEM_SPEC = pl.BlockSpec(memory_space=pltpu.VMEM)
ANY_SPEC = pl.BlockSpec(memory_space=pl.ANY)


def layer_keep(tiles, feat, width, spread):
    rows = (HOP_PAIRS, GROUPS, 2 * GROUP)
    return [
        pltpu.VMEM((tiles, *rows, feat), BF16),
        pltpu.VMEM((tiles, TOKENS, width), F32),
        pltpu.VMEM((tiles, TOKENS, width), BF16),
        pltpu.VMEM((tiles, *rows, 3 * width), BF16),
        pltpu.VMEM((tiles, *rows, width), BF16),
        pltpu.VMEM((width, width), F32),
        pltpu.VMEM((width, spread), F32),
        pltpu.VMEM((spread, width), F32),
        pltpu.VMEM((width // QUAD, tiles, GROUPS, GROUP * HOP_TOKENS, QUAD), BF16),
    ]


def layer_part(
    lines, counts, adjacency, features, cotangent, embed, vectors, attend, merge, expand, reducer
):
    nodes, feat = features.shape
    owners = lines * PLANE
    width, spread = expand.shape[0] * owners, expand.shape[1]
    tiles = nodes // NODES_PER_TILE
    rest = (80, width)
    wide = (width // owners // 2, 3 * QUAD)

    def slots(rows, columns):
        return pltpu.VMEM((lines, PLANE, 2, rows // 2, columns), BF16)

    def buffers(shape):
        return [
            pltpu.VMEM((owners, 2) + shape, BF16),
            pltpu.VMEM((owners,) + shape, BF16),
            pltpu.VMEM((lines, PLANE) + shape, BF16),
            pltpu.VMEM((PLANE - 1, lines) + shape, BF16),
            pltpu.VMEM((lines,) + shape, BF16),
            pltpu.VMEM((lines - 1,) + shape, BF16),
            pltpu.VMEM((2,) + shape, F32),
        ]

    outs = [
        cotangent.shape,
        features.shape,
        (2,) + rest,
        (width // QUAD, 2) + wide,
        (2, 16, width // 2),
    ]
    return pl.pallas_call(
        functools.partial(layer_kernel, lines),
        in_specs=[SMEM_SPEC] + [ANY_SPEC] * 3 + [VMEM_SPEC] * 10,
        out_specs=[ANY_SPEC] + [VMEM_SPEC] * 4,
        out_shape=[sds(shape, F32) for shape in outs],
        scratch_shapes=[
            pltpu.VMEM(adjacency.shape, jnp.int32),
            pltpu.VMEM(features.shape, BF16),
            pltpu.VMEM(cotangent.shape, F32),
            pltpu.VMEM(cotangent.shape, F32),
            pltpu.SemaphoreType.DMA((4,)),
        ]
        + layer_keep(tiles, feat, width, spread)
        + [
            pltpu.VMEM((feat, width), BF16),
            pltpu.VMEM((8, width), F32),
            pltpu.VMEM((8, 128), F32),
            pltpu.VMEM((lines, PLANE, 16, width // 2 + 128), BF16),
        ]
        + [slots(attend.shape[0], width)] * 3
        + [slots(*shard.shape) for shard in (merge, expand, reducer)]
        + [pltpu.VMEM((feat, width), F32), pltpu.VMEM((8, width), F32)]
        + buffers(rest)
        + buffers(wide) * 2
        + [
            pltpu.VMEM((PLANE, lines + 1, 16, width // 2), BF16),
            pltpu.VMEM((PLANE - 1, lines + 1, 16, width // 2), BF16),
            pltpu.VMEM((lines, 2, 16, width // 2), BF16),
            pltpu.VMEM((lines - 1, 2, 16, width // 2), BF16),
            pltpu.VMEM((2, 16, width // 2), F32),
            pltpu.VMEM((2, 16, width // 2), F32),
        ]
        + [
            pltpu.SemaphoreType.DMA((7, lines + PLANE)),
            pltpu.SemaphoreType.DMA((7, lines + PLANE)),
            pltpu.SemaphoreType.DMA((4, 2, PLANE + lines)),
        ],
        compiler_params=pltpu.CompilerParams(
            vmem_limit_bytes=VMEM_GRANT, collective_id=0, has_side_effects=True
        ),
        name="layer",
    )(counts, adjacency, features, cotangent, embed, *vectors, attend, merge, expand, reducer)


def layer_alone_part(
    counts, adjacency, features, cotangent, rows, embed, attend, merge, expand, reducer
):
    nodes, feat = features.shape
    width, spread = expand.shape
    tiles = nodes // NODES_PER_TILE
    wide = (PACK, 2, width // PACK // 2, 3 * QUAD)
    return pl.pallas_call(
        layer_alone_kernel,
        in_specs=[SMEM_SPEC] + [VMEM_SPEC] * 11,
        out_specs=[VMEM_SPEC] * 7,
        out_shape=[
            sds(cotangent.shape, F32),
            sds(features.shape, F32),
            sds((PACK, 2, 80, width), BF16),
            sds(wide, BF16),
            sds(wide, BF16),
            sds((feat, width), F32),
            sds((8, width), F32),
        ],
        scratch_shapes=layer_keep(tiles, feat, width, spread),
        compiler_params=pltpu.CompilerParams(vmem_limit_bytes=VMEM_GRANT),
        name="layer_alone",
    )(
        counts,
        adjacency,
        features,
        cotangent,
        rows,
        embed,
        attend[:, :width],
        attend[:, width : 2 * width],
        attend[:, 2 * width :],
        merge,
        expand,
        reducer,
    )


def unpack_part(middle, attend, tail, features, nodes, shapes):
    return pl.pallas_call(
        unpack_kernel,
        out_shape=[sds(shape, F32) for shape in [nodes.shape, features.shape] + shapes],
        compiler_params=pltpu.CompilerParams(vmem_limit_bytes=VMEM_GRANT),
        name="unpack_shares",
    )(middle, attend, tail, features, nodes)


def gather(block):
    return lax.all_gather(block, "fsdp", axis=0, tiled=True)


def share(term):
    part = lax.psum_scatter(term.astype(BF16), "fsdp", scatter_dimension=0, tiled=True)
    return lax.psum(part.astype(F32), "grp")


def body(
    features,
    adjacency,
    counts,
    input_weight,
    first_gain,
    first_shift,
    attend_weight,
    merge_weight,
    second_gain,
    second_shift,
    expand_weight,
    reduce_weight,
    readout_weight,
    cotangent,
):
    vectors = (first_gain, first_shift, second_gain, second_shift, readout_weight)
    owners = lax.axis_size("fsdp")
    if owners % PLANE == 0 and input_weight.shape[0] == 8 and attend_weight.shape[0] == 32:
        lines = owners // PLANE
        tiles = cotangent.shape[0] // NODES_PER_TILE
        output, grad_features, *shares = layer_part(
            lines,
            counts,
            adjacency,
            features,
            cotangent.reshape(tiles, NODES_PER_TILE, cotangent.shape[1]),
            input_weight,
            vectors,
            attend_weight,
            merge_weight,
            expand_weight,
            reduce_weight,
        )
        shapes = [
            weight.shape
            for weight in (
                input_weight,
                first_gain,
                first_shift,
                attend_weight,
                merge_weight,
                second_gain,
                second_shift,
                expand_weight,
                reduce_weight,
                readout_weight,
            )
        ]
        return tuple(
            unpack_part(*shares, grad_features, output.reshape(cotangent.shape), shapes)
        )
    return body_apart(
        features,
        adjacency,
        counts,
        input_weight,
        vectors,
        attend_weight,
        merge_weight,
        expand_weight,
        reduce_weight,
        cotangent,
    )


def body_apart(
    features,
    adjacency,
    counts,
    input_weight,
    vectors,
    attend_weight,
    merge_weight,
    expand_weight,
    reduce_weight,
    cotangent,
):
    lengths = [v.shape[0] for v in vectors]
    places = [sum(lengths[:i]) for i in range(len(lengths) + 1)]
    packed = lax.all_gather(jnp.concatenate(vectors), "fsdp", axis=0, tiled=False)
    width = merge_weight.shape[1]
    full = [
        packed[:, places[i] : places[i + 1]].astype(F32).reshape(-1, width)
        for i in range(len(lengths))
    ]
    rows = jnp.concatenate(full + [jnp.zeros((2, width), F32)], axis=0)
    embed, attend, merge, expand, reducer = map(
        gather, (input_weight, attend_weight, merge_weight, expand_weight, reduce_weight)
    )
    tiles = cotangent.shape[0] // NODES_PER_TILE
    output, grad_features, terms, early, late, grad_embed, rows_grad = layer_alone_part(
        counts,
        adjacency,
        features,
        cotangent.reshape(tiles, NODES_PER_TILE, width),
        rows,
        embed,
        attend,
        merge,
        expand,
        reducer,
    )
    grad_attend = jnp.stack([early.reshape(width, 3, QUAD), late.reshape(width, 3, QUAD)], axis=2)
    grad_attend = grad_attend.reshape(width, 3 * width)
    spread = expand.shape[1]
    grad_expand = jnp.concatenate([terms[:, :, 0:16], terms[:, :, 16:32]], axis=-1)
    parts = lax.axis_size("fsdp")
    pieces = [rows_grad[i] for i in range(4)] + [rows_grad[4:6]]
    packed_grad = jnp.concatenate([piece.reshape(parts, -1) for piece in pieces], axis=1)
    packed_grad = lax.psum(
        lax.psum_scatter(packed_grad, "fsdp", scatter_dimension=0, tiled=True), "grp"
    ).reshape(-1)
    small = [packed_grad[places[i] : places[i + 1]] for i in range(len(lengths))]
    return (
        output.reshape(cotangent.shape),
        grad_features,
        share(grad_embed),
        small[0],
        small[1],
        share(grad_attend),
        share(terms[:, :, 64:80].reshape(width, width)),
        small[2],
        small[3],
        share(grad_expand.reshape(width, spread)),
        share(terms[:, :, 32:64].reshape(spread, width)),
        small[4],
    )


def solution(mesh):
    nodes = ("grp", "fsdp")
    rows = P("fsdp", None)
    vector = P("fsdp")
    in_specs = (
        P(nodes, None),
        P(nodes, None, None),
        P(nodes),
        rows,
        vector,
        vector,
        rows,
        rows,
        vector,
        vector,
        rows,
        rows,
        vector,
        P(nodes, None),
    )
    out_specs = (
        P(nodes, None),
        P(nodes, None),
        rows,
        vector,
        vector,
        rows,
        rows,
        vector,
        vector,
        rows,
        rows,
        vector,
    )
    return jax.shard_map(body, mesh=mesh, in_specs=in_specs, out_specs=out_specs, check_vma=False)
```

```python
import functools

import jax
import jax.numpy as jnp
from jax import lax
from jax.experimental import pallas as pl
from jax.experimental.pallas import tpu as pltpu
from jax.sharding import PartitionSpec as P

HEADS = 8
HEAD = 64
HOPS = 7
HOP_TOKENS = HOPS + 1
NODES_PER_TILE = 64
TOKENS = NODES_PER_TILE * HOP_TOKENS
GROUP = 8
STREAMS = 2
FEEDS = 1
SKEW = 0
GROUPS = NODES_PER_TILE // GROUP
HOP_PAIRS = HOP_TOKENS // 2
QUAD = 4 * HEAD
MIB = 1 << 20
VMEM_GRANT = 62 * MIB
F32 = jnp.float32
BF16 = jnp.bfloat16
GELU_A = 0.7978845608028654
GELU_B = 0.044715
LOG2_E = 1.4426950408889634
PLANE = 4
PACK = 16
MESH = pl.DeviceIdType.MESH


def dot(left, right):
    return jnp.dot(left, right, preferred_element_type=F32)


def dot_lead(left, right):
    return lax.dot_general(left, right, (((0,), (0,)), ((), ())), preferred_element_type=F32)


def dot_last(left, right):
    return lax.dot_general(left, right, (((1,), (1,)), ((), ())), preferred_element_type=F32)


def link_of(adjacency, count):
    slots = adjacency.shape[0]
    rows = lax.broadcasted_iota(jnp.int32, (slots, slots), 0)
    cols = lax.broadcasted_iota(jnp.int32, (slots, slots), 1)
    live = jnp.logical_and(rows < count, cols < count)
    link = jnp.where(live, adjacency, 0) + jnp.where(rows == cols, 1, 0)
    link = link.astype(F32)
    root = lax.rsqrt(jnp.sum(link, axis=-1, keepdims=True))
    return link.astype(BF16), root


def hop(link, root, state):
    width = state.shape[1]
    scaled = state * root
    high = scaled.astype(BF16)
    rest = scaled - high.astype(F32)
    middle = rest.astype(BF16)
    low = (rest - middle.astype(F32)).astype(BF16)
    spread = dot(link, jnp.concatenate([high, middle, low], axis=1))
    return (spread[:, :width] + (spread[:, width : 2 * width] + spread[:, 2 * width :])) * root


def live_rows(count, first, rows):
    index = lax.broadcasted_iota(jnp.int32, (rows, 1), 0) + first
    return jnp.where(index < count, 1.0, 0.0).astype(F32)


def norm_stats(values):
    mean = jnp.mean(values, axis=-1, keepdims=True)
    centred = values - mean
    var = jnp.mean(centred * centred, axis=-1, keepdims=True)
    inv = lax.rsqrt(var + 1e-05)
    return centred * inv, inv


def quad_stack(block):
    head = lax.broadcasted_iota(jnp.int32, block.shape, 1) // HEAD
    return jnp.concatenate(
        [jnp.where(head == h, block, jnp.zeros_like(block)) for h in range(4)], axis=0
    )


def grad_softmax(probs, grad_probs):
    tokens, columns = probs.shape
    weighted = (probs * grad_probs).reshape(HOP_TOKENS, GROUP, columns)
    total = jnp.sum(weighted, axis=0)
    shaped = probs.reshape(HOP_TOKENS, GROUP, columns)
    return (weighted - shaped * total[None]).reshape(tokens, columns).astype(BF16)


def quad_probs(scores, scale):
    tokens, columns = scores.shape
    scores = scores.reshape(HOP_TOKENS, GROUP, columns)
    top = jnp.max(scores, axis=0)
    power = jnp.exp2((scores - top[None]) * (scale * LOG2_E))
    row = lax.broadcasted_iota(jnp.int32, (GROUP, columns), 0)
    col = lax.broadcasted_iota(jnp.int32, (GROUP, columns), 1) % GROUP
    share = jnp.where(row == col, 1.0 / jnp.sum(power, axis=0), 0.0)
    return (power * share[None]).reshape(tokens, columns)


def queries_from(weights, block):
    tokens = block.shape[0]
    out = []
    lane = lax.broadcasted_iota(jnp.int32, (tokens, 2 * HEAD), 1)
    for first in (0, 2 * HEAD):
        both = dot_lead(weights[:, first : first + 2 * HEAD], block[:, first : first + 2 * HEAD])
        out.append(jnp.where(lane < HEAD, both[:tokens], both[tokens:]))
    return jnp.concatenate(out, axis=1)


def hop_rows(values, index):
    shaped = values.reshape(HOP_PAIRS, GROUPS, 2, GROUP, values.shape[-1])
    return shaped[index // 2, :, index % 2].reshape(NODES_PER_TILE, values.shape[-1])


def hop_join(parts):
    width = parts[0].shape[-1]
    blocks = []
    for pair in range(HOP_PAIRS):
        both = [parts[2 * pair + k].reshape(GROUPS, 1, GROUP, width) for k in range(2)]
        blocks.append(jnp.concatenate(both, axis=1))
    return jnp.concatenate(blocks, axis=0).reshape(TOKENS, width)


def interleave(streams):
    live = list(enumerate(streams))
    turn = 0
    while live:
        live = [
            (place, stream)
            for place, stream in live
            if turn < place * SKEW or next(stream, live) is not live
        ]
        turn += 1


class Place:
    def __init__(self, lines):
        self.lines = lines
        self.core = lax.axis_index("grp")
        self.owner = lax.axis_index("fsdp")
        self.line = lax.div(self.owner, PLANE)
        self.spot = lax.rem(self.owner, PLANE)

    def line_turn(self, ahead):
        return lax.rem(self.line + ahead + self.lines, self.lines)

    def spot_turn(self, ahead):
        return lax.rem(self.spot + ahead + PLANE, PLANE)

    def line_peer(self, ahead):
        return (self.core, self.line_turn(ahead) * PLANE + self.spot)

    def plane_peer(self, ahead):
        return (self.core, self.line * PLANE + self.spot_turn(ahead))

    def side_peer(self):
        return (self.core, self.owner + 1 - 2 * lax.rem(self.spot, 2))

    def side_spot(self):
        return self.spot + 1 - 2 * lax.rem(self.spot, 2)

    def sibling(self):
        return (1 - self.core, self.owner)

    def peers(self):
        return (
            [self.line_peer(d) for d in range(1, self.lines)]
            + [self.plane_peer(e) for e in range(1, PLANE)]
            + [self.sibling()]
        )

    def greet(self):
        barrier = pltpu.get_barrier_semaphore()
        for peer in self.peers():
            pl.semaphore_signal(barrier, inc=1, device_id=peer, device_id_type=MESH)

    def greeted(self):
        pl.semaphore_wait(pltpu.get_barrier_semaphore(), self.lines + PLANE - 1)


def remote(source, target, send, recv, device):
    return pltpu.make_async_remote_copy(
        src_ref=source,
        dst_ref=target,
        send_sem=send,
        recv_sem=recv,
        device_id=device,
        device_id_type=MESH,
    )


class Gather:
    def __init__(self, place, slots, send, recv, halves):
        self.place, self.slots, self.send, self.recv = place, slots, send, recv
        self.halves = halves

    def slot(self, line, spot):
        if self.halves:
            return self.slots.at[line, spot, self.place.core]
        return self.slots.at[line, spot]

    def line_copies(self):
        place = self.place
        own = self.slot(place.line, place.spot)
        return [
            remote(own, own, self.send.at[d], self.recv.at[d], place.line_peer(d))
            for d in range(1, place.lines)
        ]

    def plane_copies(self):
        place = self.place
        line = self.slot(slice(None), place.spot)
        first = place.lines - 1
        return [
            remote(line, line, self.send.at[first + e], self.recv.at[first + e], place.plane_peer(e))
            for e in range(1, PLANE)
        ]

    def start(self):
        for copy in self.line_copies():
            copy.start()

    def forward(self):
        for copy in self.line_copies():
            copy.wait()
        for copy in self.plane_copies():
            copy.start()

    def finish(self):
        for copy in self.plane_copies():
            copy.wait()

    def pair(self):
        half = self.slots.at[:, :, self.place.core]
        return remote(half, half, self.send.at[0], self.recv.at[0], self.place.sibling())


class CrossGather(Gather):
    def step_copies(self):
        place = self.place
        line = self.slot(slice(None), place.spot)
        first = place.lines
        return [
            remote(line, line, self.send.at[first + k], self.recv.at[first + k], peer)
            for k, peer in enumerate((place.side_peer(), place.plane_peer(2)))
        ]

    def cross_copies(self):
        place = self.place
        first = place.lines + 2
        half = self.slots.shape[-1] // 2
        copies = []
        for k, (spot, peer) in enumerate(
            ((place.side_spot(), place.plane_peer(2)), (place.spot_turn(2), place.side_peer()))
        ):
            part = self.slots.at[:, spot, place.core, :, k * half : (k + 1) * half]
            copies.append(
                remote(part, part, self.send.at[first + k], self.recv.at[first + k], peer)
            )
        return copies

    def forward(self):
        for copy in self.line_copies():
            copy.wait()
        for copy in self.step_copies():
            copy.start()

    def cross(self):
        for copy in self.step_copies():
            copy.wait()
        for copy in self.cross_copies():
            copy.start()

    def finish(self):
        for copy in self.cross_copies():
            copy.wait()


class Scatter:
    def __init__(self, place, terms, got, chip, plane_got, line_out, line_got, result, sems):
        self.place, self.terms, self.got, self.chip = place, terms, got, chip
        self.plane_got, self.line_out, self.line_got = plane_got, line_out, line_got
        self.result, self.sems = result, sems

    def pair(self):
        place = self.place
        return remote(
            self.terms.at[:, 1 - place.core],
            self.got,
            self.sems.at[0, 0],
            self.sems.at[1, 0],
            place.sibling(),
        )

    def plane(self):
        place = self.place
        return [
            remote(
                self.chip.at[:, place.spot_turn(e)],
                self.plane_got.at[e - 1],
                self.sems.at[0, e],
                self.sems.at[1, e],
                place.plane_peer(e),
            )
            for e in range(1, PLANE)
        ]

    def line(self):
        place = self.place
        return [
            remote(
                self.line_out.at[place.line_turn(d)],
                self.line_got.at[d - 1],
                self.sems.at[0, PLANE + d - 1],
                self.sems.at[1, PLANE + d - 1],
                place.line_peer(d),
            )
            for d in range(1, place.lines)
        ]

    def last(self):
        place = self.place
        half = self.result.at[place.core]
        k = PLANE + place.lines - 1
        return remote(half, half, self.sems.at[0, k], self.sems.at[1, k], place.sibling())

    def begin(self):
        self.pair().start()

    def to_plane(self):
        place = self.place
        self.pair().wait()

        def add(line, carry):
            for spot in range(PLANE):
                owner = line * PLANE + spot
                self.chip[line, spot] = self.terms[owner, place.core] + self.got[owner]
            return carry

        lax.fori_loop(0, place.lines, add, 0)
        for copy in self.plane():
            copy.start()

    def to_line(self):
        place = self.place
        for copy in self.plane():
            copy.wait()

        def add(line, carry):
            total = self.chip[line, place.spot].astype(F32)
            for e in range(PLANE - 1):
                total = total + self.plane_got[e, line].astype(F32)
            self.line_out[line] = total.astype(BF16)
            return carry

        lax.fori_loop(0, place.lines, add, 0)
        for copy in self.line():
            copy.start()

    def to_sibling(self):
        place = self.place
        for copy in self.line():
            copy.wait()
        total = self.line_out[place.line].astype(F32)
        for d in range(place.lines - 1):
            total = total + self.line_got[d].astype(F32)
        self.result[place.core] = total
        self.last().start()

    def end(self):
        self.last().wait()


class TailScatter:
    def __init__(self, place, own, plane_got, line_out, line_got, mine, other, sems):
        self.place, self.own, self.plane_got, self.line_out = place, own, plane_got, line_out
        self.line_got, self.mine, self.other, self.sems = line_got, mine, other, sems

    def plane(self):
        place = self.place
        return [
            remote(
                self.own.at[place.spot_turn(e)],
                self.plane_got.at[e - 1],
                self.sems.at[0, e],
                self.sems.at[1, e],
                place.plane_peer(e),
            )
            for e in range(1, PLANE)
        ]

    def line(self):
        place = self.place
        return [
            remote(
                self.line_out.at[place.line_turn(d)],
                self.line_got.at[d - 1],
                self.sems.at[0, PLANE + d - 1],
                self.sems.at[1, PLANE + d - 1],
                place.line_peer(d),
            )
            for d in range(1, place.lines)
        ]

    def last(self):
        return remote(
            self.mine, self.other, self.sems.at[0, 0], self.sems.at[1, 0], self.place.sibling()
        )

    def begin(self):
        for copy in self.plane():
            copy.start()

    def to_line(self):
        place = self.place
        for copy in self.plane():
            copy.wait()
        total = self.own[place.spot].astype(F32)
        for e in range(PLANE - 1):
            total = total + self.plane_got[e].astype(F32)
        total = total.astype(BF16)
        for line in range(place.lines):
            self.line_out[line, 0] = total[line]
            self.line_out[line, 1] = total[place.lines]
        for copy in self.line():
            copy.start()

    def to_sibling(self):
        place = self.place
        for copy in self.line():
            copy.wait()
        total = self.line_out[place.line].astype(F32)
        for d in range(place.lines - 1):
            total = total + self.line_got[d].astype(F32)
        self.mine[...] = total
        self.last().start()

    def end(self):
        self.last().wait()
        return self.mine[...] + self.other[...]


def hop_states(counts_ref, adjacency_ref, features_ref, stacked_ref):
    clusters, slots = adjacency_ref.shape[:2]
    per_cluster = slots // NODES_PER_TILE
    links = []
    states = []
    for cluster in range(clusters):
        count = counts_ref[cluster]
        links.append(link_of(adjacency_ref[cluster], count))
        states.append(
            features_ref[cluster * slots : (cluster + 1) * slots].astype(F32)
            * live_rows(count, 0, slots)
        )
    earlier = [None] * clusters
    for index in range(HOP_TOKENS):
        for cluster in range(clusters):
            if index > 0:
                states[cluster] = hop(*links[cluster], states[cluster])
            if index % 2 == 0:
                earlier[cluster] = states[cluster]
                continue
            for part in range(per_cluster):
                rows = slice(part * NODES_PER_TILE, (part + 1) * NODES_PER_TILE)
                both = [
                    state[rows].reshape(GROUPS, GROUP, state.shape[-1])
                    for state in (earlier[cluster], states[cluster])
                ]
                stacked_ref[cluster * per_cluster + part, index // 2] = jnp.concatenate(
                    both, axis=1
                ).astype(BF16)


def spread_vectors(small, owners, width):
    rows = small.shape[0]
    lane = lax.broadcasted_iota(jnp.int32, (128, width), 0)
    column = lax.broadcasted_iota(jnp.int32, (128, width), 1)
    row = lax.broadcasted_iota(jnp.int32, (rows, width), 0)
    place = lax.broadcasted_iota(jnp.int32, (rows, width), 1)
    piece = width // owners
    pieces = dot(small, jnp.where(lane == column % piece, 1.0, 0.0).astype(BF16))
    out = []
    for vector in range(4):
        mine = jnp.logical_and(row % 8 == vector, lax.div(row, 8) == lax.div(place, piece))
        out.append(jnp.sum(jnp.where(mine, pieces, 0.0), axis=0, keepdims=True))
    pieces = dot(small, jnp.where(lane == column % (2 * piece), 1.0, 0.0).astype(BF16))
    for first in (0, owners // 2):
        owner = lax.div(place, 2 * piece) + first
        mine = jnp.logical_and(row % 8 == 4, lax.div(row, 8) == owner)
        out.append(jnp.sum(jnp.where(mine, pieces, 0.0), axis=0, keepdims=True))
    return jnp.concatenate(out + [jnp.zeros((2, width), F32)], axis=0)


def hop_back(counts_ref, adjacency_ref, grad_stacked_ref, grad_features_ref, between):
    clusters, slots = adjacency_ref.shape[:2]
    feat = grad_features_ref.shape[1]
    rows = TOKENS // HOP_PAIRS
    per_cluster = slots // NODES_PER_TILE
    links = []
    states = []

    def hop_grad(cluster, index):
        return jnp.concatenate(
            [
                grad_stacked_ref[
                    cluster * per_cluster + p, index // 2 * rows : (index // 2 + 1) * rows, 0:feat
                ]
                .reshape(GROUPS, 2, GROUP, feat)[:, index % 2]
                .reshape(NODES_PER_TILE, feat)
                for p in range(per_cluster)
            ],
            axis=0,
        )

    for cluster in range(clusters):
        links.append(link_of(adjacency_ref[cluster], counts_ref[cluster]))
        states.append(hop_grad(cluster, HOPS))
    for index in range(HOPS - 1, -1, -1):
        for cluster in range(clusters):
            states[cluster] = hop_grad(cluster, index) + hop(*links[cluster], states[cluster])
        if index in between:
            between[index]()
    for cluster in range(clusters):
        grad_features_ref[cluster * slots : (cluster + 1) * slots] = states[cluster] * live_rows(
            counts_ref[cluster], 0, slots
        )


def block_of(ref, tile, group, first):
    return ref[tile, :, group, :, first : first + QUAD].reshape(GROUP * HOP_TOKENS, QUAD)


def put_block(ref, tile, group, first, block):
    ref[tile, :, group, :, first : first + QUAD] = block.astype(BF16).reshape(
        HOP_PAIRS, 2 * GROUP, QUAD
    )


def tokens_of(ref, tile):
    return ref[tile].reshape(TOKENS, ref.shape[-1])


def embed_tile(tile, stacked_ref, embed, gain, shift, second_ref, normed_ref):
    hidden = dot(tokens_of(stacked_ref, tile), embed)
    second_ref[tile] = hidden
    normal, _ = norm_stats(hidden)
    normed_ref[tile] = (normal * gain + shift).astype(BF16)


def project_step(first_tile, kind, normed_ref, weight, triple_ref):
    width = normed_ref.shape[-1]
    tiles = pl.ds(first_tile, STREAMS)
    normed = normed_ref[tiles].reshape(STREAMS * TOKENS, width)
    triple_ref[tiles, :, :, :, kind * width : (kind + 1) * width] = (
        dot(normed, weight).astype(BF16).reshape(STREAMS, *triple_ref.shape[1:-1], width)
    )


def attend_tile(tile, normed_ref, value_weight, triple_ref, mixed_ref, probs_ref):
    width = normed_ref.shape[-1]
    triple_ref[tile, :, :, :, 2 * width :] = (
        dot(normed_ref[tile], value_weight).astype(BF16).reshape(*triple_ref.shape[1:-1], width)
    )
    places = [(tile, g, first) for g in range(GROUPS) for first in range(0, width, QUAD)]
    keys = [block_of(triple_ref, t, g, width + first) for t, g, first in places]
    queries = [quad_stack(block_of(triple_ref, *place)) for place in places]
    scores = [dot_last(k, q) for k, q in zip(keys, queries)]
    probs = [quad_probs(score, HEAD ** (-0.5)).astype(BF16) for score in scores]
    values = [block_of(triple_ref, t, g, 2 * width + first) for t, g, first in places]
    blocks = [queries_from(p, v) for p, v in zip(probs, values)]
    for place, block, prob in zip(places, blocks, probs):
        put_block(mixed_ref, *place, block)
        probs_ref[place[2] // QUAD, tile, place[1]] = prob


def middle_step(
    first_tile,
    counts_ref,
    second_ref,
    mixed_ref,
    cotangent_ref,
    rows_ref,
    expand,
    reducer,
    output_ref,
    rows_grad_ref,
    grad_merge_ref,
    grad_expand_ref,
    grad_reduce_ref,
):
    width = second_ref.shape[-1]
    gain, shift = rows_ref[2:3], rows_ref[3:4]
    row_node, row_hop = rows_ref[4:5], rows_ref[5:6]

    def stream(part):
        tile = first_tile + part
        second = second_ref[tile]
        normal, inv = norm_stats(second)
        inner = (normal * gain + shift).astype(BF16)
        yield
        before = dot(inner, expand)
        yield
        square = before * before
        gate = 0.5 + 0.5 * jnp.tanh(before * (square * (GELU_A * GELU_B) + GELU_A))
        gated = before * gate
        after = gated.astype(BF16)
        slope = gate + (gated - gated * gate) * (
            square * (6.0 * GELU_A * GELU_B) + 2.0 * GELU_A
        )
        yield
        third = second + dot(after, reducer)
        yield
        shaped = [hop_rows(third, k) for k in range(HOP_TOKENS)]
        node = tile * NODES_PER_TILE
        keep = live_rows(counts_ref[lax.div(node, 128)], lax.rem(node, 128), NODES_PER_TILE)
        centre = shaped[0]
        base = jnp.sum(centre * row_node, axis=-1, keepdims=True)
        logits = [
            base + jnp.sum(shaped[k] * row_hop, axis=-1, keepdims=True)
            for k in range(1, HOP_TOKENS)
        ]
        top = functools.reduce(jnp.maximum, logits)
        powers = [jnp.exp(logit - top) for logit in logits]
        scale = 1.0 / functools.reduce(jnp.add, powers)
        shares = [power * scale for power in powers]
        total = centre
        for k in range(1, HOP_TOKENS):
            total = total + shares[k - 1] * shaped[k]
        output_ref[tile] = total * keep
        cotangent = cotangent_ref[tile] * keep
        grad_shares = [
            jnp.sum(cotangent * shaped[k], axis=-1, keepdims=True) for k in range(1, HOP_TOKENS)
        ]
        mean_share = functools.reduce(jnp.add, [s * g for s, g in zip(shares, grad_shares)])
        grad_logits = [s * (g - mean_share) for s, g in zip(shares, grad_shares)]
        grad_base = functools.reduce(jnp.add, grad_logits)
        parts = [cotangent + grad_base * row_node]
        read_hop = jnp.zeros((NODES_PER_TILE, width), F32)
        for k in range(1, HOP_TOKENS):
            parts.append(shares[k - 1] * cotangent + grad_logits[k - 1] * row_hop)
            read_hop = read_hop + grad_logits[k - 1] * shaped[k]
        rows_grad_ref[4:5] += jnp.sum(grad_base * centre, axis=0, keepdims=True)
        rows_grad_ref[5:6] += jnp.sum(read_hop, axis=0, keepdims=True)
        grad_third = hop_join(parts)
        grad_branch = grad_third.astype(BF16)
        yield
        grad_after = dot_last(grad_branch, reducer)
        grad_reduce_ref[...] += dot_lead(after, grad_branch)
        yield
        grad_before = (slope * grad_after).astype(BF16)
        yield
        grad_inner = dot_last(grad_before, expand)
        grad_expand_ref[...] += dot_lead(inner, grad_before)
        yield
        rows_grad_ref[2:3] += jnp.sum(grad_inner * normal, axis=0, keepdims=True)
        rows_grad_ref[3:4] += jnp.sum(grad_inner, axis=0, keepdims=True)
        grad_normal = grad_inner * gain
        grad_second = grad_third + inv * (
            grad_normal
            - jnp.mean(grad_normal, axis=-1, keepdims=True)
            - normal * jnp.mean(grad_normal * normal, axis=-1, keepdims=True)
        )
        second_ref[tile] = grad_second
        yield
        grad_merge_ref[...] += dot_lead(tokens_of(mixed_ref, tile), grad_second.astype(BF16))

    interleave([stream(part) for part in range(FEEDS)])


def pack_terms(terms_ref, grad_merge_ref, grad_expand_ref, grad_reduce_ref):
    width, spread = grad_expand_ref.shape
    wide = grad_expand_ref[...].astype(BF16).reshape(PACK, 2, width // PACK // 2, spread)
    deep = grad_reduce_ref[...].astype(BF16).reshape(PACK, 2, spread // PACK // 2, width)
    square = grad_merge_ref[...].astype(BF16).reshape(PACK, 2, width // PACK // 2, width)
    terms_ref[:, :, 0:16] = wide[..., :width]
    terms_ref[:, :, 16:32] = wide[..., width:]
    terms_ref[:, :, 32:64] = deep
    terms_ref[:, :, 64:80] = square


def attend_back_step(
    quad,
    first_tile,
    triple_ref,
    probs_ref,
    second_ref,
    normed_ref,
    merge,
    grad_mixed_ref,
    grad_attend_ref,
):
    width = normed_ref.shape[-1]
    for part in range(STREAMS):
        grad_mixed = dot_last(second_ref[first_tile + part].astype(BF16), merge).astype(BF16)
        grad_mixed_ref[part, :, :, :, 0:QUAD] = grad_mixed.reshape(
            *grad_mixed_ref.shape[1:-1], QUAD
        )
    places = [(part, group) for part in range(STREAMS) for group in range(GROUPS)]
    scale = jnp.asarray(HEAD ** (-0.5), BF16)
    starts = [kind * width + quad * QUAD for kind in range(3)]

    def read(kind):
        return [block_of(triple_ref, first_tile + p, g, starts[kind]) for p, g in places]

    keys = read(1)
    queries = [quad_stack(block * scale) for block in read(0)]
    probs = [probs_ref[quad, first_tile + part, group] for part, group in places]
    values = read(2)
    out_grads = [quad_stack(block_of(grad_mixed_ref, p, g, 0)) for p, g in places]
    grad_probs = [dot_last(v, o) for v, o in zip(values, out_grads)]
    grad_scores = [grad_softmax(p.astype(F32), g) for p, g in zip(probs, grad_probs)]
    grad_values = [dot(p, o) for p, o in zip(probs, out_grads)]
    grad_keys = [dot(s, q) for s, q in zip(grad_scores, queries)]
    grad_queries = [queries_from(s, k * scale) for s, k in zip(grad_scores, keys)]
    for (part, group), a, b, c in zip(places, grad_queries, grad_keys, grad_values):
        for start, block in zip(starts, (a, b, c)):
            put_block(triple_ref, first_tile + part, group, start, block)
    tiles = pl.ds(first_tile, STREAMS)
    grads = jnp.concatenate(
        [
            triple_ref[tiles, :, :, :, start : start + QUAD].reshape(STREAMS * TOKENS, QUAD)
            for start in starts
        ],
        axis=1,
    )
    grad_attend_ref[:, 0 : 3 * QUAD] += dot_lead(
        normed_ref[tiles].reshape(STREAMS * TOKENS, width), grads
    )


def embed_back_step(
    first_tile,
    stacked_ref,
    second_ref,
    triple_ref,
    attend,
    embed,
    gain,
    rows_keep,
    grad_embed_ref,
    normed_ref,
):
    def stream(part):
        tile = first_tile + part
        stacked = tokens_of(stacked_ref, tile)
        grad_normed = dot_last(tokens_of(triple_ref, tile), attend)
        hidden = dot(stacked, embed)
        yield
        normal, inv = norm_stats(hidden)
        rows_keep[0:1] += jnp.sum(grad_normed * normal, axis=0, keepdims=True)
        rows_keep[1:2] += jnp.sum(grad_normed, axis=0, keepdims=True)
        grad_normal = grad_normed * gain
        grad_hidden = second_ref[tile] + inv * (
            grad_normal
            - jnp.mean(grad_normal, axis=-1, keepdims=True)
            - normal * jnp.mean(grad_normal * normal, axis=-1, keepdims=True)
        )
        grad_hidden = grad_hidden.astype(BF16)
        yield
        grad_embed_ref[...] += dot_lead(stacked, grad_hidden)
        normed_ref[tile] = grad_hidden

    interleave([stream(part) for part in range(STREAMS)])


class Silent:
    def __getattr__(self, name):
        return lambda *arguments: None


def loop(count, step, unroll=1):
    def body(index, carry):
        step(index)
        return carry

    lax.fori_loop(0, count, body, 0, unroll=unroll)


def layer_phases(
    counts_ref,
    adjacency_ref,
    features_ref,
    cotangent_ref,
    rows_ref,
    embed_ref,
    query_ref,
    key_ref,
    value_ref,
    merge_ref,
    expand_ref,
    reduce_ref,
    output_ref,
    grad_features_ref,
    terms_ref,
    early_terms,
    late_terms,
    grad_embed_ref,
    rows_keep,
    keep,
    transfers,
):
    (
        stacked_ref,
        second_ref,
        normed_ref,
        triple_ref,
        mixed_ref,
        grad_merge_ref,
        grad_expand_ref,
        grad_reduce_ref,
        probs_ref,
    ) = keep
    tiles, _, width = second_ref.shape
    pairs = tiles // STREAMS
    sums = (grad_merge_ref, grad_expand_ref, grad_reduce_ref)

    def clear():
        for ref in (rows_keep, grad_embed_ref, *sums):
            ref[...] = jnp.zeros_like(ref)

    transfers.lead()
    hop_states(counts_ref, adjacency_ref, features_ref, stacked_ref)
    if not transfers.head(clear):
        clear()

    def embed_step(tile):
        embed_tile(
            tile, stacked_ref, embed_ref[...], rows_ref[0:1], rows_ref[1:2], second_ref, normed_ref
        )
        transfers.beside_embed(tile, tiles)

    loop(tiles, embed_step)
    for kind, weight_ref in enumerate((query_ref, key_ref)):
        transfers.before_projection(kind)

        def project(pair, kind=kind, weight_ref=weight_ref):
            weight = weight_ref[...].reshape(width, width)
            project_step(pair * STREAMS, kind, normed_ref, weight, triple_ref)
            transfers.beside_projection(kind, pair)

        loop(pairs, project)
    transfers.before_projection(2)

    def attend_step(tile):
        attend_tile(
            tile,
            normed_ref,
            value_ref[...].reshape(width, width),
            triple_ref,
            mixed_ref,
            probs_ref,
        )
        transfers.beside_attention(tile, tiles)

    loop(tiles, attend_step)
    transfers.before_merge()

    def merge_step(pair):
        mixed = mixed_ref[pl.ds(pair * STREAMS, STREAMS)].reshape(STREAMS * TOKENS, width)
        second_ref[pl.ds(pair * STREAMS, STREAMS)] += dot(
            mixed, merge_ref[...].reshape(width, width)
        ).reshape(STREAMS, TOKENS, width)

    loop(pairs, merge_step, pairs)
    transfers.before_middle()
    spread = grad_expand_ref.shape[1]

    def feed_step(pair):
        middle_step(
            pair * FEEDS,
            counts_ref,
            second_ref,
            mixed_ref,
            cotangent_ref,
            rows_ref,
            expand_ref[...].reshape(width, spread),
            reduce_ref[...].reshape(spread, width),
            output_ref,
            rows_keep,
            grad_merge_ref,
            grad_expand_ref,
            grad_reduce_ref,
        )

    loop(tiles // FEEDS, feed_step, 2)
    pack_terms(terms_ref, grad_merge_ref, grad_expand_ref, grad_reduce_ref)
    transfers.after_middle()
    grad_attend_ref = grad_expand_ref
    for quad, terms in enumerate((early_terms, late_terms)):
        grad_attend_ref[...] = jnp.zeros_like(grad_attend_ref)

        def back_step(pair, quad=quad):
            attend_back_step(
                quad,
                pair * STREAMS,
                triple_ref,
                probs_ref,
                second_ref,
                normed_ref,
                merge_ref[...].reshape(width, width)[quad * QUAD : (quad + 1) * QUAD],
                mixed_ref,
                grad_attend_ref,
            )
            transfers.beside_backward(quad, pair, pairs)

        loop(pairs, back_step)
        terms[...] = grad_attend_ref[:, 0 : 3 * QUAD].astype(BF16).reshape(terms.shape)
        transfers.after_backward(quad)

    def embed_back(pair):
        embed_back_step(
            pair * STREAMS,
            stacked_ref,
            second_ref,
            triple_ref,
            jnp.concatenate(
                [ref[...].reshape(width, width) for ref in (query_ref, key_ref, value_ref)], axis=1
            ),
            embed_ref[...],
            rows_ref[0:1],
            rows_keep,
            grad_embed_ref,
            normed_ref,
        )
        transfers.beside_embed_back(pair, pairs)

    loop(pairs, embed_back)
    transfers.after_embed_back()

    def stacked_back(pair):
        grad_hidden = normed_ref[pl.ds(pair * STREAMS, STREAMS)].reshape(STREAMS * TOKENS, width)
        second_ref[pl.ds(pair * STREAMS, STREAMS), :, 0 : embed_ref.shape[0]] = dot_last(
            grad_hidden, embed_ref[...]
        ).reshape(STREAMS, TOKENS, embed_ref.shape[0])

    loop(pairs, stacked_back, pairs)
    hop_back(
        counts_ref,
        adjacency_ref,
        second_ref,
        grad_features_ref,
        {1: transfers.beside_hops},
    )
    transfers.end()


class Transfers:
    def __init__(self, place, gathers, scatters, copies, fill, unpack_head, pack_tail, publish):
        self.place = place
        self.first, *self.attend = gathers[:4]
        self.merge, self.expand, self.reducer = gathers[4:]
        self.middle, self.early, self.late, self.tail = scatters
        self.inputs, self.cotangent, self.output = copies[:2], copies[2], copies[3]
        self.fill = fill
        self.unpack_head, self.pack_tail, self.publish = unpack_head, pack_tail, publish

    def lead(self):
        for copy in (*self.inputs, self.cotangent):
            copy.start()
        self.place.greeted()
        self.first.start()
        self.fill()
        for part in self.attend[:2]:
            part.start()
        for copy in self.inputs:
            copy.wait()

    def head(self, clear):
        queries, keys, values = self.attend
        self.first.forward()
        values.start()
        self.merge.start()
        queries.forward()
        clear()
        self.first.finish()
        keys.forward()
        self.unpack_head()
        values.forward()
        self.expand.start()
        return True

    def beside_embed(self, tile, tiles):
        @pl.when(tile == 2)
        def _():
            self.attend[0].finish()
            self.attend[0].pair().start()

        @pl.when(tile == tiles - 2)
        def _():
            self.attend[1].cross()

        @pl.when(tile == tiles - 1)
        def _():
            self.merge.forward()

    def before_projection(self, kind):
        self.attend[kind].pair().wait()

    def beside_projection(self, kind, pair):
        @pl.when(pair == 0)
        def _():
            if kind == 0:
                self.attend[2].cross()
                self.reducer.start()
            self.attend[kind + 1].finish()
            self.attend[kind + 1].pair().start()

        @pl.when(pair == 1)
        def _():
            if kind == 0:
                self.expand.forward()
            else:
                self.merge.cross()
                self.reducer.forward()

    def beside_attention(self, tile, tiles):
        @pl.when(tile == 1)
        def _():
            self.expand.cross()
            self.merge.finish()
            self.merge.pair().start()

        @pl.when(tile == tiles - 3)
        def _():
            self.reducer.cross()

        @pl.when(tile == tiles - 2)
        def _():
            self.expand.finish()
            self.expand.pair().start()

        @pl.when(tile == tiles - 1)
        def _():
            self.reducer.finish()
            self.reducer.pair().start()

    def before_merge(self):
        self.merge.pair().wait()

    def before_middle(self):
        self.expand.pair().wait()
        self.reducer.pair().wait()
        self.cotangent.wait()

    def after_middle(self):
        self.middle.begin()
        self.output.start()

    def beside_backward(self, quad, pair, pairs):
        if quad == 0:

            @pl.when(pair == 0)
            def _():
                self.middle.to_plane()

        else:

            @pl.when(pair == 0)
            def _():
                self.early.to_plane()

            @pl.when(pair == pairs - 2)
            def _():
                self.middle.to_line()

    def after_backward(self, quad):
        if quad == 0:
            self.early.begin()
        else:
            self.late.begin()
            self.early.to_line()

    def beside_embed_back(self, pair, pairs):
        @pl.when(pair == 0)
        def _():
            self.late.to_plane()

        @pl.when(pair == 1)
        def _():
            self.middle.to_sibling()

    def after_embed_back(self):
        self.pack_tail()
        self.tail.begin()
        self.early.to_sibling()

    def beside_hops(self):
        self.late.to_line()
        self.tail.to_line()

    def end(self):
        self.tail.to_sibling()
        self.middle.end()
        self.early.end()
        self.late.to_sibling()
        tail = self.tail.end()
        self.late.end()
        self.output.wait()
        self.publish(tail)


def fold(block):
    half = block.shape[-1] // 2
    return jnp.concatenate([block[..., :half], block[..., half:]], axis=-2)


def layer_kernel(
    lines,
    counts_ref,
    adjacency_in,
    features_in,
    cotangent_in,
    embed_shard,
    vector_a,
    vector_b,
    vector_c,
    vector_d,
    vector_e,
    attend_shard,
    merge_shard,
    expand_shard,
    reduce_shard,
    output_out,
    grad_features_ref,
    middle_share_ref,
    attend_share_ref,
    tail_share_ref,
    adjacency_ref,
    features_ref,
    cotangent_ref,
    output_ref,
    local,
    *scratch,
):
    keep = scratch[0:9]
    scratch = scratch[9:]
    embed_ref, rows_ref, small_keep, head_slots = scratch[0:4]
    attend_slots = scratch[4:7]
    merge_slots, expand_slots, reduce_slots = scratch[7:10]
    grad_embed_ref, rows_keep = scratch[10:12]
    middle_refs, early_refs, late_refs = scratch[12:19], scratch[19:26], scratch[26:33]
    tail_refs = scratch[33:39]
    send, recv, scatter_sems = scratch[39:42]
    owners = lines * PLANE
    width = embed_ref.shape[-1]
    half_width = width // 2
    place = Place(lines)
    core, line, spot = place.core, place.line, place.spot
    place.greet()

    small_keep[...] = jnp.zeros_like(small_keep)
    for index, vector in enumerate((vector_a, vector_b, vector_c, vector_d, vector_e)):
        length = vector.shape[0]
        small_keep[index : index + 1, 0:length] = vector[...].astype(F32).reshape(1, length)
    mine = embed_shard[...].astype(F32)
    packed = jnp.concatenate(
        [
            jnp.concatenate([mine[:, :half_width], small_keep[...]], axis=1),
            jnp.concatenate([mine[:, half_width:], jnp.zeros((8, 128), F32)], axis=1),
        ],
        axis=0,
    )
    head_slots[line, spot] = packed.astype(BF16)

    def half_of(shard):
        rows = shard.shape[0] // 2
        return shard[pl.ds(pl.multiple_of(core * rows, rows), rows)]

    matrices = (merge_slots, expand_slots, reduce_slots)

    def fill():
        whole_attend = half_of(attend_shard)
        for kind, slots in enumerate(attend_slots):
            slots[line, spot, core] = whole_attend[:, kind * width : (kind + 1) * width]
        for slots, shard in zip(matrices, (merge_shard, expand_shard, reduce_shard)):
            slots[line, spot, core] = half_of(shard)

    copies = [
        pltpu.make_async_copy(source, target, local.at[index])
        for index, (source, target) in enumerate(
            (
                (adjacency_in, adjacency_ref),
                (features_in, features_ref),
                (cotangent_in, cotangent_ref),
                (output_ref, output_out),
            )
        )
    ]
    gathers = [
        (CrossGather if index > 1 else Gather)(
            place, slots, send.at[index], recv.at[index], index > 0
        )
        for index, slots in enumerate((head_slots, *attend_slots, *matrices))
    ]
    middle = Scatter(place, *middle_refs, scatter_sems.at[0])
    early = Scatter(place, *early_refs, scatter_sems.at[1])
    late = Scatter(place, *late_refs, scatter_sems.at[2])
    tail = TailScatter(place, *tail_refs, scatter_sems.at[3])

    def unpack_head():
        whole_head = head_slots[...].astype(F32).reshape(owners, 16, half_width + 128)
        top = whole_head[:, 0:8].reshape(owners * 8, half_width + 128)
        bottom = whole_head[:, 8:16].reshape(owners * 8, half_width + 128)
        embed_ref[:, :half_width] = top[:, :half_width].astype(BF16)
        embed_ref[:, half_width:] = bottom[:, :half_width].astype(BF16)
        rows_ref[...] = spread_vectors(top[:, half_width:].astype(BF16), owners, width)

    def pack_tail():
        own = fold(grad_embed_ref[...].reshape(owners, 8, width)).astype(BF16)
        own = own.reshape(lines, PLANE, 16, half_width)
        rows = fold(rows_keep[...].reshape(1, 8, width))[0].astype(BF16)
        for peer_spot in range(PLANE):
            tail.own[peer_spot, 0:lines] = own[:, peer_spot]
            tail.own[peer_spot, lines] = rows

    def publish(tail_total):
        middle_share_ref[...] = middle.result[...]
        attend_share_ref[0] = early.result[...]
        attend_share_ref[1] = late.result[...]
        tail_share_ref[...] = tail_total

    scatters = (middle, early, late, tail)
    transfers = Transfers(
        place, gathers, scatters, copies, fill, unpack_head, pack_tail, publish
    )
    layer_phases(
        counts_ref,
        adjacency_ref,
        features_ref,
        cotangent_ref,
        rows_ref,
        embed_ref,
        *attend_slots,
        merge_slots,
        expand_slots,
        reduce_slots,
        output_ref,
        grad_features_ref,
        middle.terms,
        early.terms,
        late.terms,
        grad_embed_ref,
        rows_keep,
        keep,
        transfers,
    )


def layer_alone_kernel(*refs):
    layer_phases(*refs[:19], refs[19:], Silent())


def unpack_kernel(
    middle_ref,
    attend_ref,
    tail_ref,
    features_ref,
    nodes_ref,
    output_ref,
    grad_features_ref,
    grad_embed_ref,
    grad_gain_one,
    grad_shift_one,
    grad_attend,
    grad_merge,
    grad_gain_two,
    grad_shift_two,
    grad_expand,
    grad_reduce,
    grad_readout,
):
    owner = lax.axis_index("fsdp")
    width = middle_ref.shape[-1]
    output_ref[...] = nodes_ref[...]
    grad_features_ref[...] = features_ref[...]
    for half in range(2):
        for quad in range(width // QUAD):
            for kind in range(3):
                first = kind * width + quad * QUAD
                grad_attend[half * 16 : half * 16 + 16, first : first + QUAD] = attend_ref[
                    quad, half, :, kind * QUAD : (kind + 1) * QUAD
                ]
        grad_expand[half * 16 : half * 16 + 16, 0:width] = middle_ref[half, 0:16]
        grad_expand[half * 16 : half * 16 + 16, width : 2 * width] = middle_ref[half, 16:32]
        grad_reduce[half * 32 : half * 32 + 32] = middle_ref[half, 32:64]
        grad_merge[half * 16 : half * 16 + 16] = middle_ref[half, 64:80]
    grad_embed_ref[...] = jnp.concatenate([tail_ref[0, 0:8], tail_ref[0, 8:16]], axis=1)
    rows = jnp.concatenate([tail_ref[1, 0:8], tail_ref[1, 8:16]], axis=1)
    length = grad_gain_one.shape[0]
    turned = pltpu.roll(rows, lax.rem(width - owner * length, width), 1)
    for index, ref in enumerate((grad_gain_one, grad_shift_one, grad_gain_two, grad_shift_two)):
        ref[...] = turned[index : index + 1, 0:length].reshape(length)
    length = grad_readout.shape[0]
    first = owner * length
    turned = pltpu.roll(rows, lax.rem(2 * width - first, width), 1)
    row = jnp.where(first < width, turned[4:5, 0:length], turned[5:6, 0:length])
    grad_readout[...] = row.reshape(length)


def sds(shape, dtype):
    return jax.ShapeDtypeStruct(shape, dtype)


SMEM_SPEC = pl.BlockSpec(memory_space=pltpu.SMEM)
VMEM_SPEC = pl.BlockSpec(memory_space=pltpu.VMEM)
ANY_SPEC = pl.BlockSpec(memory_space=pl.ANY)


def layer_keep(tiles, feat, width, spread):
    rows = (HOP_PAIRS, GROUPS, 2 * GROUP)
    return [
        pltpu.VMEM((tiles, *rows, feat), BF16),
        pltpu.VMEM((tiles, TOKENS, width), F32),
        pltpu.VMEM((tiles, TOKENS, width), BF16),
        pltpu.VMEM((tiles, *rows, 3 * width), BF16),
        pltpu.VMEM((tiles, *rows, width), BF16),
        pltpu.VMEM((width, width), F32),
        pltpu.VMEM((width, spread), F32),
        pltpu.VMEM((spread, width), F32),
        pltpu.VMEM((width // QUAD, tiles, GROUPS, GROUP * HOP_TOKENS, QUAD), BF16),
    ]


def layer_part(
    lines, counts, adjacency, features, cotangent, embed, vectors, attend, merge, expand, reducer
):
    nodes, feat = features.shape
    owners = lines * PLANE
    width, spread = expand.shape[0] * owners, expand.shape[1]
    tiles = nodes // NODES_PER_TILE
    rest = (80, width)
    wide = (width // owners // 2, 3 * QUAD)

    def slots(rows, columns):
        return pltpu.VMEM((lines, PLANE, 2, rows // 2, columns), BF16)

    def buffers(shape):
        return [
            pltpu.VMEM((owners, 2) + shape, BF16),
            pltpu.VMEM((owners,) + shape, BF16),
            pltpu.VMEM((lines, PLANE) + shape, BF16),
            pltpu.VMEM((PLANE - 1, lines) + shape, BF16),
            pltpu.VMEM((lines,) + shape, BF16),
            pltpu.VMEM((lines - 1,) + shape, BF16),
            pltpu.VMEM((2,) + shape, F32),
        ]

    outs = [
        cotangent.shape,
        features.shape,
        (2,) + rest,
        (width // QUAD, 2) + wide,
        (2, 16, width // 2),
    ]
    return pl.pallas_call(
        functools.partial(layer_kernel, lines),
        in_specs=[SMEM_SPEC] + [ANY_SPEC] * 3 + [VMEM_SPEC] * 10,
        out_specs=[ANY_SPEC] + [VMEM_SPEC] * 4,
        out_shape=[sds(shape, F32) for shape in outs],
        scratch_shapes=[
            pltpu.VMEM(adjacency.shape, jnp.int32),
            pltpu.VMEM(features.shape, BF16),
            pltpu.VMEM(cotangent.shape, F32),
            pltpu.VMEM(cotangent.shape, F32),
            pltpu.SemaphoreType.DMA((4,)),
        ]
        + layer_keep(tiles, feat, width, spread)
        + [
            pltpu.VMEM((feat, width), BF16),
            pltpu.VMEM((8, width), F32),
            pltpu.VMEM((8, 128), F32),
            pltpu.VMEM((lines, PLANE, 16, width // 2 + 128), BF16),
        ]
        + [slots(attend.shape[0], width)] * 3
        + [slots(*shard.shape) for shard in (merge, expand, reducer)]
        + [pltpu.VMEM((feat, width), F32), pltpu.VMEM((8, width), F32)]
        + buffers(rest)
        + buffers(wide) * 2
        + [
            pltpu.VMEM((PLANE, lines + 1, 16, width // 2), BF16),
            pltpu.VMEM((PLANE - 1, lines + 1, 16, width // 2), BF16),
            pltpu.VMEM((lines, 2, 16, width // 2), BF16),
            pltpu.VMEM((lines - 1, 2, 16, width // 2), BF16),
            pltpu.VMEM((2, 16, width // 2), F32),
            pltpu.VMEM((2, 16, width // 2), F32),
        ]
        + [
            pltpu.SemaphoreType.DMA((7, lines + PLANE)),
            pltpu.SemaphoreType.DMA((7, lines + PLANE)),
            pltpu.SemaphoreType.DMA((4, 2, PLANE + lines)),
        ],
        compiler_params=pltpu.CompilerParams(
            vmem_limit_bytes=VMEM_GRANT, collective_id=0, has_side_effects=True
        ),
        name="layer",
    )(counts, adjacency, features, cotangent, embed, *vectors, attend, merge, expand, reducer)


def layer_alone_part(
    counts, adjacency, features, cotangent, rows, embed, attend, merge, expand, reducer
):
    nodes, feat = features.shape
    width, spread = expand.shape
    tiles = nodes // NODES_PER_TILE
    wide = (PACK, 2, width // PACK // 2, 3 * QUAD)
    return pl.pallas_call(
        layer_alone_kernel,
        in_specs=[SMEM_SPEC] + [VMEM_SPEC] * 11,
        out_specs=[VMEM_SPEC] * 7,
        out_shape=[
            sds(cotangent.shape, F32),
            sds(features.shape, F32),
            sds((PACK, 2, 80, width), BF16),
            sds(wide, BF16),
            sds(wide, BF16),
            sds((feat, width), F32),
            sds((8, width), F32),
        ],
        scratch_shapes=layer_keep(tiles, feat, width, spread),
        compiler_params=pltpu.CompilerParams(vmem_limit_bytes=VMEM_GRANT),
        name="layer_alone",
    )(
        counts,
        adjacency,
        features,
        cotangent,
        rows,
        embed,
        attend[:, :width],
        attend[:, width : 2 * width],
        attend[:, 2 * width :],
        merge,
        expand,
        reducer,
    )


def unpack_part(middle, attend, tail, features, nodes, shapes):
    return pl.pallas_call(
        unpack_kernel,
        out_shape=[sds(shape, F32) for shape in [nodes.shape, features.shape] + shapes],
        compiler_params=pltpu.CompilerParams(vmem_limit_bytes=VMEM_GRANT),
        name="unpack_shares",
    )(middle, attend, tail, features, nodes)


def gather(block):
    return lax.all_gather(block, "fsdp", axis=0, tiled=True)


def share(term):
    part = lax.psum_scatter(term.astype(BF16), "fsdp", scatter_dimension=0, tiled=True)
    return lax.psum(part.astype(F32), "grp")


def body(
    features,
    adjacency,
    counts,
    input_weight,
    first_gain,
    first_shift,
    attend_weight,
    merge_weight,
    second_gain,
    second_shift,
    expand_weight,
    reduce_weight,
    readout_weight,
    cotangent,
):
    vectors = (first_gain, first_shift, second_gain, second_shift, readout_weight)
    owners = lax.axis_size("fsdp")
    if owners % PLANE == 0 and input_weight.shape[0] == 8 and attend_weight.shape[0] == 32:
        lines = owners // PLANE
        tiles = cotangent.shape[0] // NODES_PER_TILE
        output, grad_features, *shares = layer_part(
            lines,
            counts,
            adjacency,
            features,
            cotangent.reshape(tiles, NODES_PER_TILE, cotangent.shape[1]),
            input_weight,
            vectors,
            attend_weight,
            merge_weight,
            expand_weight,
            reduce_weight,
        )
        shapes = [
            weight.shape
            for weight in (
                input_weight,
                first_gain,
                first_shift,
                attend_weight,
                merge_weight,
                second_gain,
                second_shift,
                expand_weight,
                reduce_weight,
                readout_weight,
            )
        ]
        return tuple(
            unpack_part(*shares, grad_features, output.reshape(cotangent.shape), shapes)
        )
    return body_apart(
        features,
        adjacency,
        counts,
        input_weight,
        vectors,
        attend_weight,
        merge_weight,
        expand_weight,
        reduce_weight,
        cotangent,
    )


def body_apart(
    features,
    adjacency,
    counts,
    input_weight,
    vectors,
    attend_weight,
    merge_weight,
    expand_weight,
    reduce_weight,
    cotangent,
):
    lengths = [v.shape[0] for v in vectors]
    places = [sum(lengths[:i]) for i in range(len(lengths) + 1)]
    packed = lax.all_gather(jnp.concatenate(vectors), "fsdp", axis=0, tiled=False)
    width = merge_weight.shape[1]
    full = [
        packed[:, places[i] : places[i + 1]].astype(F32).reshape(-1, width)
        for i in range(len(lengths))
    ]
    rows = jnp.concatenate(full + [jnp.zeros((2, width), F32)], axis=0)
    embed, attend, merge, expand, reducer = map(
        gather, (input_weight, attend_weight, merge_weight, expand_weight, reduce_weight)
    )
    tiles = cotangent.shape[0] // NODES_PER_TILE
    output, grad_features, terms, early, late, grad_embed, rows_grad = layer_alone_part(
        counts,
        adjacency,
        features,
        cotangent.reshape(tiles, NODES_PER_TILE, width),
        rows,
        embed,
        attend,
        merge,
        expand,
        reducer,
    )
    grad_attend = jnp.stack([early.reshape(width, 3, QUAD), late.reshape(width, 3, QUAD)], axis=2)
    grad_attend = grad_attend.reshape(width, 3 * width)
    spread = expand.shape[1]
    grad_expand = jnp.concatenate([terms[:, :, 0:16], terms[:, :, 16:32]], axis=-1)
    parts = lax.axis_size("fsdp")
    pieces = [rows_grad[i] for i in range(4)] + [rows_grad[4:6]]
    packed_grad = jnp.concatenate([piece.reshape(parts, -1) for piece in pieces], axis=1)
    packed_grad = lax.psum(
        lax.psum_scatter(packed_grad, "fsdp", scatter_dimension=0, tiled=True), "grp"
    ).reshape(-1)
    small = [packed_grad[places[i] : places[i + 1]] for i in range(len(lengths))]
    return (
        output.reshape(cotangent.shape),
        grad_features,
        share(grad_embed),
        small[0],
        small[1],
        share(grad_attend),
        share(terms[:, :, 64:80].reshape(width, width)),
        small[2],
        small[3],
        share(grad_expand.reshape(width, spread)),
        share(terms[:, :, 32:64].reshape(spread, width)),
        small[4],
    )


def solution(mesh):
    nodes = ("grp", "fsdp")
    rows = P("fsdp", None)
    vector = P("fsdp")
    in_specs = (
        P(nodes, None),
        P(nodes, None, None),
        P(nodes),
        rows,
        vector,
        vector,
        rows,
        rows,
        vector,
        vector,
        rows,
        rows,
        vector,
        P(nodes, None),
    )
    out_specs = (
        P(nodes, None),
        P(nodes, None),
        rows,
        vector,
        vector,
        rows,
        rows,
        vector,
        vector,
        rows,
        rows,
        vector,
    )
    return jax.shard_map(body, mesh=mesh, in_specs=in_specs, out_specs=out_specs, check_vma=False)
```
